32 devices in a mesh: dp: 16 (over z, x, core), tensor: 2 (over y).
Axes of the slice: x: 2, y: 2, z: 4, core: 2. Of those that a mesh axis runs over, the one named last changes fastest.
Arguments:
- inputs: bfloat16 [8192, 2560], P(('dp', 'tensor')), may hold values from -1.5 to 1.5
- cotangent: bfloat16 [8192, 2560], P(('dp', 'tensor')), may hold values from -6 to 6
- segment_ids: int32 [8192], P('dp'), may hold values from 0 to 510, as said below
- gains: float32 [6144], P(('dp', 'tensor')), may hold values from 0.5 to 1.5
- gains_first: float32 [6144], P(('dp', 'tensor'))
- gains_second: float32 [6144], P(('dp', 'tensor')), as said below
- query_down: float32 [2560, 768], P(('dp', 'tensor')), may hold values from -0.125 to 0.125
- query_down_first: float32 [2560, 768], P(('dp', 'tensor'))
- query_down_second: float32 [2560, 768], P(('dp', 'tensor')), as said below
- latent_down: float32 [2560, 288], P(('dp', 'tensor')), may hold values from -0.125 to 0.125
- latent_down_first: float32 [2560, 288], P(('dp', 'tensor'))
- latent_down_second: float32 [2560, 288], P(('dp', 'tensor')), as said below
- query_up: float32 [768, 3840], P('dp', 'tensor'), may hold values from -0.21875 to 0.21875
- query_up_first: float32 [768, 3840], P('dp', 'tensor')
- query_up_second: float32 [768, 3840], P('dp', 'tensor'), as said below
- latent_up: float32 [256, 5120], P('dp', 'tensor'), may hold values from -0.375 to 0.375
- latent_up_first: float32 [256, 5120], P('dp', 'tensor')
- latent_up_second: float32 [256, 5120], P('dp', 'tensor'), as said below
- output_proj: float32 [2560, 2560], P(('tensor', 'dp')), may hold values from -1 to 1
- output_proj_first: float32 [2560, 2560], P(('tensor', 'dp'))
- output_proj_second: float32 [2560, 2560], P(('tensor', 'dp')), as said below
- gate_proj: float32 [2560, 6400], P('dp', 'tensor'), may hold values from -0.125 to 0.125
- gate_proj_first: float32 [2560, 6400], P('dp', 'tensor')
- gate_proj_second: float32 [2560, 6400], P('dp', 'tensor'), as said below
- up_proj: float32 [2560, 6400], P('dp', 'tensor'), may hold values from -0.125 to 0.125
- up_proj_first: float32 [2560, 6400], P('dp', 'tensor')
- up_proj_second: float32 [2560, 6400], P('dp', 'tensor'), as said below
- down_proj: float32 [6400, 2560], P(('tensor', 'dp')), may hold values from -0.21875 to 0.21875
- down_proj_first: float32 [6400, 2560], P(('tensor', 'dp'))
- down_proj_second: float32 [6400, 2560], P(('tensor', 'dp')), as said below
Outputs:
- block_output: bfloat16 [8192, 2560], P(('dp', 'tensor'))
- input_grad: bfloat16 [8192, 2560], P(('dp', 'tensor'))
- gains_new: float32 [6144], P(('dp', 'tensor'))
- gains_first_new: float32 [6144], P(('dp', 'tensor'))
- gains_second_new: float32 [6144], P(('dp', 'tensor'))
- query_down_new: float32 [2560, 768], P(('dp', 'tensor'))
- query_down_first_new: float32 [2560, 768], P(('dp', 'tensor'))
- query_down_second_new: float32 [2560, 768], P(('dp', 'tensor'))
- latent_down_new: float32 [2560, 288], P(('dp', 'tensor'))
- latent_down_first_new: float32 [2560, 288], P(('dp', 'tensor'))
- latent_down_second_new: float32 [2560, 288], P(('dp', 'tensor'))
- query_up_new: float32 [768, 3840], P('dp', 'tensor')
- query_up_first_new: float32 [768, 3840], P('dp', 'tensor')
- query_up_second_new: float32 [768, 3840], P('dp', 'tensor')
- latent_up_new: float32 [256, 5120], P('dp', 'tensor')
- latent_up_first_new: float32 [256, 5120], P('dp', 'tensor')
- latent_up_second_new: float32 [256, 5120], P('dp', 'tensor')
- output_proj_new: float32 [2560, 2560], P(('tensor', 'dp'))
- output_proj_first_new: float32 [2560, 2560], P(('tensor', 'dp'))
- output_proj_second_new: float32 [2560, 2560], P(('tensor', 'dp'))
- gate_proj_new: float32 [2560, 6400], P('dp', 'tensor')
- gate_proj_first_new: float32 [2560, 6400], P('dp', 'tensor')
- gate_proj_second_new: float32 [2560, 6400], P('dp', 'tensor')
- up_proj_new: float32 [2560, 6400], P('dp', 'tensor')
- up_proj_first_new: float32 [2560, 6400], P('dp', 'tensor')
- up_proj_second_new: float32 [2560, 6400], P('dp', 'tensor')
- down_proj_new: float32 [6400, 2560], P(('tensor', 'dp'))
- down_proj_first_new: float32 [6400, 2560], P(('tensor', 'dp'))
- down_proj_second_new: float32 [6400, 2560], P(('tensor', 'dp'))
The draws below stay inside these ranges and needn't reach their ends.
Inputs may be any that keep to these rules, and one draw needn't show every extreme that they name: `segment_ids`: within each pack of 512 consecutive tokens the ids count documents from 0 upward, start at 0 and never fall; the tokens at indices 512 // 2 - 1 and 256 of a pack have the same id; some pack reaches the largest id. `gains_second`: positive. `query_down_second`: positive. `latent_down_second`: positive. `query_up_second`: positive. `latent_up_second`: positive. `output_proj_second`: positive. `gate_proj_second`: positive. `up_proj_second`: positive. `down_proj_second`: positive.
All inputs are finite; a program needn't handle non-finite values.
Results may differ from the reference program's by a relative error of at most 0.02.
Values may be sent and summed in bfloat16 or wider, within the bound.
A program may use at most 248 MiB of HBM per device.

```python
import math
import jax
import jax.numpy as jnp
from jax import lax

D = 2560
H = 40
DN = 64
DR = 32
DV = 64
QR = 768
KVR = 256
FF = 6400
PACK = 512
STEP = 10
QH = 96
KH = 128
GAINS = 6144
TOKENS = 8192


def moment_draw(key, array_shape, grad_size):
    return 0.1 / 0.9 * grad_size * jax.random.normal(key, array_shape, jnp.float32)


def square_draw(key, array_shape, grad_size):
    factor = jnp.exp(jax.random.uniform(key, array_shape, jnp.float32, 0.0, math.log(4.0)))
    return 0.05 / 0.95 * grad_size * grad_size * factor


def gains_size():
    gain_index = jnp.arange(GAINS, dtype=jnp.int32)
    level = jnp.where(gain_index < D, 1.0, jnp.where(gain_index < D + QR, 1.1, jnp.where(gain_index < D + QR + KVR, 2.2, 0.45)))
    return level.astype(jnp.float32) * math.sqrt(TOKENS)


def draw_segment_ids(key, part):
    key = jax.random.fold_in(key, 1)
    key_rates, key_rolls, key_whole, key_busy = jax.random.split(key, 4)
    pack_count = TOKENS // PACK
    rates = jax.random.randint(key_rates, (pack_count, 1), 0, 4)
    rolls = jax.random.randint(key_rolls, (pack_count, PACK), 0, PACK)
    whole_pack = jax.random.randint(key_whole, (), 0, pack_count)
    busy_pack = (whole_pack + 1 + jax.random.randint(key_busy, (), 0, pack_count - 1)) % pack_count
    token_index = jnp.arange(PACK, dtype=jnp.int32)[None, :]
    pack_index = jnp.arange(pack_count, dtype=jnp.int32)[:, None]
    cuts = ((rolls < 4 * rates) | (pack_index == busy_pack)) & (token_index > 0) & (token_index != PACK // 2) & (pack_index != whole_pack)
    return jnp.cumsum(cuts.astype(jnp.int32), axis=1).reshape(TOKENS).astype(jnp.int32)


def draw_gains_first(key, part):
    key = jax.random.fold_in(key, 2)
    return moment_draw(key, (GAINS,), gains_size())


def draw_gains_second(key, part):
    key = jax.random.fold_in(key, 3)
    return square_draw(key, (GAINS,), gains_size())


def draw_query_down_first(key, part):
    key = jax.random.fold_in(key, 4)
    return moment_draw(key, (D, QR), 1.1 * math.sqrt(TOKENS))


def draw_query_down_second(key, part):
    key = jax.random.fold_in(key, 5)
    return square_draw(key, (D, QR), 1.1 * math.sqrt(TOKENS))


def draw_latent_down_first(key, part):
    key = jax.random.fold_in(key, 6)
    return moment_draw(key, (D, KVR + DR), 2.0 * math.sqrt(TOKENS))


def draw_latent_down_second(key, part):
    key = jax.random.fold_in(key, 7)
    return square_draw(key, (D, KVR + DR), 2.0 * math.sqrt(TOKENS))


def draw_query_up_first(key, part):
    key = jax.random.fold_in(key, 8)
    return moment_draw(key, (QR, H * QH), 0.5 * math.sqrt(TOKENS))


def draw_query_up_second(key, part):
    key = jax.random.fold_in(key, 9)
    return square_draw(key, (QR, H * QH), 0.5 * math.sqrt(TOKENS))


def draw_latent_up_first(key, part):
    key = jax.random.fold_in(key, 10)
    return moment_draw(key, (KVR, H * KH), 0.5 * math.sqrt(TOKENS))


def draw_latent_up_second(key, part):
    key = jax.random.fold_in(key, 11)
    return square_draw(key, (KVR, H * KH), 0.5 * math.sqrt(TOKENS))


def draw_output_proj_first(key, part):
    key = jax.random.fold_in(key, 12)
    return moment_draw(key, (H * DV, D), 0.04 * math.sqrt(TOKENS))


def draw_output_proj_second(key, part):
    key = jax.random.fold_in(key, 13)
    return square_draw(key, (H * DV, D), 0.04 * math.sqrt(TOKENS))


def draw_gate_proj_first(key, part):
    key = jax.random.fold_in(key, 14)
    return moment_draw(key, (D, FF), 0.2 * math.sqrt(TOKENS))


def draw_gate_proj_second(key, part):
    key = jax.random.fold_in(key, 15)
    return square_draw(key, (D, FF), 0.2 * math.sqrt(TOKENS))


def draw_up_proj_first(key, part):
    key = jax.random.fold_in(key, 16)
    return moment_draw(key, (D, FF), 0.2 * math.sqrt(TOKENS))


def draw_up_proj_second(key, part):
    key = jax.random.fold_in(key, 17)
    return square_draw(key, (D, FF), 0.2 * math.sqrt(TOKENS))


def draw_down_proj_first(key, part):
    key = jax.random.fold_in(key, 18)
    return moment_draw(key, (FF, D), 0.09 * math.sqrt(TOKENS))


def draw_down_proj_second(key, part):
    key = jax.random.fold_in(key, 19)
    return square_draw(key, (FF, D), 0.09 * math.sqrt(TOKENS))


def shard_levels(stream_key, extent, cuts, least, top_value):
    level = 1.0
    for dim, shards_of in cuts:
        heights = jax.random.uniform(jax.random.fold_in(jax.random.fold_in(stream_key, 6), dim), (shards_of,), jnp.float32, least / len(cuts), top_value / len(cuts))
        level = level * jnp.repeat(jnp.exp(heights), extent[dim] // shards_of).reshape((-1,) + (1,) * (len(extent) - 1 - dim))
    return level


def centred(rng, dims, width, bound, pieces=(), kind=jnp.bfloat16):
    values = jax.random.normal(rng, dims, jnp.float32) * width
    if len(pieces) > 0:
        values = shard_levels(rng, dims, pieces, -0.22, 0.18) * values
    return jnp.clip(values, min=-bound, max=bound).astype(kind)


def setup_inputs(seed: int = 0) -> dict:
    keys = jax.random.split(jax.random.key(seed), 31)
    inputs = centred(keys[0], (TOKENS, D), 0.25, 1.5, ((0, 32),))
    cotangent = centred(keys[1], (TOKENS, D), 1.0, 6.0, ((0, 32),))
    segment_ids = draw_segment_ids(jax.random.fold_in(keys[30], 71), 0)
    gains = jnp.clip(1.0 + 0.1 * jax.random.normal(keys[3], (GAINS,), jnp.float32), 0.5, 1.5)
    gains_first = draw_gains_first(jax.random.fold_in(keys[30], 71), 0)
    gains_second = draw_gains_second(jax.random.fold_in(keys[30], 71), 0)
    query_down = centred(keys[6], (D, QR), D ** -0.5, 0.125, ((0, 32),), jnp.float32)
    query_down_first = draw_query_down_first(jax.random.fold_in(keys[30], 71), 0)
    query_down_second = draw_query_down_second(jax.random.fold_in(keys[30], 71), 0)
    latent_down = centred(keys[9], (D, KVR + DR), D ** -0.5, 0.125, ((0, 32),), jnp.float32)
    latent_down_first = draw_latent_down_first(jax.random.fold_in(keys[30], 71), 0)
    latent_down_second = draw_latent_down_second(jax.random.fold_in(keys[30], 71), 0)
    query_up = centred(keys[12], (QR, H * QH), QR ** -0.5, 0.21875, ((0, 16), (1, 2)), jnp.float32)
    query_up_first = draw_query_up_first(jax.random.fold_in(keys[30], 71), 0)
    query_up_second = draw_query_up_second(jax.random.fold_in(keys[30], 71), 0)
    latent_up = centred(keys[15], (KVR, H * KH), KVR ** -0.5, 0.375, ((0, 16), (1, 2)), jnp.float32)
    latent_up_first = draw_latent_up_first(jax.random.fold_in(keys[30], 71), 0)
    latent_up_second = draw_latent_up_second(jax.random.fold_in(keys[30], 71), 0)
    output_proj = centred(keys[18], (H * DV, D), (H * DV // 64) ** -0.5, 1.0, ((0, 32),), jnp.float32)
    output_proj_first = draw_output_proj_first(jax.random.fold_in(keys[30], 71), 0)
    output_proj_second = draw_output_proj_second(jax.random.fold_in(keys[30], 71), 0)
    gate_proj = centred(keys[21], (D, FF), D ** -0.5, 0.125, ((0, 16), (1, 2)), jnp.float32)
    gate_proj_first = draw_gate_proj_first(jax.random.fold_in(keys[30], 71), 0)
    gate_proj_second = draw_gate_proj_second(jax.random.fold_in(keys[30], 71), 0)
    up_proj = centred(keys[24], (D, FF), D ** -0.5, 0.125, ((0, 16), (1, 2)), jnp.float32)
    up_proj_first = draw_up_proj_first(jax.random.fold_in(keys[30], 71), 0)
    up_proj_second = draw_up_proj_second(jax.random.fold_in(keys[30], 71), 0)
    down_proj = centred(keys[27], (FF, D), (FF // 8) ** -0.5, 0.21875, ((0, 32),), jnp.float32)
    down_proj_first = draw_down_proj_first(jax.random.fold_in(keys[30], 71), 0)
    down_proj_second = draw_down_proj_second(jax.random.fold_in(keys[30], 71), 0)
    return {"inputs": inputs, "cotangent": cotangent, "segment_ids": segment_ids, "gains": gains, "gains_first": gains_first, "gains_second": gains_second, "query_down": query_down, "query_down_first": query_down_first, "query_down_second": query_down_second, "latent_down": latent_down, "latent_down_first": latent_down_first, "latent_down_second": latent_down_second, "query_up": query_up, "query_up_first": query_up_first, "query_up_second": query_up_second, "latent_up": latent_up, "latent_up_first": latent_up_first, "latent_up_second": latent_up_second, "output_proj": output_proj, "output_proj_first": output_proj_first, "output_proj_second": output_proj_second, "gate_proj": gate_proj, "gate_proj_first": gate_proj_first, "gate_proj_second": gate_proj_second, "up_proj": up_proj, "up_proj_first": up_proj_first, "up_proj_second": up_proj_second, "down_proj": down_proj, "down_proj_first": down_proj_first, "down_proj_second": down_proj_second}


RESIDUAL = 1.4 / math.sqrt(62.0)
NORM_EPSILON = 1e-05
MOMENT_DECAY = 0.9
SQUARE_DECAY = 0.95
ADAM_EPSILON = 1e-08
WEIGHT_DECAY = 0.1
GAIN_RATE = 0.3
ROPE_BASE = 10000.0
MASKED = -1e+30

@jax.custom_vjp
def low(v):
    return lax.optimization_barrier(v.astype(jnp.bfloat16)).astype(jnp.float32)

@jax.custom_vjp
def low_back(v):
    return v

def low_keep(v):
    return (low(v), None)

def low_pass(kept, grad):
    return (grad,)

def back_keep(v):
    return (v, None)

def back_low(kept, grad):
    return (low(grad),)
low.defvjp(low_keep, low_pass)
low_back.defvjp(back_keep, back_low)

def product(left_side, right_side):
    return jnp.dot(left_side, right_side, precision=lax.Precision.HIGHEST, preferred_element_type=jnp.float32)

def rms_norm(values, gain_values):
    return values * lax.rsqrt(lax.optimization_barrier(jnp.mean(values * values, axis=-1, keepdims=True)) + NORM_EPSILON) * gain_values

def rotate(values, rope_cosine, rope_sine):
    half_width = values.shape[-1] // 2
    first_half = values[..., :half_width]
    second_half = values[..., half_width:]
    return jnp.concatenate([first_half * rope_cosine - second_half * rope_sine, second_half * rope_cosine + first_half * rope_sine], axis=-1)

def pack_tables(segment):
    token_index = jnp.arange(segment.shape[0], dtype=jnp.int32)
    doc_start = jnp.concatenate([jnp.ones((1,), dtype=jnp.bool_), segment[1:] != segment[:-1]])
    starts = lax.cummax(jnp.where(doc_start, token_index, 0), axis=0)
    position = (token_index - starts).astype(jnp.float32)
    exponent = jnp.arange(DR // 2, dtype=jnp.float32) * (2.0 / DR)
    rope_angle = position[:, None] * (ROPE_BASE ** (-exponent))[None, :]
    allowed = (segment[:, None] == segment[None, :]) & (token_index[None, :] <= token_index[:, None])
    return (jnp.cos(rope_angle), jnp.sin(rope_angle), allowed)

def pack_attention(items):
    query_raw, latent_raw, rope_raw, segment = items
    rope_cosine, rope_sine, allowed = pack_tables(segment)
    query_raw = low_back(query_raw)
    queries = low(jnp.concatenate([query_raw[..., :DN], rotate(query_raw[..., DN:], rope_cosine[:, None, :], rope_sine[:, None, :])], axis=-1))
    latent_heads = low(low_back(latent_raw))
    rope_key = low(rotate(rope_raw, rope_cosine, rope_sine))
    key_heads = jnp.concatenate([latent_heads[..., :DN], jnp.broadcast_to(rope_key[:, None, :], (rope_key.shape[0], H, DR))], axis=-1)
    scores = low_back(jnp.einsum('ihd,jhd->hij', queries, key_heads, precision=lax.Precision.HIGHEST) * QH ** (-0.5))
    scores = jnp.where(allowed[None], scores, MASKED)
    row_top = lax.optimization_barrier(jnp.max(scores, axis=-1, keepdims=True))
    exponent_rows = jnp.exp(scores - row_top)
    probs = exponent_rows / lax.optimization_barrier(jnp.sum(exponent_rows, axis=-1, keepdims=True))
    mixed_heads = jnp.einsum('hij,jhd->ihd', low(probs), latent_heads[..., DN:], precision=lax.Precision.HIGHEST)
    return low(low_back(mixed_heads)).reshape(segment.shape[0], H * DV)

def block_forward(incoming, gain_all, query_down, latent_down, query_up, latent_up, output_proj, gate_proj, up_proj, down_proj, segment_ids):
    gain_low = low(gain_all)
    gain_attention = gain_low[:D]
    gain_query = gain_low[D:D + QR]
    gain_latent = gain_low[D + QR:D + QR + KVR]
    gain_ffn = gain_low[D + QR + KVR:]
    normed_attn = low(rms_norm(incoming, gain_attention))
    query_latent = low_back(product(normed_attn, low(query_down)))
    query_normed = low(rms_norm(query_latent, gain_query))
    latent = low_back(product(normed_attn, low(latent_down)))
    latent_normed = low(rms_norm(latent[:, :KVR], gain_latent))
    pack_count = TOKENS // PACK
    query_heads = product(query_normed, low(query_up)).reshape(pack_count, PACK, H, QH)
    latent_heads = product(latent_normed, low(latent_up)).reshape(pack_count, PACK, H, KH)
    rope_raw = latent[:, KVR:].reshape(pack_count, PACK, DR)
    mixed_all = lax.map(jax.checkpoint(pack_attention), (query_heads, latent_heads, rope_raw, segment_ids.reshape(pack_count, PACK)))
    mixed_all = mixed_all.reshape(TOKENS, H * DV)
    residual = incoming + RESIDUAL * low_back(product(mixed_all, low(output_proj)))
    normed_ffn = low(rms_norm(residual, gain_ffn))
    gate_value = low_back(product(normed_ffn, low(gate_proj)))
    up_value = low_back(product(normed_ffn, low(up_proj)))
    hidden = low(gate_value * lax.logistic(gate_value) * up_value)
    return residual + RESIDUAL * low_back(product(hidden, low(down_proj)))

def adamw_update(weight, first_moment, second_moment, gradient, step_rate):
    new_first = MOMENT_DECAY * first_moment + (1.0 - MOMENT_DECAY) * gradient
    new_second = SQUARE_DECAY * second_moment + (1.0 - SQUARE_DECAY) * gradient * gradient
    first_hat = new_first / (1.0 - MOMENT_DECAY ** STEP)
    second_hat = new_second / (1.0 - SQUARE_DECAY ** STEP)
    new_weight = weight - step_rate * (first_hat / (jnp.sqrt(second_hat) + ADAM_EPSILON) + WEIGHT_DECAY * weight)
    return (new_weight, new_first, new_second)

def matrix_rate(fan_in):
    return 2.0 / math.sqrt(fan_in)

def reference(inputs, cotangent, segment_ids, gains, gains_first, gains_second, query_down, query_down_first, query_down_second, latent_down, latent_down_first, latent_down_second, query_up, query_up_first, query_up_second, latent_up, latent_up_first, latent_up_second, output_proj, output_proj_first, output_proj_second, gate_proj, gate_proj_first, gate_proj_second, up_proj, up_proj_first, up_proj_second, down_proj, down_proj_first, down_proj_second):

    def forward_only(incoming, gain_all, qdown_w, ldown_w, qup_w, lup_w, out_w, gate_w, up_w, down_w):
        return block_forward(incoming, gain_all, qdown_w, ldown_w, qup_w, lup_w, out_w, gate_w, up_w, down_w, segment_ids)
    output, pullback = jax.vjp(forward_only, inputs.astype(jnp.float32), gains, query_down, latent_down, query_up, latent_up, output_proj, gate_proj, up_proj, down_proj)
    gradients = pullback(cotangent.astype(jnp.float32))
    gains_new = adamw_update(gains, gains_first, gains_second, gradients[1], GAIN_RATE)
    query_down_new = adamw_update(query_down, query_down_first, query_down_second, gradients[2], matrix_rate(D))
    latent_down_new = adamw_update(latent_down, latent_down_first, latent_down_second, gradients[3], matrix_rate(D))
    query_up_new = adamw_update(query_up, query_up_first, query_up_second, gradients[4], matrix_rate(QR))
    latent_up_new = adamw_update(latent_up, latent_up_first, latent_up_second, gradients[5], matrix_rate(KVR))
    output_proj_new = adamw_update(output_proj, output_proj_first, output_proj_second, gradients[6], matrix_rate(H * DV // 64))
    gate_proj_new = adamw_update(gate_proj, gate_proj_first, gate_proj_second, gradients[7], matrix_rate(D))
    up_proj_new = adamw_update(up_proj, up_proj_first, up_proj_second, gradients[8], matrix_rate(D))
    down_proj_new = adamw_update(down_proj, down_proj_first, down_proj_second, gradients[9], matrix_rate(FF // 8))
    return (output.astype(jnp.bfloat16), gradients[0].astype(jnp.bfloat16), gains_new[0], gains_new[1], gains_new[2], query_down_new[0], query_down_new[1], query_down_new[2], latent_down_new[0], latent_down_new[1], latent_down_new[2], query_up_new[0], query_up_new[1], query_up_new[2], latent_up_new[0], latent_up_new[1], latent_up_new[2], output_proj_new[0], output_proj_new[1], output_proj_new[2], gate_proj_new[0], gate_proj_new[1], gate_proj_new[2], up_proj_new[0], up_proj_new[1], up_proj_new[2], down_proj_new[0], down_proj_new[1], down_proj_new[2])
```

```python
import functools
import math

import jax
import jax.numpy as jnp
from jax import lax
from jax.experimental import pallas as pl
from jax.experimental.pallas import tpu as pltpu
from jax.sharding import PartitionSpec as P

D = 2560
H = 40
DN = 64
DR = 32
DV = 64
QR = 768
KVR = 256
FF = 6400
STEP = 10
QH = 96
KH = 128


RESIDUAL = 1.4 / math.sqrt(62.0)
NORM_EPSILON = 1e-05
MOMENT_DECAY = 0.9
SQUARE_DECAY = 0.95
ADAM_EPSILON = 1e-08
WEIGHT_DECAY = 0.1
GAIN_RATE = 0.3
ROPE_BASE = 10000.0
MASKED = -1e30


def right_transposed(left_side, right_side):
    return lax.dot_general(
        left_side, right_side, (((1,), (1,)), ((), ())), preferred_element_type=jnp.float32
    )


def left_transposed(left_side, right_side):
    return lax.dot_general(
        left_side, right_side, (((0,), (0,)), ((), ())), preferred_element_type=jnp.float32
    )


def norm_forward(values, gain_values):
    inverse = lax.rsqrt(jnp.mean(values * values, axis=-1, keepdims=True) + NORM_EPSILON)
    return (values * inverse * gain_values, inverse)


def norm_backward(values, inverse, gain_values, grad_out):
    unit_values = values * inverse
    weighted = grad_out * gain_values
    grad_values = inverse * (
        weighted - unit_values * jnp.mean(weighted * unit_values, axis=-1, keepdims=True)
    )
    return (grad_values, jnp.sum(grad_out * unit_values, axis=0))


def rotate(values, rope_cosine, rope_sine):
    half_width = values.shape[-1] // 2
    first_half = values[..., :half_width]
    second_half = values[..., half_width:]
    return jnp.concatenate(
        [
            first_half * rope_cosine - second_half * rope_sine,
            second_half * rope_cosine + first_half * rope_sine,
        ],
        axis=-1,
    )


def unrotate(grads_in, rope_cosine, rope_sine):
    half_width = grads_in.shape[-1] // 2
    first_half = grads_in[..., :half_width]
    second_half = grads_in[..., half_width:]
    return jnp.concatenate(
        [
            first_half * rope_cosine + second_half * rope_sine,
            second_half * rope_cosine - first_half * rope_sine,
        ],
        axis=-1,
    )


def adamw_update(weight, first_moment, second_moment, gradient, step_rate):
    new_first = MOMENT_DECAY * first_moment + (1.0 - MOMENT_DECAY) * gradient
    new_second = SQUARE_DECAY * second_moment + (1.0 - SQUARE_DECAY) * gradient * gradient
    first_hat = new_first / (1.0 - MOMENT_DECAY**STEP)
    second_hat = new_second / (1.0 - SQUARE_DECAY**STEP)
    new_weight = weight - step_rate * (
        first_hat / (jnp.sqrt(second_hat) + ADAM_EPSILON) + WEIGHT_DECAY * weight
    )
    return (new_weight, new_first, new_second)


def matrix_rate(fan_in):
    return 2.0 / math.sqrt(fan_in)


PLANE = 4
LINE = 4
LINK = 1e5
MESH = pl.DeviceIdType.MESH
VMEM_LIMIT = 56 * 1024 * 1024
HBM_SPEC = pl.BlockSpec(memory_space=pl.ANY)
VMEM_SPEC = pl.BlockSpec(memory_space=pltpu.VMEM)


class Board:
    def __init__(self, send_sems, recv_sems, local_sems):
        self.sems = (send_sems, recv_sems, local_sems)
        self.remotes = 0
        self.locals = 0
        self.closing = []
        self.d = lax.axis_index("dp")
        self.t = lax.axis_index("tensor")
        self.z = self.d // PLANE
        self.i = self.d % PLANE
        self.middle = (self.z == 1) | (self.z == 2)
        self.known = {
            name: self.work_out(name) for name in NEAR_OCTET + NEAR_PLANE + NEAR_LINE
        }

    def place_xor(self, k):
        i = self.i
        return (i, i + 1 - 2 * (i % 2), i + 2 - 4 * (i // 2), 3 - i)[k]

    def line_xor(self, k):
        z = self.z
        return (z, z + 1 - 2 * (z % 2), z + 2 - 4 * (z // 2), 3 - z)[k]

    def device(self, name):
        return self.known[name]

    def work_out(self, name):
        if name == "y":
            return (self.d, 1 - self.t)
        kind, k = name
        if kind == "plane":
            return (self.z * PLANE + self.place_xor(k), self.t)
        return (self.line_xor(k) * PLANE + self.i, self.t)

    def greet(self, names):
        barrier = pltpu.get_barrier_semaphore()
        known = [name for name in names if name != "transposed"]
        for name in known:
            pl.semaphore_signal(
                barrier, inc=1, device_id=self.device(name), device_id_type=MESH
            )
        if len(known) == len(names):
            pl.semaphore_wait(barrier, len(known))
            return

        @pl.when(self.i != self.z)
        def _():
            pl.semaphore_signal(
                barrier,
                inc=1,
                device_id=(self.i * PLANE + self.z, self.t),
                device_id_type=MESH,
            )
            pl.semaphore_wait(barrier, len(known) + 1)

        @pl.when(self.i == self.z)
        def _():
            pl.semaphore_wait(barrier, len(known))

    def slot(self):
        self.remotes += 1
        return self.remotes - 1

    def make(self, slot, source, target, name):
        return pltpu.make_async_remote_copy(
            src_ref=source,
            dst_ref=target,
            send_sem=self.sems[0].at[slot],
            recv_sem=self.sems[1].at[slot],
            device_id=self.device(name),
            device_id_type=MESH,
        )

    def send(self, source, target, name):
        copy = self.make(self.slot(), source, target, name)
        copy.start()
        self.closing.append(copy.wait_send)
        return copy

    def move(self, source, target, close=True):
        copy = pltpu.make_async_copy(source, target, self.sems[2].at[self.locals])
        self.locals += 1
        copy.start()
        if close:
            self.closing.append(copy.wait)
        return copy


def octet_place(core, x, y, half):
    return ((core * 2 + x) * 2 + y) * 2 + half


def octet_gather_steps(board, own_ref, all_ref, begin=0.0):
    h = own_ref.shape[0] // 2
    unit = 2.2 * math.prod(own_ref.shape) / LINK

    def rows(place, count=1):
        return all_ref.at[pl.ds(place * h, count * h)]

    core, along_x, along_y = ("plane", 1), ("plane", 2), "y"
    first, second = own_ref.at[pl.ds(0, h)], own_ref.at[pl.ds(h, h)]
    first_x = board.send(first, rows(octet_place(0, 1, 0, 0)), along_x)
    second_y = board.send(second, rows(octet_place(0, 0, 1, 1)), along_y)
    first_y = board.send(first, rows(octet_place(0, 0, 1, 0)), along_y)
    second_x = board.send(second, rows(octet_place(0, 1, 0, 1)), along_x)
    arrivals = [board.send(own_ref, rows(octet_place(1, 0, 0, 0), 2), core)]
    board.move(own_ref, rows(0, 2))

    def onward(place, name):
        source = rows(octet_place(*place[0]))
        return board.send(source, rows(octet_place(*place[1])), name)

    yield begin + unit
    first_x.wait_recv()
    first_xy = onward(((0, 1, 0, 0), (0, 1, 1, 0)), along_y)
    arrivals.append(onward(((0, 1, 0, 0), (1, 1, 0, 0)), core))
    second_y.wait_recv()
    second_xy = onward(((0, 0, 1, 1), (0, 1, 1, 1)), along_x)
    arrivals.append(onward(((0, 0, 1, 1), (1, 0, 1, 1)), core))
    for n, (copy, place) in enumerate(
        (
            (first_y, (1, 0, 1, 0)),
            (second_x, (1, 1, 0, 1)),
            (first_xy, (1, 1, 1, 0)),
            (second_xy, (1, 1, 1, 1)),
        )
    ):
        yield begin + unit * (2 + n // 2)
        copy.wait_recv()
        arrivals.append(onward(((0,) + place[1:], place), core))
    yield begin + unit * 3.1
    for copy in arrivals:
        copy.wait_recv()


def add_rows(target, other):
    if target.shape[-2] % 16 == 0:
        count = target.shape[-2] // 16

        def part(step):
            return (pl.ds(pl.multiple_of(step * 16, 16), 16), slice(None))

    else:
        assert target.shape[-1] % 128 == 0
        count = target.shape[-1] // 128

        def part(step):
            return (slice(None), pl.ds(pl.multiple_of(step * 128, 128), 128))

    for lead in range(math.prod(target.shape[:-2])):
        a, b = target, other
        if len(target.shape) > 2:
            a, b = target.at[lead], other.at[lead]

        @pl.loop(0, count)
        def _(step):
            here = part(step)
            a[here] = (a[here].astype(jnp.float32) + b[here].astype(jnp.float32)).astype(a.dtype)


def octet_reduce_steps(board, terms_ref, sum_ref, mine, from_core, from_link, begin=0.0):
    h = sum_ref.shape[0] // 2
    unit = 2.2 * math.prod(sum_ref.shape) / LINK
    core, along_x, along_y = ("plane", 1), ("plane", 2), "y"
    order = (
        (1, 1, 0),
        (1, 1, 1),
        (0, 1, 0),
        (1, 0, 1),
        (1, 0, 0),
        (0, 1, 1),
        (0, 0, 0),
        (0, 0, 1),
    )
    over_core = {}
    loads = {}
    for x, y, half in order:
        place = octet_place(0, x, y, half)
        loads[place] = board.move(
            terms_ref.at[pl.ds(place * h, h)], mine.at[place], close=False
        )
        over_core[place] = board.send(
            terms_ref.at[pl.ds((8 + place) * h, h)], from_core.at[place], core
        )

    def add_core(x, y, half):
        place = octet_place(0, x, y, half)
        loads[place].wait()
        over_core[place].wait_recv()
        add_rows(mine.at[place], from_core.at[place])
        return place

    second = {}
    for n, (x, y, half) in enumerate(order[:4]):
        yield begin + 0.1 * unit * (n + 1)
        place = add_core(x, y, half)
        second[(x, y, half)] = board.send(
            mine.at[place], from_link.at[n], along_y if half == 0 else along_x
        )
    third = {}
    for n, (x, y, half) in enumerate(order[4:6]):
        yield begin + unit * 1.2
        place = add_core(x, y, half)
        second[(1, 1, half)].wait_recv()
        add_rows(mine.at[place], from_link.at[half])
        third[half] = board.send(
            mine.at[place], from_link.at[4 + n], along_x if half == 0 else along_y
        )
    for half, sent in ((0, (0, 1, 0)), (1, (1, 0, 1))):
        yield begin + unit * 3.1
        place = add_core(0, 0, half)
        second[sent].wait_recv()
        third[half].wait_recv()

        @pl.loop(0, h // 16)
        def _(step):
            rows = pl.ds(pl.multiple_of(step * 16, 16), 16)
            out_rows = pl.ds(pl.multiple_of(half * h + step * 16, 16), 16)
            sum_ref[out_rows, :] = (
                mine[place, rows, :].astype(jnp.float32)
                + from_link[2 + half, rows, :].astype(jnp.float32)
                + from_link[4 + half, rows, :].astype(jnp.float32)
            )


def line_gather_steps(board, shard_ref, whole_ref, begin=0.0):
    unit = 4.4 * math.prod(shard_ref.shape) / LINK
    z = board.z
    far, near = board.line_xor(2), ("line", 1)
    two = board.send(shard_ref, whole_ref.at[z], ("line", 2))
    one = board.send(shard_ref, whole_ref.at[z], near)
    three_slot, on_slot = board.slot(), board.slot()
    three = board.make(three_slot, shard_ref, whole_ref.at[z], ("line", 3))
    onward = pltpu.make_async_remote_copy(
        src_ref=whole_ref.at[far],
        dst_ref=whole_ref.at[far],
        send_sem=board.sems[0].at[on_slot],
        recv_sem=board.sems[1].at[three_slot],
        device_id=board.device(near),
        device_id_type=MESH,
    )

    @pl.when(board.middle)
    def _():
        three.start()

    keep = board.move(shard_ref, whole_ref.at[z], close=False)
    yield begin + 2.0 * unit
    two.wait_recv()

    @pl.when(board.middle)
    def _():
        onward.start()

    yield begin + 3.1 * unit
    keep.wait()
    one.wait_recv()
    three.wait_recv()

    @pl.when(board.middle)
    def _():
        three.wait_send()
        onward.wait_send()


def line_reduce_steps(board, terms_ref, got_ref, held, carried, begin=0.0):
    unit = 4.4 * math.prod(got_ref.shape[1:]) / LINK
    near, two_off, three_off = ("line", 1), ("line", 2), ("line", 3)
    z_near, z_two, z_three = (board.line_xor(k) for k in (1, 2, 3))
    carry = board.make(board.slot(), terms_ref.at[z_three], carried, near)
    direct = board.make(board.slot(), terms_ref.at[z_three], got_ref.at[2], three_off)
    two_slot = board.slot()
    two_end = board.make(two_slot, terms_ref.at[z_two], got_ref.at[1], two_off)
    two_mid = board.make(two_slot, held, got_ref.at[1], two_off)

    @pl.when(jnp.logical_not(board.middle))
    def _():
        carry.start()
        two_end.start()

    @pl.when(board.middle)
    def _():
        direct.start()

    one = board.send(terms_ref.at[z_near], got_ref.at[0], near)
    load = board.move(terms_ref.at[z_two], held, close=False)
    yield begin + 1.3 * unit
    load.wait()

    @pl.when(board.middle)
    def _():
        carry.wait_recv()
        add_rows(held, carried)
        two_mid.start()

    yield begin + 3.1 * unit
    one.wait_recv()
    two_end.wait_recv()
    two_end.wait_send()

    @pl.when(board.middle)
    def _():
        direct.wait_recv()
        direct.wait_send()

    @pl.when(jnp.logical_not(board.middle))
    def _():
        carry.wait_send()


def plane_exchange_steps(board, blocks_ref, given_ref, begin=0.0):
    copies = [
        board.send(
            blocks_ref.at[board.place_xor(k)], given_ref.at[board.i], ("plane", k)
        )
        for k in (3, 2, 1)
    ]
    keep = board.move(blocks_ref.at[board.i], given_ref.at[board.i], close=False)
    yield begin + 9.0 * math.prod(blocks_ref.shape[1:]) / LINK
    for copy in copies:
        copy.wait_recv()
    keep.wait()


def transpose_steps(board, shard_ref, given_ref, begin=0.0):
    slot, spot = board.slot(), board.locals
    board.locals += 1
    other = (board.i * PLANE + board.z, board.t)
    copy = pltpu.make_async_remote_copy(
        src_ref=shard_ref,
        dst_ref=given_ref,
        send_sem=board.sems[0].at[slot],
        recv_sem=board.sems[1].at[slot],
        device_id=other,
        device_id_type=MESH,
    )
    keep = pltpu.make_async_copy(shard_ref, given_ref, board.sems[2].at[spot])

    @pl.when(board.i != board.z)
    def _():
        copy.start()

    @pl.when(board.i == board.z)
    def _():
        keep.start()

    yield begin + 9.0 * math.prod(shard_ref.shape) / LINK

    @pl.when(board.i != board.z)
    def _():
        copy.wait()

    @pl.when(board.i == board.z)
    def _():
        keep.wait()


NEAR_OCTET = (("plane", 1), ("plane", 2), "y")
NEAR_PLANE = (("plane", 1), ("plane", 2), ("plane", 3))
NEAR_LINE = (("line", 1), ("line", 2), ("line", 3))


def hbm(shape):
    return (jax.ShapeDtypeStruct(shape, jnp.bfloat16), HBM_SPEC)


class OctetGather:
    near, remotes, moves = NEAR_OCTET, 13, 1

    def __init__(self, own):
        self.given = own
        self.outs = [hbm((8 * own.shape[0],) + own.shape[1:])]
        self.scratch = []

    def steps(self, board, own, outs, scratch):
        return octet_gather_steps(board, own, outs[0])

    def read(self, outs):
        return outs[0]


class OctetReduce:
    near, remotes, moves = NEAR_OCTET, 14, 8

    def __init__(self, terms):
        self.given = terms
        m, n = terms.shape[0] // 8, terms.shape[1]
        self.outs = [(jax.ShapeDtypeStruct((m, n), jnp.float32), VMEM_SPEC)]
        self.scratch = [pltpu.VMEM((k, m // 2, n), terms.dtype) for k in (8, 8, 6)]

    def steps(self, board, terms, outs, scratch):
        return octet_reduce_steps(board, terms, outs[0], *scratch)

    def read(self, outs):
        return outs[0]


class LineGather:
    near, remotes, moves = NEAR_LINE, 4, 1

    def __init__(self, shard):
        self.given = shard
        self.outs = [hbm((LINE,) + shard.shape)]
        self.scratch = []

    def steps(self, board, shard, outs, scratch):
        return line_gather_steps(board, shard, outs[0])

    def read(self, outs):
        return outs[0]

    def plain(self):
        return lax.all_gather(self.given, "dp", axis_index_groups=line_groups(), axis=0)


class LineReduce:
    near, remotes, moves = NEAR_LINE, 4, 1

    def __init__(self, terms):
        self.given = terms
        shape = terms.shape[1:]
        self.outs = [hbm((3,) + shape)]
        self.scratch = [pltpu.VMEM(shape, terms.dtype)] * 2

    def steps(self, board, terms, outs, scratch):
        return line_reduce_steps(board, terms, outs[0], *scratch)

    def read(self, outs):
        z = line_index()
        got = outs[0].astype(jnp.float32)
        middle = (z == 1) | (z == 2)
        own = take(self.given, z).astype(jnp.float32)
        return own + got[0] + got[1] + jnp.where(middle, got[2], 0.0)

    def plain(self):
        return lax.psum_scatter(
            self.given, "dp", axis_index_groups=line_groups(), scatter_dimension=0
        ).astype(jnp.float32)


class PlaneExchange:
    near, remotes, moves = NEAR_PLANE, 3, 1

    def __init__(self, blocks):
        self.given = blocks
        self.outs = [hbm(blocks.shape)]
        self.scratch = []

    def steps(self, board, blocks, outs, scratch):
        return plane_exchange_steps(board, blocks, outs[0])

    def read(self, outs):
        return outs[0]

    def plain(self):
        i = plane_index()
        whole = jnp.zeros_like(self.given)
        for k in range(PLANE):
            piece = take(self.given, i ^ k)
            if k:
                piece = swap(piece, k)
            whole = lax.dynamic_update_index_in_dim(whole, piece, i ^ k, 0)
        return whole


class GatherColumns:
    near, remotes, moves = NEAR_PLANE + NEAR_LINE, 7, 2

    def __init__(self, blocks):
        self.given = blocks
        self.outs = [hbm(blocks.shape), hbm((LINE,) + blocks.shape)]
        self.scratch = []

    def steps(self, board, blocks, outs, scratch):
        begin = 9.0 * math.prod(blocks.shape[1:]) / LINK
        yield from plane_exchange_steps(board, blocks, outs[0])
        yield from line_gather_steps(board, outs[0], outs[1], begin)

    def read(self, outs):
        return outs[1]

    def plain(self):
        return LineGather(PlaneExchange(self.given).plain()).plain()


class GatherPack:
    near, remotes, moves = NEAR_LINE + NEAR_OCTET, 17, 2

    def __init__(self, shard):
        self.given = shard
        self.outs = [hbm((LINE,) + shard.shape), hbm((8 * LINE,) + shard.shape)]
        self.scratch = []

    def steps(self, board, shard, outs, scratch):
        begin = 13.2 * math.prod(shard.shape) / LINK
        yield from line_gather_steps(board, shard, outs[0])
        yield from octet_gather_steps(board, outs[0], outs[1], begin)

    def read(self, outs):
        return outs[1]


class Transpose:
    near, remotes, moves = ("transposed",), 1, 1

    def __init__(self, shard, back=False):
        self.given = shard
        self.back = back
        self.outs = [hbm(shard.shape)]
        self.scratch = []

    def steps(self, board, shard, outs, scratch):
        return transpose_steps(board, shard, outs[0])

    def read(self, outs):
        return outs[0]

    def plain(self):
        line = lax.axis_size("dp") // PLANE
        pairs = [(i * line + z, z * PLANE + i) for i in range(PLANE) for z in range(line)]
        if self.back:
            pairs = [(b, a) for a, b in pairs]
        return lax.ppermute(self.given, "dp", pairs)


def communicate(collective_id, *tasks, compute=None):
    if lax.axis_size("dp") != PLANE * LINE:
        results = []
        for n, task in enumerate(tasks):
            alone = 4 * collective_id + n
            if isinstance(task, (OctetGather, OctetReduce)):
                results += run_kernel(alone, [task])
            elif isinstance(task, GatherPack):
                results += run_kernel(alone, [OctetGather(LineGather(task.given).plain())])
            else:
                results.append(task.plain())
        return results + (run_kernel(None, [], compute) if compute else [])
    return run_kernel(collective_id, tasks, compute)


def run_kernel(collective_id, tasks, compute=None):
    near = []
    for task in tasks:
        near += [name for name in task.near if name not in near]
    n_outs = [len(task.outs) for task in tasks]
    n_scratch = [len(task.scratch) for task in tasks]
    more_givens = compute.givens if compute else []
    more_outs = compute.outs if compute else []
    more_scratch = compute.scratch if compute else []

    def kernel(*refs):
        refs = list(refs)

        def first(count):
            part = refs[:count]
            del refs[:count]
            return part

        givens, compute_givens = first(len(tasks)), first(len(more_givens))
        outs, compute_outs = first(sum(n_outs)), first(len(more_outs))
        scratch, compute_scratch = first(sum(n_scratch)), first(len(more_scratch))
        running, closing = [], []
        if tasks:
            board = Board(*refs)
            closing = board.closing
            board.greet(near)
        for n, task in enumerate(tasks):
            steps = task.steps(
                board,
                givens[n],
                outs[sum(n_outs[:n]) : sum(n_outs[: n + 1])],
                scratch[sum(n_scratch[:n]) : sum(n_scratch[: n + 1])],
            )
            running.append((next(steps), n, steps))
        phases = []
        if compute:
            phases = compute.phases(compute_givens, compute_outs, compute_scratch)
        done = 0.0
        while running or phases:
            running.sort(key=lambda item: item[:2])
            if phases and not (running and running[0][0] <= done):
                phases.pop(0)()
                done += compute.phase_time
                continue
            when, n, steps = running.pop(0)
            when = next(steps, None)
            if when is not None:
                running.append((when, n, steps))
        for close in closing:
            close()

    sems = []
    if tasks:
        sems = [
            pltpu.SemaphoreType.DMA((sum(task.remotes for task in tasks),)),
            pltpu.SemaphoreType.DMA((sum(task.remotes for task in tasks),)),
            pltpu.SemaphoreType.DMA((sum(task.moves for task in tasks),)),
        ]
    outs = pl.pallas_call(
        kernel,
        out_shape=[shape for task in tasks for shape, _ in task.outs] + more_outs,
        in_specs=[HBM_SPEC] * len(tasks) + [VMEM_SPEC] * len(more_givens),
        out_specs=[spec for task in tasks for _, spec in task.outs]
        + [VMEM_SPEC] * len(more_outs),
        scratch_shapes=[shape for task in tasks for shape in task.scratch]
        + more_scratch
        + sems,
        compiler_params=pltpu.CompilerParams(
            collective_id=collective_id,
            has_side_effects=bool(tasks),
            vmem_limit_bytes=VMEM_LIMIT,
        ),
        cost_estimate=pl.CostEstimate(flops=0, bytes_accessed=2**28, transcendentals=0),
    )(*[task.given for task in tasks], *more_givens)
    results = [
        task.read(outs[sum(n_outs[:n]) : sum(n_outs[: n + 1])]) for n, task in enumerate(tasks)
    ]
    return results + ([outs[sum(n_outs) :]] if compute else [])


def take(array, position):
    return lax.dynamic_index_in_dim(array, position, 0, keepdims=False)


def line_index():
    return lax.axis_index("dp") // PLANE


def plane_index():
    return lax.axis_index("dp") % PLANE


def line_groups():
    size = lax.axis_size("dp")
    return [[i + PLANE * z for z in range(size // PLANE)] for i in range(PLANE)]


def swap(array, bits):
    size = lax.axis_size("dp")
    return lax.ppermute(array, "dp", [(d, d ^ bits) for d in range(size)])


HEAD = 128
ROW_BLOCK = 256


def column_dot(left_side, right_side):
    return jnp.dot(left_side, right_side, preferred_element_type=jnp.float32)


def lane_index(shape):
    return lax.broadcasted_iota(jnp.int32, shape, len(shape) - 1)


def turn(values, wave, low_wave, high_wave):
    half = DR // 2
    return (
        values * wave
        + pltpu.roll(values, HEAD - half, 1) * low_wave
        + pltpu.roll(values, half, 1) * high_wave
    )


def score_bias(keys_ref, bounds_ref, bias, pack, pack_rows):
    @pl.loop(0, pack_rows // ROW_BLOCK)
    def _(block):
        rows = pl.ds(pl.multiple_of(block * ROW_BLOCK, ROW_BLOCK), ROW_BLOCK)
        here = bounds_ref[pl.ds(pack * pack_rows + block * ROW_BLOCK, ROW_BLOCK), :]
        key = keys_ref[pack, 0:1, :]
        allowed = (key >= here[:, 0:1]) & (key <= here[:, 1:2])
        bias[rows, :] = jnp.where(allowed, 0.0, MASKED)


class AttentionForward:
    def __init__(self, tokens, keys, bounds, waves, query_up, latent_up, packs, heads):
        rows = tokens.shape[0]
        self.packs, self.heads, self.pack_rows = packs, heads, rows // packs
        self.givens = [tokens, keys, bounds, *waves, query_up, latent_up]
        low = jnp.bfloat16
        self.pairs = -(-heads // 2)
        self.outs = [
            jax.ShapeDtypeStruct((rows, heads * HEAD), low),
            jax.ShapeDtypeStruct((rows, heads * HEAD), low),
            jax.ShapeDtypeStruct((rows, self.pairs * HEAD), low),
            jax.ShapeDtypeStruct((rows, HEAD), jnp.float32),
        ]
        self.scratch = [
            pltpu.VMEM((self.pack_rows, self.pack_rows), jnp.float32),
            pltpu.VMEM((self.pack_rows, HEAD), low),
        ]
        self.phase_time = 10.0

    def phases(self, givens, outs, scratch):
        tokens, keys, bounds, wave, low_wave, high_wave, query_up, latent_up = givens
        queries, heads_out, mixed, totals = outs
        bias, keys_tile = scratch
        scale = QH ** (-0.5)
        size = self.pack_rows

        def run(pack):
            score_bias(keys, bounds, bias, pack, size)
            start = pack * size
            rope_key = tokens[start : start + size, QR + KVR : QR + KVR + HEAD]
            for n in range(self.pairs):
                mixed[start : start + size, n * HEAD : (n + 1) * HEAD] = jnp.zeros(
                    (size, HEAD), mixed.dtype
                )
            totals[start : start + size, :] = jnp.zeros((size, HEAD), jnp.float32)

            @pl.loop(0, self.heads)
            def _(head):
                lanes = pl.ds(pl.multiple_of(head * HEAD, HEAD), HEAD)
                pair = pl.ds(pl.multiple_of((head // 2) * HEAD, HEAD), HEAD)
                tile = column_dot(
                    tokens[start : start + size, QR : QR + KVR], latent_up[:, lanes]
                ).astype(jnp.bfloat16)
                heads_out[start : start + size, lanes] = tile
                lane = lane_index((size, HEAD))
                keys_tile[...] = jnp.where(
                    lane < DN,
                    tile.astype(jnp.float32),
                    pltpu.roll(rope_key.astype(jnp.float32), DN, 1),
                ).astype(jnp.bfloat16)

                @pl.loop(0, size // ROW_BLOCK)
                def _(block):
                    at = pl.multiple_of(start + block * ROW_BLOCK, ROW_BLOCK)
                    rows = pl.ds(at, ROW_BLOCK)
                    raw = column_dot(tokens[rows, 0:QR], query_up[:, lanes])
                    query = turn(
                        raw, wave[rows, :], low_wave[rows, :], high_wave[rows, :]
                    ).astype(jnp.bfloat16)
                    queries[rows, lanes] = query
                    scores = right_transposed(query, keys_tile[...]) * scale + bias[
                        pl.ds(pl.multiple_of(block * ROW_BLOCK, ROW_BLOCK), ROW_BLOCK), :
                    ]
                    top = jnp.max(scores, axis=1, keepdims=True)
                    exponent = jnp.exp(scores - top)
                    total = jnp.sum(exponent, axis=1, keepdims=True)
                    prob = (exponent * (1.0 / total)).astype(jnp.bfloat16)
                    out = column_dot(prob, heads_out[start : start + size, lanes])
                    lane = lane_index((ROW_BLOCK, HEAD))
                    totals[rows, :] = jnp.where(
                        lane == head, top + jnp.log(total), totals[rows, :]
                    )
                    even = head % 2 == 0
                    placed = jnp.where(even, pltpu.roll(out, DN, 1), out)
                    before = mixed[rows, pair].astype(jnp.float32)
                    mixed[rows, pair] = jnp.where(
                        (lane < DN) == even, placed, before
                    ).astype(mixed.dtype)

        return [functools.partial(run, pack) for pack in range(self.packs)]


class AttentionBackward:
    def __init__(
        self,
        queries,
        latent_heads,
        totals,
        grad_mixed,
        tokens,
        keys,
        bounds,
        waves,
        query_up,
        latent_up,
        packs,
        heads,
    ):
        rows = tokens.shape[0]
        self.packs, self.heads, self.pack_rows = packs, heads, rows // packs
        self.givens = [
            queries,
            latent_heads,
            totals,
            grad_mixed,
            tokens,
            keys,
            bounds,
            *waves,
            query_up,
            latent_up,
        ]
        low = jnp.bfloat16
        self.outs = [
            jax.ShapeDtypeStruct((rows, heads * HEAD), low),
            jax.ShapeDtypeStruct((rows, heads * HEAD), low),
            jax.ShapeDtypeStruct((rows, QR + KVR + HEAD), low),
        ]
        size = self.pack_rows
        self.scratch = [
            pltpu.VMEM((size, size), jnp.float32),
            pltpu.VMEM((size, HEAD), low),
            pltpu.VMEM((size, HEAD), jnp.float32),
            pltpu.VMEM((size, HEAD), jnp.float32),
            pltpu.VMEM((size, HEAD), jnp.float32),
        ]
        self.phase_time = 14.0

    def phases(self, givens, outs, scratch):
        (
            queries,
            heads_in,
            totals,
            grad_mixed,
            tokens,
            keys,
            bounds,
            wave,
            low_wave,
            high_wave,
            query_up,
            latent_up,
        ) = givens
        grad_queries, grad_heads, terms = outs
        bias, keys_tile, grad_key, grad_value, grad_rope = scratch
        scale = QH ** (-0.5)
        size = self.pack_rows

        def run(pack):
            score_bias(keys, bounds, bias, pack, size)
            start = pack * size
            rope_key = tokens[start : start + size, QR + KVR : QR + KVR + HEAD]
            grad_rope[...] = jnp.zeros_like(grad_rope)

            @pl.loop(0, self.heads)
            def _(head):
                lanes = pl.ds(pl.multiple_of(head * HEAD, HEAD), HEAD)
                pair = pl.ds(pl.multiple_of((head // 2) * HEAD, HEAD), HEAD)
                lane = lane_index((size, HEAD))
                keys_tile[...] = jnp.where(
                    lane < DN,
                    heads_in[start : start + size, lanes].astype(jnp.float32),
                    pltpu.roll(rope_key.astype(jnp.float32), DN, 1),
                ).astype(jnp.bfloat16)
                grad_key[...] = jnp.zeros_like(grad_key)
                grad_value[...] = jnp.zeros_like(grad_value)

                @pl.loop(0, size // ROW_BLOCK)
                def _(block):
                    at = pl.multiple_of(start + block * ROW_BLOCK, ROW_BLOCK)
                    rows = pl.ds(at, ROW_BLOCK)
                    lane = lane_index((ROW_BLOCK, HEAD))
                    query = queries[rows, lanes]
                    key_all = keys_tile[...]
                    scores = right_transposed(query, key_all) * scale + bias[
                        pl.ds(pl.multiple_of(block * ROW_BLOCK, ROW_BLOCK), ROW_BLOCK), :
                    ]
                    total = jnp.sum(
                        jnp.where(lane == head, totals[rows, :], 0.0), axis=1, keepdims=True
                    )
                    prob = jnp.exp(scores - total)
                    grad_pair = grad_mixed[rows, pair].astype(jnp.float32)
                    even = head % 2 == 0
                    grad_out = jnp.where(
                        lane < DN, 0.0, jnp.where(even, pltpu.roll(grad_pair, DN, 1), grad_pair)
                    ).astype(jnp.bfloat16)
                    grad_prob = right_transposed(grad_out, heads_in[start : start + size, lanes])
                    inner = jnp.sum(prob * grad_prob, axis=1, keepdims=True)
                    grad_score = (prob * (grad_prob - inner)).astype(jnp.bfloat16)
                    grad_value[...] += left_transposed(prob.astype(jnp.bfloat16), grad_out)
                    grad_key[...] += left_transposed(grad_score, query)
                    grad_query = column_dot(grad_score, key_all) * scale
                    grad_queries[rows, lanes] = turn(
                        grad_query, wave[rows, :], -low_wave[rows, :], -high_wave[rows, :]
                    ).astype(grad_queries.dtype)

                scaled = grad_key[...] * scale
                grad_rope[...] += scaled
                grad_heads[start : start + size, lanes] = jnp.where(
                    lane < DN, scaled, grad_value[...]
                ).astype(grad_heads.dtype)

            @pl.loop(0, size // ROW_BLOCK)
            def _(block):
                at = pl.multiple_of(start + block * ROW_BLOCK, ROW_BLOCK)
                rows = pl.ds(at, ROW_BLOCK)
                here = pl.ds(pl.multiple_of(block * ROW_BLOCK, ROW_BLOCK), ROW_BLOCK)
                terms[rows, 0:QR] = right_transposed(grad_queries[rows, :], query_up[...]).astype(
                    terms.dtype
                )
                terms[rows, QR : QR + KVR] = right_transposed(
                    grad_heads[rows, :], latent_up[...]
                ).astype(terms.dtype)
                terms[rows, QR + KVR :] = pltpu.roll(grad_rope[here, :], HEAD - DN, 1).astype(
                    terms.dtype
                )

        return [functools.partial(run, pack) for pack in range(self.packs)]


def positions(segment_ids):
    token_index = jnp.arange(segment_ids.shape[0], dtype=jnp.int32)
    doc_start = jnp.concatenate(
        [jnp.ones((1,), dtype=jnp.bool_), segment_ids[1:] != segment_ids[:-1]]
    )
    starts = lax.cummax(jnp.where(doc_start, token_index, 0), axis=0)
    return token_index - starts


def rope_tables(position):
    exponent = jnp.arange(DR // 2, dtype=jnp.float32) * (2.0 / DR)
    rope_angle = position[:, None] * (ROPE_BASE ** (-exponent))[None, :]
    return (jnp.cos(rope_angle), jnp.sin(rope_angle))


def local(
    inputs,
    cotangent,
    segment_ids,
    gains,
    gains_first,
    gains_second,
    query_down,
    query_down_first,
    query_down_second,
    latent_down,
    latent_down_first,
    latent_down_second,
    query_up,
    query_up_first,
    query_up_second,
    latent_up,
    latent_up_first,
    latent_up_second,
    output_proj,
    output_proj_first,
    output_proj_second,
    gate_proj,
    gate_proj_first,
    gate_proj_second,
    up_proj,
    up_proj_first,
    up_proj_second,
    down_proj,
    down_proj_first,
    down_proj_second,
):
    size = lax.axis_size("dp")
    tensor = lax.axis_size("tensor")
    line = size // PLANE
    z, i, t = line_index(), plane_index(), lax.axis_index("tensor")
    half_rows = inputs.shape[0]
    pack_rows = segment_ids.shape[0]
    packs = PLANE
    rows_all = packs * pack_rows
    low = jnp.bfloat16
    local_heads = H // (PLANE * tensor)
    units = FF // (PLANE * tensor)
    mixed_width = -(-local_heads // 2) * HEAD

    def column_blocks(weight, columns):
        return weight.astype(low).reshape(-1, PLANE, columns).transpose(1, 0, 2)

    def unit_blocks(weight):
        return (
            weight.astype(low)
            .reshape(weight.shape[0], line, PLANE, units // line)
            .transpose(2, 0, 1, 3)
            .reshape(PLANE, weight.shape[0], units)
        )

    down_rows = query_down.shape[0]
    pack_height = down_rows + 16
    gain_width = gains.shape[0]
    down_pack = jnp.concatenate(
        [
            jnp.concatenate([query_down, latent_down], axis=1).astype(low),
            jnp.pad(gains.astype(low)[None], ((0, 15), (0, QR + KVR + DR - gain_width))),
        ],
        axis=0,
    )
    def head_blocks(weight):
        blocks = weight.astype(low).reshape(-1, PLANE, local_heads, QH)
        blocks = jnp.pad(blocks, ((0, 0), (0, 0), (0, 0), (0, HEAD - QH)))
        return blocks.reshape(-1, PLANE, local_heads * HEAD).transpose(1, 0, 2)

    pack_all, query_up_all, latent_up_all, gate_plane, output_moved = communicate(
        1,
        GatherPack(down_pack),
        GatherColumns(head_blocks(query_up)),
        GatherColumns(column_blocks(latent_up, local_heads * KH)),
        PlaneExchange(unit_blocks(gate_proj)),
        Transpose(output_proj.astype(low)),
    )
    query_up_all = query_up_all.reshape(QR, local_heads * HEAD)
    latent_up_all = latent_up_all.reshape(KVR, local_heads * KH)
    down_octet = pack_all.reshape(2, 2, tensor, line, pack_height, QR + KVR + DR)
    down_blocks = jnp.zeros((PLANE, tensor, line, pack_height, QR + KVR + DR), low)
    for k in range(PLANE):
        for y in range(tensor):
            down_blocks = lax.dynamic_update_slice(
                down_blocks,
                down_octet[k % 2, k // 2, y][None, None],
                (i ^ k, (t + y) % tensor, 0, 0, 0),
            )
    down_blocks = down_blocks.transpose(2, 0, 1, 3, 4)
    down_both = down_blocks[..., :down_rows, :].reshape(D, QR + KVR + DR)
    gain_values = down_blocks[..., down_rows, :gain_width].reshape(-1).astype(jnp.float32)
    gain_attention = gain_values[:D]
    gain_query = gain_values[D : D + QR]
    gain_latent = gain_values[D + QR : D + QR + KVR]
    gain_ffn = gain_values[D + QR + KVR :]

    incoming = inputs.astype(jnp.float32)
    attn_unit, inverse_attention = norm_forward(incoming, gain_attention)
    normed_attn = attn_unit.astype(low)
    both_latent = jnp.dot(normed_attn, down_both, preferred_element_type=jnp.float32)
    query_latent = both_latent[:, :QR]
    latent = both_latent[:, QR:]
    query_unit, inverse_query = norm_forward(query_latent, gain_query)
    latent_unit, inverse_latent = norm_forward(latent[:, :KVR], gain_latent)
    own_position = lax.dynamic_slice_in_dim(positions(segment_ids), t * half_rows, half_rows)
    own_segment = lax.dynamic_slice_in_dim(segment_ids, t * half_rows, half_rows)
    own_cosine, own_sine = rope_tables(own_position.astype(jnp.float32))
    own_rope_key = rotate(latent[:, KVR:], own_cosine, own_sine)
    marks = jnp.stack(
        [own_segment // 16, own_segment % 16, own_position // 16, own_position % 16], axis=1
    )
    tokens_own = jnp.concatenate(
        [
            query_unit.astype(low),
            latent_unit.astype(low),
            own_rope_key.astype(low),
            marks.astype(low),
            jnp.zeros((half_rows, 128 - DR - 4), low),
        ],
        axis=1,
    )
    tokens_all, output_all = communicate(3, OctetGather(tokens_own), LineGather(output_moved))
    output_all = jnp.pad(
        output_all.reshape(local_heads * DV, D), ((0, mixed_width - local_heads * DV), (0, 0))
    )
    marks_all = tokens_all[:, QR + KVR + DR : QR + KVR + DR + 4].astype(jnp.float32)
    key_base = (marks_all[:, 0] * 16.0 + marks_all[:, 1]) * pack_rows
    position = marks_all[:, 2] * 16.0 + marks_all[:, 3]
    key = key_base + position
    keys = jnp.broadcast_to(key.reshape(packs, 1, pack_rows), (packs, 8, pack_rows))
    bounds = jnp.pad(jnp.stack([key_base, key], axis=1), ((0, 0), (0, HEAD - 2)))
    rope_cosine, rope_sine = rope_tables(position)
    nothing = jnp.zeros((rows_all, DR), jnp.float32)
    still = jnp.zeros((rows_all, DN), jnp.float32)
    waves = (
        jnp.concatenate([still + 1.0, rope_cosine, rope_cosine, nothing], axis=1),
        jnp.concatenate([still, -rope_sine, nothing, nothing[:, : DR // 2]], axis=1),
        jnp.concatenate([still, nothing[:, : DR // 2], rope_sine, nothing], axis=1),
    )
    grad_ffn, up_plane, gate_all, (queries, latent_heads, mixed_heads, log_totals) = communicate(
        2,
        OctetGather((RESIDUAL * cotangent.astype(jnp.float32)).astype(low)),
        PlaneExchange(unit_blocks(up_proj)),
        LineGather(gate_plane),
        compute=AttentionForward(
            tokens_all, keys, bounds, waves, query_up_all, latent_up_all, packs, local_heads
        ),
    )
    gate_all = gate_all.reshape(D, units)
    attention_terms = jnp.dot(mixed_heads, output_all, preferred_element_type=jnp.float32)
    attention_sum, up_all = communicate(
        4, OctetReduce(attention_terms.astype(low)), LineGather(up_plane)
    )
    up_all = up_all.reshape(D, units)
    residual = incoming + RESIDUAL * attention_sum

    ffn_unit, inverse_ffn = norm_forward(residual, gain_ffn)
    normed_ffn, down_all = communicate(
        5, OctetGather(ffn_unit.astype(low)), LineGather(down_proj.astype(low))
    )
    down_all = down_all.reshape(units, D)
    gate_value = jnp.dot(normed_ffn, gate_all, preferred_element_type=jnp.float32)
    up_value = jnp.dot(normed_ffn, up_all, preferred_element_type=jnp.float32)
    gate_sigmoid = lax.logistic(gate_value)
    silu_gate = gate_value * gate_sigmoid
    hidden = (silu_gate * up_value).astype(low)
    grad_hidden = right_transposed(grad_ffn, down_all)
    grad_gate = (
        grad_hidden * up_value * gate_sigmoid * (1.0 + gate_value * (1.0 - gate_sigmoid))
    ).astype(low)
    grad_up = (grad_hidden * silu_gate).astype(low)
    ffn_back_terms = right_transposed(grad_gate, gate_all) + right_transposed(grad_up, up_all)
    down_grad = left_transposed(hidden, grad_ffn).astype(low).reshape(line, -1, D)
    gate_grad = left_transposed(normed_ffn, grad_gate).astype(low)
    up_grad = left_transposed(normed_ffn, grad_up).astype(low)
    ffn_terms = jnp.dot(hidden, down_all, preferred_element_type=jnp.float32).astype(low)
    grad_normed_ffn, down_shard = communicate(
        6, OctetReduce(ffn_back_terms.astype(low)), LineReduce(down_grad)
    )
    outer_grad = cotangent.astype(jnp.float32)
    grad_incoming_ffn, gain_ffn_grad = norm_backward(
        residual, inverse_ffn, gain_ffn, grad_normed_ffn
    )
    grad_residual = outer_grad + grad_incoming_ffn

    grad_branch, gate_sum = communicate(
        7,
        OctetGather((RESIDUAL * grad_residual).astype(low)),
        LineReduce(gate_grad.reshape(line, PLANE, -1, units)),
    )
    output_grad = (
        left_transposed(mixed_heads, grad_branch)
        .astype(low)[: local_heads * DV]
        .reshape(line, -1, D)
    )
    grad_mixed = right_transposed(grad_branch, output_all).astype(low)
    ffn_sum, up_sum, (grad_query_heads, grad_latent_heads, grad_unit_terms) = communicate(
        8,
        OctetReduce(ffn_terms),
        LineReduce(up_grad.reshape(line, PLANE, -1, units)),
        compute=AttentionBackward(
            queries,
            latent_heads,
            log_totals,
            grad_mixed,
            tokens_all,
            keys,
            bounds,
            waves,
            query_up_all,
            latent_up_all,
            packs,
            local_heads,
        ),
    )
    block_output = (residual + RESIDUAL * ffn_sum).astype(low)
    query_up_grad = left_transposed(tokens_all[:, :QR], grad_query_heads).astype(low)
    latent_up_grad = left_transposed(tokens_all[:, QR : QR + KVR], grad_latent_heads).astype(low)
    grad_units, output_sum, gate_parts = communicate(
        9,
        OctetReduce(grad_unit_terms),
        LineReduce(output_grad),
        PlaneExchange(gate_sum.astype(low)),
    )
    grad_query_wide, gain_query_grad = norm_backward(
        query_latent, inverse_query, gain_query, grad_units[:, :QR]
    )
    grad_latent_part, gain_latent_grad = norm_backward(
        latent[:, :KVR], inverse_latent, gain_latent, grad_units[:, QR : QR + KVR]
    )
    grad_rope = unrotate(grad_units[:, QR + KVR : QR + KVR + DR], own_cosine, own_sine)
    grad_both = jnp.concatenate([grad_query_wide, grad_latent_part, grad_rope], axis=1).astype(low)
    down_both_grad = left_transposed(normed_attn, grad_both).astype(low)
    grad_normed_attn = right_transposed(grad_both, down_both)
    grad_incoming_attn, gain_attention_grad = norm_backward(
        incoming, inverse_attention, gain_attention, grad_normed_attn
    )
    input_grad = (grad_residual + grad_incoming_attn).astype(low)
    gains_grad = jnp.concatenate(
        [gain_attention_grad, gain_query_grad, gain_latent_grad, gain_ffn_grad]
    ).astype(low)
    pack_grad = jnp.concatenate(
        [
            down_both_grad.reshape(line, PLANE, tensor, down_rows, QR + KVR + DR),
            jnp.pad(
                gains_grad.reshape(line, PLANE, tensor, 1, gain_width),
                ((0, 0), (0, 0), (0, 0), (0, 15), (0, QR + KVR + DR - gain_width)),
            ),
        ],
        axis=3,
    ).transpose(1, 2, 0, 3, 4)
    pack_terms = jnp.concatenate(
        [
            lax.dynamic_slice(
                pack_grad,
                (i ^ (core + 2 * x), (t + y) % tensor, 0, 0, 0),
                (1, 1) + pack_grad.shape[2:],
            ).reshape(line * pack_height, QR + KVR + DR)
            for core in range(2)
            for x in range(2)
            for y in range(tensor)
        ],
        axis=0,
    )
    pack_octet, query_up_sum, latent_up_sum, up_parts, output_shard = communicate(
        10,
        OctetReduce(pack_terms),
        LineReduce(query_up_grad.reshape(line, PLANE, -1, local_heads * HEAD)),
        LineReduce(latent_up_grad.reshape(line, PLANE, -1, local_heads * KH)),
        PlaneExchange(up_sum.astype(low)),
        Transpose(output_sum.astype(low), back=True),
    )
    pack_sum, query_up_parts, latent_up_parts = communicate(
        11,
        LineReduce(pack_octet.astype(low).reshape(line, pack_height, QR + KVR + DR)),
        PlaneExchange(query_up_sum.astype(low)),
        PlaneExchange(latent_up_sum.astype(low)),
    )
    query_down_shard = pack_sum[:down_rows, :QR]
    latent_down_shard = pack_sum[:down_rows, QR:]
    gains_shard = pack_sum[down_rows, :gain_width]

    def unit_columns(blocks):
        return (
            blocks.astype(jnp.float32)
            .reshape(PLANE, -1, line, units // line)
            .transpose(1, 2, 0, 3)
            .reshape(-1, PLANE * units)
        )

    def head_columns(blocks):
        return blocks.astype(jnp.float32).transpose(1, 0, 2).reshape(blocks.shape[1], -1)

    gate_shard, up_shard = unit_columns(gate_parts), unit_columns(up_parts)
    query_up_parts = query_up_parts.reshape(PLANE, -1, local_heads, HEAD)[..., :QH]
    query_up_shard = head_columns(query_up_parts.reshape(PLANE, -1, local_heads * QH))
    latent_up_shard = head_columns(latent_up_parts)
    output_shard = output_shard.astype(jnp.float32)

    gains_out = adamw_update(gains, gains_first, gains_second, gains_shard, GAIN_RATE)
    query_down_out = adamw_update(
        query_down, query_down_first, query_down_second, query_down_shard, matrix_rate(D)
    )
    latent_down_out = adamw_update(
        latent_down, latent_down_first, latent_down_second, latent_down_shard, matrix_rate(D)
    )
    query_up_out = adamw_update(
        query_up, query_up_first, query_up_second, query_up_shard, matrix_rate(QR)
    )
    latent_up_out = adamw_update(
        latent_up, latent_up_first, latent_up_second, latent_up_shard, matrix_rate(KVR)
    )
    output_out = adamw_update(
        output_proj, output_proj_first, output_proj_second, output_shard, matrix_rate(H * DV // 64)
    )
    gate_out = adamw_update(
        gate_proj, gate_proj_first, gate_proj_second, gate_shard, matrix_rate(D)
    )
    up_out = adamw_update(up_proj, up_proj_first, up_proj_second, up_shard, matrix_rate(D))
    down_out = adamw_update(
        down_proj, down_proj_first, down_proj_second, down_shard, matrix_rate(FF // 8)
    )
    return (
        block_output,
        input_grad,
        gains_out[0],
        gains_out[1],
        gains_out[2],
        query_down_out[0],
        query_down_out[1],
        query_down_out[2],
        latent_down_out[0],
        latent_down_out[1],
        latent_down_out[2],
        query_up_out[0],
        query_up_out[1],
        query_up_out[2],
        latent_up_out[0],
        latent_up_out[1],
        latent_up_out[2],
        output_out[0],
        output_out[1],
        output_out[2],
        gate_out[0],
        gate_out[1],
        gate_out[2],
        up_out[0],
        up_out[1],
        up_out[2],
        down_out[0],
        down_out[1],
        down_out[2],
    )


def solution(mesh):
    in_specs = (
        P(("dp", "tensor"), None),
        P(("dp", "tensor"), None),
        P("dp"),
        P(("dp", "tensor")),
        P(("dp", "tensor")),
        P(("dp", "tensor")),
        P(("dp", "tensor"), None),
        P(("dp", "tensor"), None),
        P(("dp", "tensor"), None),
        P(("dp", "tensor"), None),
        P(("dp", "tensor"), None),
        P(("dp", "tensor"), None),
        P("dp", "tensor"),
        P("dp", "tensor"),
        P("dp", "tensor"),
        P("dp", "tensor"),
        P("dp", "tensor"),
        P("dp", "tensor"),
        P(("tensor", "dp"), None),
        P(("tensor", "dp"), None),
        P(("tensor", "dp"), None),
        P("dp", "tensor"),
        P("dp", "tensor"),
        P("dp", "tensor"),
        P("dp", "tensor"),
        P("dp", "tensor"),
        P("dp", "tensor"),
        P(("tensor", "dp"), None),
        P(("tensor", "dp"), None),
        P(("tensor", "dp"), None),
    )
    out_specs = (
        P(("dp", "tensor"), None),
        P(("dp", "tensor"), None),
        P(("dp", "tensor")),
        P(("dp", "tensor")),
        P(("dp", "tensor")),
        P(("dp", "tensor"), None),
        P(("dp", "tensor"), None),
        P(("dp", "tensor"), None),
        P(("dp", "tensor"), None),
        P(("dp", "tensor"), None),
        P(("dp", "tensor"), None),
        P("dp", "tensor"),
        P("dp", "tensor"),
        P("dp", "tensor"),
        P("dp", "tensor"),
        P("dp", "tensor"),
        P("dp", "tensor"),
        P(("tensor", "dp"), None),
        P(("tensor", "dp"), None),
        P(("tensor", "dp"), None),
        P("dp", "tensor"),
        P("dp", "tensor"),
        P("dp", "tensor"),
        P("dp", "tensor"),
        P("dp", "tensor"),
        P("dp", "tensor"),
        P(("tensor", "dp"), None),
        P(("tensor", "dp"), None),
        P(("tensor", "dp"), None),
    )
    return jax.shard_map(local, mesh=mesh, in_specs=in_specs, out_specs=out_specs, check_vma=False)
```

```python
import functools
import math

import jax
import jax.numpy as jnp
from jax import lax
from jax.experimental import pallas as pl
from jax.experimental.pallas import tpu as pltpu
from jax.sharding import PartitionSpec as P

D = 2560
H = 40
DN = 64
DR = 32
DV = 64
QR = 768
KVR = 256
FF = 6400
STEP = 10
QH = 96
KH = 128


RESIDUAL = 1.4 / math.sqrt(62.0)
NORM_EPSILON = 1e-05
MOMENT_DECAY = 0.9
SQUARE_DECAY = 0.95
ADAM_EPSILON = 1e-08
WEIGHT_DECAY = 0.1
GAIN_RATE = 0.3
ROPE_BASE = 10000.0
MASKED = -1e30


def right_transposed(left_side, right_side):
    return lax.dot_general(
        left_side, right_side, (((1,), (1,)), ((), ())), preferred_element_type=jnp.float32
    )


def left_transposed(left_side, right_side):
    return lax.dot_general(
        left_side, right_side, (((0,), (0,)), ((), ())), preferred_element_type=jnp.float32
    )


def norm_forward(values, gain_values):
    inverse = lax.rsqrt(jnp.mean(values * values, axis=-1, keepdims=True) + NORM_EPSILON)
    return (values * inverse * gain_values, inverse)


def norm_backward(values, inverse, gain_values, grad_out):
    unit_values = values * inverse
    weighted = grad_out * gain_values
    grad_values = inverse * (
        weighted - unit_values * jnp.mean(weighted * unit_values, axis=-1, keepdims=True)
    )
    return (grad_values, jnp.sum(grad_out * unit_values, axis=0))


def rotate(values, rope_cosine, rope_sine):
    half_width = values.shape[-1] // 2
    first_half = values[..., :half_width]
    second_half = values[..., half_width:]
    return jnp.concatenate(
        [
            first_half * rope_cosine - second_half * rope_sine,
            second_half * rope_cosine + first_half * rope_sine,
        ],
        axis=-1,
    )


def unrotate(grads_in, rope_cosine, rope_sine):
    half_width = grads_in.shape[-1] // 2
    first_half = grads_in[..., :half_width]
    second_half = grads_in[..., half_width:]
    return jnp.concatenate(
        [
            first_half * rope_cosine + second_half * rope_sine,
            second_half * rope_cosine - first_half * rope_sine,
        ],
        axis=-1,
    )


def adamw_update(weight, first_moment, second_moment, gradient, step_rate):
    new_first = MOMENT_DECAY * first_moment + (1.0 - MOMENT_DECAY) * gradient
    new_second = SQUARE_DECAY * second_moment + (1.0 - SQUARE_DECAY) * gradient * gradient
    first_hat = new_first / (1.0 - MOMENT_DECAY**STEP)
    second_hat = new_second / (1.0 - SQUARE_DECAY**STEP)
    new_weight = weight - step_rate * (
        first_hat / (jnp.sqrt(second_hat) + ADAM_EPSILON) + WEIGHT_DECAY * weight
    )
    return (new_weight, new_first, new_second)


def matrix_rate(fan_in):
    return 2.0 / math.sqrt(fan_in)


PLANE = 4
LINE = 4
LINK = 8.4e4
MESH = pl.DeviceIdType.MESH
VMEM_LIMIT = 56 * 1024 * 1024
HBM_SPEC = pl.BlockSpec(memory_space=pl.ANY)
VMEM_SPEC = pl.BlockSpec(memory_space=pltpu.VMEM)


class Board:
    def __init__(self, send_sems, recv_sems, local_sems):
        self.sems = (send_sems, recv_sems, local_sems)
        self.remotes = 0
        self.locals = 0
        self.closing = []
        self.here = set()
        self.d = lax.axis_index("dp")
        self.t = lax.axis_index("tensor")
        self.z = self.d // PLANE
        self.i = self.d % PLANE
        self.middle = (self.z == 1) | (self.z == 2)
        self.known = {
            name: self.work_out(name) for name in NEAR_OCTET + NEAR_PLANE + NEAR_LINE
        }

    def place_xor(self, k):
        i = self.i
        return (i, i + 1 - 2 * (i % 2), i + 2 - 4 * (i // 2), 3 - i)[k]

    def line_xor(self, k):
        z = self.z
        return (z, z + 1 - 2 * (z % 2), z + 2 - 4 * (z // 2), 3 - z)[k]

    def device(self, name):
        return self.known[name]

    def work_out(self, name):
        if name == "y":
            return (self.d, 1 - self.t)
        kind, k = name
        if kind == "plane":
            return (self.z * PLANE + self.place_xor(k), self.t)
        return (self.line_xor(k) * PLANE + self.i, self.t)

    def greet(self, names):
        barrier = pltpu.get_barrier_semaphore()
        known = [name for name in names if name != "transposed"]
        for name in known:
            pl.semaphore_signal(
                barrier, inc=1, device_id=self.device(name), device_id_type=MESH
            )
        if len(known) == len(names):
            pl.semaphore_wait(barrier, len(known))
            return

        @pl.when(self.i != self.z)
        def _():
            pl.semaphore_signal(
                barrier,
                inc=1,
                device_id=(self.i * PLANE + self.z, self.t),
                device_id_type=MESH,
            )
            pl.semaphore_wait(barrier, len(known) + 1)

        @pl.when(self.i == self.z)
        def _():
            pl.semaphore_wait(barrier, len(known))

    def slot(self):
        self.remotes += 1
        return self.remotes - 1

    def make(self, slot, source, target, name):
        return pltpu.make_async_remote_copy(
            src_ref=source,
            dst_ref=target,
            send_sem=self.sems[0].at[slot],
            recv_sem=self.sems[1].at[slot],
            device_id=self.device(name),
            device_id_type=MESH,
        )

    def send(self, source, target, name):
        copy = self.make(self.slot(), source, target, name)
        copy.start()
        self.closing.append(copy.wait_send)
        return copy

    def move(self, source, target, close=True):
        copy = pltpu.make_async_copy(source, target, self.sems[2].at[self.locals])
        self.locals += 1
        copy.start()
        if close:
            self.closing.append(copy.wait)
        return copy


def octet_place(core, x, y, half):
    return ((core * 2 + x) * 2 + y) * 2 + half


def octet_unit(shape):
    return 2.0 * math.prod(shape) / LINK


def octet_gather_steps(board, own_ref, all_ref, begin=0.0):
    h = own_ref.shape[0] // 2
    unit = octet_unit(own_ref.shape)

    def rows(place, count=1):
        return all_ref.at[pl.ds(place * h, count * h)]

    core, along_x, along_y = ("plane", 1), ("plane", 2), "y"
    first, second = own_ref.at[pl.ds(0, h)], own_ref.at[pl.ds(h, h)]
    first_x = board.send(first, rows(octet_place(0, 1, 0, 0)), along_x)
    second_y = board.send(second, rows(octet_place(0, 0, 1, 1)), along_y)
    first_y = board.send(first, rows(octet_place(0, 0, 1, 0)), along_y)
    second_x = board.send(second, rows(octet_place(0, 1, 0, 1)), along_x)
    whole_core = board.send(own_ref, rows(octet_place(1, 0, 0, 0), 2), core)
    board.move(own_ref, rows(0, 2))

    def onward(start, end, name):
        return board.send(rows(octet_place(*start)), rows(octet_place(*end)), name)

    def to_core(*place):
        return onward((0,) + place, (1,) + place, core)

    yield begin + 0.25 * unit
    whole_core.wait_recv()
    board.here.add((1, 0, 0))
    yield begin + unit
    first_x.wait_recv()
    first_xy = onward((0, 1, 0, 0), (0, 1, 1, 0), along_y)
    core_x = [to_core(1, 0, 0)]
    second_y.wait_recv()
    second_xy = onward((0, 0, 1, 1), (0, 1, 1, 1), along_x)
    core_y = [to_core(0, 1, 1)]
    yield begin + 2.0 * unit
    first_y.wait_recv()
    core_y.append(to_core(0, 1, 0))
    second_x.wait_recv()
    core_x.append(to_core(1, 0, 1))
    board.here.update(((0, 0, 1), (0, 1, 0)))
    yield begin + 2.3 * unit
    for copy in core_x + core_y:
        copy.wait_recv()
    board.here.update(((1, 0, 1), (1, 1, 0)))
    yield begin + 3.0 * unit
    first_xy.wait_recv()
    core_xy = [to_core(1, 1, 0)]
    second_xy.wait_recv()
    core_xy.append(to_core(1, 1, 1))
    board.here.add((0, 1, 1))
    yield begin + 3.3 * unit
    for copy in core_xy:
        copy.wait_recv()
    board.here.add((1, 1, 1))


def add_rows(target, other):
    if target.shape[-2] % 16 == 0:
        count = target.shape[-2] // 16

        def part(step):
            return (pl.ds(pl.multiple_of(step * 16, 16), 16), slice(None))

    else:
        assert target.shape[-1] % 128 == 0
        count = target.shape[-1] // 128

        def part(step):
            return (slice(None), pl.ds(pl.multiple_of(step * 128, 128), 128))

    for lead in range(math.prod(target.shape[:-2])):
        a, b = target, other
        if len(target.shape) > 2:
            a, b = target.at[lead], other.at[lead]

        @pl.loop(0, count)
        def _(step):
            here = part(step)
            a[here] = (a[here].astype(jnp.float32) + b[here].astype(jnp.float32)).astype(a.dtype)


def octet_reduce_steps(board, terms_ref, sum_ref, mine, from_core, from_link, begin=0.0):
    h = sum_ref.shape[0] // 2
    unit = octet_unit(sum_ref.shape)
    core, along_x, along_y = ("plane", 1), ("plane", 2), "y"
    order = (
        (1, 1, 0),
        (1, 1, 1),
        (0, 1, 0),
        (1, 0, 1),
        (1, 0, 0),
        (0, 1, 1),
        (0, 0, 0),
        (0, 0, 1),
    )
    over_core = {}
    loads = {}
    for x, y, half in order:
        place = octet_place(0, x, y, half)
        loads[place] = board.move(
            terms_ref.at[pl.ds(place * h, h)], mine.at[place], close=False
        )
        over_core[place] = board.send(
            terms_ref.at[pl.ds((8 + place) * h, h)], from_core.at[place], core
        )

    def add_core(x, y, half):
        place = octet_place(0, x, y, half)
        loads[place].wait()
        over_core[place].wait_recv()
        add_rows(mine.at[place], from_core.at[place])
        return place

    second = {}
    for n, (x, y, half) in enumerate(order[:4]):
        yield begin + 0.1 * unit * (n + 1)
        place = add_core(x, y, half)
        second[(x, y, half)] = board.send(
            mine.at[place], from_link.at[n], along_y if half == 0 else along_x
        )
    third = {}
    for n, (x, y, half) in enumerate(order[4:6]):
        yield begin + unit * 1.2
        place = add_core(x, y, half)
        second[(1, 1, half)].wait_recv()
        add_rows(mine.at[place], from_link.at[half])
        third[half] = board.send(
            mine.at[place], from_link.at[4 + n], along_x if half == 0 else along_y
        )
    for half, sent in ((0, (0, 1, 0)), (1, (1, 0, 1))):
        yield begin + unit * 3.1
        place = add_core(0, 0, half)
        second[sent].wait_recv()
        third[half].wait_recv()

        @pl.loop(0, h // 16)
        def _(step):
            rows = pl.ds(pl.multiple_of(step * 16, 16), 16)
            out_rows = pl.ds(pl.multiple_of(half * h + step * 16, 16), 16)
            sum_ref[out_rows, :] = (
                mine[place, rows, :].astype(jnp.float32)
                + from_link[2 + half, rows, :].astype(jnp.float32)
                + from_link[4 + half, rows, :].astype(jnp.float32)
            )


def line_gather_steps(board, shard_ref, whole_ref, begin=0.0):
    unit = 4.0 * math.prod(shard_ref.shape) / LINK
    z = board.z
    far, near = board.line_xor(2), ("line", 1)
    two = board.send(shard_ref, whole_ref.at[z], ("line", 2))
    one = board.send(shard_ref, whole_ref.at[z], near)
    three_slot, on_slot = board.slot(), board.slot()
    three = board.make(three_slot, shard_ref, whole_ref.at[z], ("line", 3))
    onward = pltpu.make_async_remote_copy(
        src_ref=whole_ref.at[far],
        dst_ref=whole_ref.at[far],
        send_sem=board.sems[0].at[on_slot],
        recv_sem=board.sems[1].at[three_slot],
        device_id=board.device(near),
        device_id_type=MESH,
    )

    keep = board.move(shard_ref, whole_ref.at[z], close=False)
    yield begin + 1.9 * unit
    two.wait_recv()

    @pl.when(board.middle)
    def _():
        onward.start()
        three.start()

    yield begin + 3.1 * unit
    keep.wait()
    one.wait_recv()
    three.wait_recv()

    @pl.when(board.middle)
    def _():
        three.wait_send()
        onward.wait_send()


def line_reduce_steps(board, terms_ref, got_ref, held, carried, begin=0.0):
    unit = 4.0 * math.prod(got_ref.shape[1:]) / LINK
    near, two_off, three_off = ("line", 1), ("line", 2), ("line", 3)
    z_near, z_two, z_three = (board.line_xor(k) for k in (1, 2, 3))
    carry = board.make(board.slot(), terms_ref.at[z_three], carried, near)
    direct = board.make(board.slot(), terms_ref.at[z_three], got_ref.at[2], three_off)
    two_slot = board.slot()
    two_end = board.make(two_slot, terms_ref.at[z_two], got_ref.at[1], two_off)
    two_mid = board.make(two_slot, held, got_ref.at[1], two_off)

    one = board.make(board.slot(), terms_ref.at[z_near], got_ref.at[0], near)

    @pl.when(jnp.logical_not(board.middle))
    def _():
        carry.start()

    @pl.when(board.middle)
    def _():
        one.start()
        direct.start()

    load = board.move(terms_ref.at[z_two], held, close=False)
    yield begin + 1.05 * unit
    load.wait()

    @pl.when(jnp.logical_not(board.middle))
    def _():
        carry.wait_send()
        two_end.start()
        one.start()

    @pl.when(board.middle)
    def _():
        carry.wait_recv()
        add_rows(held, carried)
        two_mid.start()

    yield begin + 3.1 * unit
    one.wait_recv()
    one.wait_send()
    two_end.wait_recv()
    two_end.wait_send()

    @pl.when(board.middle)
    def _():
        direct.wait_recv()
        direct.wait_send()


def plane_exchange_steps(board, blocks_ref, given_ref, begin=0.0):
    copies = [
        board.send(
            blocks_ref.at[board.place_xor(k)], given_ref.at[board.i], ("plane", k)
        )
        for k in (3, 2, 1)
    ]
    keep = board.move(blocks_ref.at[board.i], given_ref.at[board.i], close=False)
    yield begin + 9.0 * math.prod(blocks_ref.shape[1:]) / LINK
    for copy in copies:
        copy.wait_recv()
    keep.wait()


def transpose_steps(board, shard_ref, given_ref, begin=0.0):
    slot, spot = board.slot(), board.locals
    board.locals += 1
    other = (board.i * PLANE + board.z, board.t)
    copy = pltpu.make_async_remote_copy(
        src_ref=shard_ref,
        dst_ref=given_ref,
        send_sem=board.sems[0].at[slot],
        recv_sem=board.sems[1].at[slot],
        device_id=other,
        device_id_type=MESH,
    )
    keep = pltpu.make_async_copy(shard_ref, given_ref, board.sems[2].at[spot])

    @pl.when(board.i != board.z)
    def _():
        copy.start()

    @pl.when(board.i == board.z)
    def _():
        keep.start()

    yield begin + 9.0 * math.prod(shard_ref.shape) / LINK

    @pl.when(board.i != board.z)
    def _():
        copy.wait()

    @pl.when(board.i == board.z)
    def _():
        keep.wait()


NEAR_OCTET = (("plane", 1), ("plane", 2), "y")
NEAR_PLANE = (("plane", 1), ("plane", 2), ("plane", 3))
NEAR_LINE = (("line", 1), ("line", 2), ("line", 3))


def hbm(shape):
    return (jax.ShapeDtypeStruct(shape, jnp.bfloat16), HBM_SPEC)


class OctetGather:
    near, remotes, moves = NEAR_OCTET, 13, 1

    def __init__(self, own):
        self.given = own
        self.outs = [hbm((8 * own.shape[0],) + own.shape[1:])]
        self.scratch = []

    def steps(self, board, own, outs, scratch):
        return octet_gather_steps(board, own, outs[0])

    def read(self, outs):
        return outs[0]


class OctetReduce:
    near, remotes, moves = NEAR_OCTET, 14, 8

    def __init__(self, terms):
        self.given = terms
        m, n = terms.shape[0] // 8, terms.shape[1]
        self.outs = [(jax.ShapeDtypeStruct((m, n), jnp.float32), VMEM_SPEC)]
        self.scratch = [pltpu.VMEM((k, m // 2, n), terms.dtype) for k in (8, 8, 6)]

    def steps(self, board, terms, outs, scratch):
        return octet_reduce_steps(board, terms, outs[0], *scratch)

    def read(self, outs):
        return outs[0]


class LineGather:
    near, remotes, moves = NEAR_LINE, 4, 1

    def __init__(self, shard):
        self.given = shard
        self.outs = [hbm((LINE,) + shard.shape)]
        self.scratch = []

    def steps(self, board, shard, outs, scratch):
        return line_gather_steps(board, shard, outs[0])

    def read(self, outs):
        return outs[0]

    def plain(self):
        return lax.all_gather(self.given, "dp", axis_index_groups=line_groups(), axis=0)


class LineReduce:
    near, remotes, moves = NEAR_LINE, 4, 1

    def __init__(self, terms):
        self.given = terms
        shape = terms.shape[1:]
        self.outs = [hbm((3,) + shape)]
        self.scratch = [pltpu.VMEM(shape, terms.dtype)] * 2

    def steps(self, board, terms, outs, scratch):
        return line_reduce_steps(board, terms, outs[0], *scratch)

    def read(self, outs):
        z = line_index()
        got = outs[0].astype(jnp.float32)
        middle = (z == 1) | (z == 2)
        own = take(self.given, z).astype(jnp.float32)
        return own + got[0] + got[1] + jnp.where(middle, got[2], 0.0)

    def plain(self):
        return lax.psum_scatter(
            self.given, "dp", axis_index_groups=line_groups(), scatter_dimension=0
        ).astype(jnp.float32)


class PlaneExchange:
    near, remotes, moves = NEAR_PLANE, 3, 1

    def __init__(self, blocks):
        self.given = blocks
        self.outs = [hbm(blocks.shape)]
        self.scratch = []

    def steps(self, board, blocks, outs, scratch):
        return plane_exchange_steps(board, blocks, outs[0])

    def read(self, outs):
        return outs[0]

    def plain(self):
        i = plane_index()
        whole = jnp.zeros_like(self.given)
        for k in range(PLANE):
            piece = take(self.given, i ^ k)
            if k:
                piece = swap(piece, k)
            whole = lax.dynamic_update_index_in_dim(whole, piece, i ^ k, 0)
        return whole


class GatherColumns:
    near, remotes, moves = NEAR_PLANE + NEAR_LINE, 7, 2

    def __init__(self, blocks):
        self.given = blocks
        self.outs = [hbm(blocks.shape), hbm((LINE,) + blocks.shape)]
        self.scratch = []

    def steps(self, board, blocks, outs, scratch):
        begin = 9.0 * math.prod(blocks.shape[1:]) / LINK
        yield from plane_exchange_steps(board, blocks, outs[0])
        yield from line_gather_steps(board, outs[0], outs[1], begin)

    def read(self, outs):
        return outs[1]

    def plain(self):
        return LineGather(PlaneExchange(self.given).plain()).plain()


class GatherPack:
    near, remotes, moves = NEAR_LINE + NEAR_OCTET, 17, 2

    def __init__(self, shard):
        self.given = shard
        self.outs = [hbm((LINE,) + shard.shape), hbm((8 * LINE,) + shard.shape)]
        self.scratch = []

    def steps(self, board, shard, outs, scratch):
        begin = 13.2 * math.prod(shard.shape) / LINK
        yield from line_gather_steps(board, shard, outs[0])
        yield from octet_gather_steps(board, outs[0], outs[1], begin)

    def read(self, outs):
        return outs[1]


class Transpose:
    near, remotes, moves = ("transposed",), 1, 1

    def __init__(self, shard, back=False):
        self.given = shard
        self.back = back
        self.outs = [hbm(shard.shape)]
        self.scratch = []

    def steps(self, board, shard, outs, scratch):
        return transpose_steps(board, shard, outs[0])

    def read(self, outs):
        return outs[0]

    def plain(self):
        line = lax.axis_size("dp") // PLANE
        pairs = [(i * line + z, z * PLANE + i) for i in range(PLANE) for z in range(line)]
        if self.back:
            pairs = [(b, a) for a, b in pairs]
        return lax.ppermute(self.given, "dp", pairs)


class GatherMoved(Transpose):
    near, remotes, moves = ("transposed",) + NEAR_LINE, 5, 2

    def __init__(self, shard):
        super().__init__(shard)
        self.outs = [hbm(shard.shape), hbm((LINE,) + shard.shape)]

    def steps(self, board, shard, outs, scratch):
        begin = 9.0 * math.prod(shard.shape) / LINK
        yield from transpose_steps(board, shard, outs[0])
        yield from line_gather_steps(board, outs[0], outs[1], begin)

    def read(self, outs):
        return outs[1]

    def plain(self):
        return LineGather(super().plain()).plain()


def communicate(collective_id, *tasks, compute=None):
    if lax.axis_size("dp") != PLANE * LINE:
        results = []
        for n, task in enumerate(tasks):
            alone = 4 * collective_id + n
            if isinstance(task, (OctetGather, OctetReduce)):
                results += run_kernel(alone, [task])
            elif isinstance(task, GatherPack):
                results += run_kernel(alone, [OctetGather(LineGather(task.given).plain())])
            else:
                results.append(task.plain())
        return results + (run_kernel(None, [], compute) if compute else [])
    return run_kernel(collective_id, tasks, compute)


def run_kernel(collective_id, tasks, compute=None):
    near = []
    for task in tasks:
        near += [name for name in task.near if name not in near]
    n_outs = [len(task.outs) for task in tasks]
    n_scratch = [len(task.scratch) for task in tasks]
    more_givens = compute.givens if compute else []
    more_outs = compute.outs if compute else []
    more_scratch = compute.scratch if compute else []
    more_given_specs = compute.given_specs if compute else []
    more_out_specs = compute.out_specs if compute else []

    def kernel(*refs):
        refs = list(refs)

        def first(count):
            part = refs[:count]
            del refs[:count]
            return part

        givens, compute_givens = first(len(tasks)), first(len(more_givens))
        outs, compute_outs = first(sum(n_outs)), first(len(more_outs))
        scratch, compute_scratch = first(sum(n_scratch)), first(len(more_scratch))
        running, closing = [], []
        if tasks:
            board = Board(*refs)
            closing = board.closing
            board.greet(near)
        for n, task in enumerate(tasks):
            steps = task.steps(
                board,
                givens[n],
                outs[sum(n_outs[:n]) : sum(n_outs[: n + 1])],
                scratch[sum(n_scratch[:n]) : sum(n_scratch[: n + 1])],
            )
            running.append((next(steps), n, steps))
        phases = []
        if compute:
            phases = compute.phases(
                compute_givens,
                compute_outs,
                compute_scratch,
                board if tasks else None,
                givens,
                outs,
            )
        while running or phases:
            running.sort(key=lambda item: item[:2])
            if phases and not (running and running[0][0] <= phases[0][0]):
                phases.pop(0)[1]()
                continue
            when, n, steps = running.pop(0)
            when = next(steps, None)
            if when is not None:
                running.append((when, n, steps))
        for close in closing:
            close()

    sems = []
    if tasks:
        sems = [
            pltpu.SemaphoreType.DMA((sum(task.remotes for task in tasks),)),
            pltpu.SemaphoreType.DMA((sum(task.remotes for task in tasks),)),
            pltpu.SemaphoreType.DMA((sum(task.moves for task in tasks),)),
        ]
    outs = pl.pallas_call(
        kernel,
        out_shape=[shape for task in tasks for shape, _ in task.outs] + more_outs,
        in_specs=[HBM_SPEC] * len(tasks) + more_given_specs,
        out_specs=[spec for task in tasks for _, spec in task.outs]
        + more_out_specs,
        scratch_shapes=[shape for task in tasks for shape in task.scratch]
        + more_scratch
        + sems,
        compiler_params=pltpu.CompilerParams(
            collective_id=collective_id,
            has_side_effects=bool(tasks),
            vmem_limit_bytes=VMEM_LIMIT,
        ),
        cost_estimate=pl.CostEstimate(flops=0, bytes_accessed=2**28, transcendentals=0),
    )(*[task.given for task in tasks], *more_givens)
    results = [
        task.read(outs[sum(n_outs[:n]) : sum(n_outs[: n + 1])]) for n, task in enumerate(tasks)
    ]
    return results + ([outs[sum(n_outs) :]] if compute else [])


def take(array, position):
    return lax.dynamic_index_in_dim(array, position, 0, keepdims=False)


def line_index():
    return lax.axis_index("dp") // PLANE


def plane_index():
    return lax.axis_index("dp") % PLANE


def line_groups():
    size = lax.axis_size("dp")
    return [[i + PLANE * z for z in range(size // PLANE)] for i in range(PLANE)]


def swap(array, bits):
    size = lax.axis_size("dp")
    return lax.ppermute(array, "dp", [(d, d ^ bits) for d in range(size)])


HEAD = 128
ROW_BLOCK = 64


def column_dot(left_side, right_side):
    return jnp.dot(left_side, right_side, preferred_element_type=jnp.float32)


def lane_index(shape):
    return lax.broadcasted_iota(jnp.int32, shape, len(shape) - 1)


def turn(values, wave, low_wave, high_wave):
    half = DR // 2
    return (
        values * wave
        + pltpu.roll(values, HEAD - half, 1) * low_wave
        + pltpu.roll(values, half, 1) * high_wave
    )


def score_bias(keys_ref, bounds_ref, bias, pack, pack_rows):
    @pl.loop(0, pack_rows // ROW_BLOCK)
    def _(block):
        rows = pl.ds(pl.multiple_of(block * ROW_BLOCK, ROW_BLOCK), ROW_BLOCK)
        here = bounds_ref[pl.ds(pack * pack_rows + block * ROW_BLOCK, ROW_BLOCK), :]
        key = keys_ref[pack, 0:1, :]
        allowed = (key >= here[:, 0:1]) & (key <= here[:, 1:2])
        bias[rows, :] = jnp.where(allowed, 0.0, MASKED)


class AttentionForward:
    def __init__(self, tokens, keys, bounds, waves, query_up, latent_up, packs, heads):
        rows = tokens.shape[0]
        self.packs, self.heads, self.pack_rows = packs, heads, rows // packs
        self.givens = [tokens, keys, bounds, *waves, query_up, latent_up]
        low = jnp.bfloat16
        self.pairs = -(-heads // 2)
        self.outs = [
            jax.ShapeDtypeStruct((rows, heads * HEAD), low),
            jax.ShapeDtypeStruct((rows, heads * HEAD), low),
            jax.ShapeDtypeStruct((rows, self.pairs * HEAD), low),
            jax.ShapeDtypeStruct((rows, HEAD), jnp.float32),
        ]
        self.scratch = [
            pltpu.VMEM((self.pack_rows, self.pack_rows), jnp.float32),
            pltpu.VMEM((self.pack_rows, heads * HEAD), jnp.float32),
            pltpu.VMEM((self.pack_rows, self.pack_rows), jnp.float32),
            pltpu.VMEM((self.pack_rows, self.pack_rows), low),
        ]
        self.phase_time = 12.0
        self.given_specs = [VMEM_SPEC] * len(self.givens)
        self.out_specs = [VMEM_SPEC] * len(self.outs)

    def phases(self, givens, outs, scratch, board, task_givens, task_outs):
        tokens, keys, bounds, wave, low_wave, high_wave, query_up, latent_up = givens
        queries, heads_out, mixed, totals = outs
        bias, raw, held, prob_low = scratch
        scale = QH ** (-0.5)
        size = self.pack_rows

        def run(pack):
            score_bias(keys, bounds, bias, pack, size)
            start = pack * size
            whole = slice(start, start + size)
            rope_key = pltpu.roll(
                tokens[whole, QR + KVR : QR + KVR + HEAD].astype(jnp.float32), DN, 1
            )
            for n in range(self.pairs):
                mixed[whole, n * HEAD : (n + 1) * HEAD] = jnp.zeros((size, HEAD), mixed.dtype)
            totals[whole, :] = jnp.zeros((size, HEAD), jnp.float32)
            heads_out[whole, :] = column_dot(
                tokens[whole, QR : QR + KVR], latent_up[...]
            ).astype(jnp.bfloat16)
            raw[...] = column_dot(tokens[whole, 0:QR], query_up[...])

            @pl.loop(0, self.heads)
            def _(head):
                lanes = pl.ds(pl.multiple_of(head * HEAD, HEAD), HEAD)
                pair = pl.ds(pl.multiple_of((head // 2) * HEAD, HEAD), HEAD)
                even = head % 2 == 0
                tile = heads_out[whole, lanes]
                key_all = jnp.where(
                    lane_index((size, HEAD)) < DN, tile.astype(jnp.float32), rope_key
                ).astype(jnp.bfloat16)
                query_all = turn(
                    raw[:, lanes], wave[whole, :], low_wave[whole, :], high_wave[whole, :]
                ).astype(jnp.bfloat16)
                queries[whole, lanes] = query_all
                held[...] = right_transposed(query_all, key_all)
                for block in range(size // ROW_BLOCK):
                    part = slice(block * ROW_BLOCK, (block + 1) * ROW_BLOCK)
                    rows = slice(start + block * ROW_BLOCK, start + (block + 1) * ROW_BLOCK)
                    scores = held[part, :] * scale + bias[part, :]
                    top = jnp.max(scores, axis=1, keepdims=True)
                    exponent = jnp.exp(scores - top)
                    total = jnp.sum(exponent, axis=1, keepdims=True)
                    prob_low[part, :] = (exponent * (1.0 / total)).astype(jnp.bfloat16)
                    totals[rows, :] = jnp.where(
                        lane_index((ROW_BLOCK, HEAD)) == head,
                        top + jnp.log(total),
                        totals[rows, :],
                    )
                out = column_dot(prob_low[...], tile)
                lane = lane_index((size, HEAD))
                placed = jnp.where(even, pltpu.roll(out, DN, 1), out)
                before = mixed[whole, pair].astype(jnp.float32)
                mixed[whole, pair] = jnp.where((lane < DN) == even, placed, before).astype(
                    mixed.dtype
                )

        return [(self.phase_time * n, functools.partial(run, n)) for n in range(self.packs)]


class AttentionBackward:
    def __init__(
        self,
        queries,
        latent_heads,
        totals,
        grad_mixed,
        tokens,
        keys,
        bounds,
        waves,
        query_up,
        latent_up,
        packs,
        heads,
    ):
        rows = tokens.shape[0]
        self.packs, self.heads, self.pack_rows = packs, heads, rows // packs
        self.givens = [
            queries,
            latent_heads,
            totals,
            grad_mixed,
            tokens,
            keys,
            bounds,
            *waves,
            query_up,
            latent_up,
        ]
        low = jnp.bfloat16
        self.outs = [
            jax.ShapeDtypeStruct((rows, heads * HEAD), low),
            jax.ShapeDtypeStruct((rows, heads * HEAD), low),
            jax.ShapeDtypeStruct((rows, QR + KVR + HEAD), low),
        ]
        size = self.pack_rows
        self.scratch = [
            pltpu.VMEM((size, size), jnp.float32),
            pltpu.VMEM((size, size), jnp.float32),
            pltpu.VMEM((size, size), jnp.float32),
            pltpu.VMEM((size, size), low),
            pltpu.VMEM((size, size), low),
            pltpu.VMEM((size, HEAD), jnp.float32),
        ]
        self.phase_time = 16.0
        self.given_specs = [VMEM_SPEC] * len(self.givens)
        self.out_specs = [VMEM_SPEC] * len(self.outs)

    def phases(self, givens, outs, scratch, board, task_givens, task_outs):
        (
            queries,
            heads_in,
            totals,
            grad_mixed,
            tokens,
            keys,
            bounds,
            wave,
            low_wave,
            high_wave,
            query_up,
            latent_up,
        ) = givens
        grad_queries, grad_heads, terms = outs
        bias, held, grad_held, prob_low, score_low, grad_rope = scratch
        scale = QH ** (-0.5)
        size = self.pack_rows

        def run(pack):
            score_bias(keys, bounds, bias, pack, size)
            start = pack * size
            whole = slice(start, start + size)
            rope_key = pltpu.roll(
                tokens[whole, QR + KVR : QR + KVR + HEAD].astype(jnp.float32), DN, 1
            )
            grad_rope[...] = jnp.zeros_like(grad_rope)

            @pl.loop(0, self.heads)
            def _(head):
                lanes = pl.ds(pl.multiple_of(head * HEAD, HEAD), HEAD)
                pair = pl.ds(pl.multiple_of((head // 2) * HEAD, HEAD), HEAD)
                even = head % 2 == 0
                lane = lane_index((size, HEAD))
                tile = heads_in[whole, lanes]
                query_all = queries[whole, lanes]
                key_all = jnp.where(lane < DN, tile.astype(jnp.float32), rope_key).astype(
                    jnp.bfloat16
                )
                grad_pair = grad_mixed[whole, pair].astype(jnp.float32)
                grad_out = jnp.where(
                    lane < DN, 0.0, jnp.where(even, pltpu.roll(grad_pair, DN, 1), grad_pair)
                ).astype(jnp.bfloat16)
                total_all = jnp.sum(
                    jnp.where(lane == head, totals[whole, :], 0.0), axis=1, keepdims=True
                )
                held[...] = right_transposed(query_all, key_all)
                grad_held[...] = right_transposed(grad_out, tile)
                for block in range(size // ROW_BLOCK):
                    part = slice(block * ROW_BLOCK, (block + 1) * ROW_BLOCK)
                    prob = jnp.exp(held[part, :] * scale + bias[part, :] - total_all[part])
                    grad_prob = grad_held[part, :]
                    inner = jnp.sum(prob * grad_prob, axis=1, keepdims=True)
                    prob_low[part, :] = prob.astype(jnp.bfloat16)
                    score_low[part, :] = (prob * (grad_prob - inner)).astype(jnp.bfloat16)
                grad_query = column_dot(score_low[...], key_all) * scale
                grad_queries[whole, lanes] = turn(
                    grad_query, wave[whole, :], -low_wave[whole, :], -high_wave[whole, :]
                ).astype(grad_queries.dtype)
                grad_value = left_transposed(prob_low[...], grad_out)
                grad_key = left_transposed(score_low[...], query_all) * scale
                grad_rope[...] += grad_key
                grad_heads[whole, lanes] = jnp.where(lane < DN, grad_key, grad_value).astype(
                    grad_heads.dtype
                )

            terms[whole, 0:QR] = right_transposed(grad_queries[whole, :], query_up[...]).astype(
                terms.dtype
            )
            terms[whole, QR : QR + KVR] = right_transposed(
                grad_heads[whole, :], latent_up[...]
            ).astype(terms.dtype)
            terms[whole, QR + KVR :] = pltpu.roll(grad_rope[...], HEAD - DN, 1).astype(terms.dtype)

        return [(self.phase_time * n, functools.partial(run, n)) for n in range(self.packs)]


class FfnForward:
    order = (
        ((0, 0, 0), 0.0),
        ((1, 0, 0), 0.26),
        ((0, 0, 1), 2.01),
        ((0, 1, 0), 2.02),
        ((1, 0, 1), 2.31),
        ((1, 1, 0), 2.32),
        ((0, 1, 1), 3.01),
        ((1, 1, 1), 3.31),
    )

    def __init__(self, gate, up, rows, unit):
        self.givens = [gate, up]
        self.given_specs = self.out_specs = [HBM_SPEC] * 2
        depth, units = gate.shape
        self.rows, self.unit = rows, unit
        self.outs = [jax.ShapeDtypeStruct((8 * rows, units), jnp.float32)] * 2
        self.scratch = [
            pltpu.VMEM((2, depth, units), gate.dtype),
            pltpu.VMEM((2, rows, depth), gate.dtype),
            pltpu.VMEM((2, 2, rows, units), jnp.float32),
            pltpu.SemaphoreType.DMA((2,)),
            pltpu.SemaphoreType.DMA((2,)),
            pltpu.SemaphoreType.DMA((2, 2)),
        ]

    def phases(self, givens, outs, scratch, board, task_givens, task_outs):
        weights, tokens, staged, weight_sems, token_sems, out_sems = scratch
        own, gathered = task_givens[0], task_outs[0]
        loads = [
            pltpu.make_async_copy(givens[n], weights.at[n], weight_sems.at[n]) for n in range(2)
        ]
        for load in loads:
            load.start()
        leaving = {}

        def run(step, place):
            spot = (place[0] * 2 + place[1]) * 2 + place[2]
            rows = pl.ds(spot * self.rows, self.rows)
            if spot:
                assert place in board.here
            slot = step % 2
            fetch = pltpu.make_async_copy(
                gathered.at[rows] if spot else own, tokens.at[slot], token_sems.at[slot]
            )
            fetch.start()
            fetch.wait()
            for n in range(2):
                if step == 0:
                    loads[n].wait()
                if step >= 2:
                    leaving.pop((slot, n)).wait()
                staged[slot, n] = column_dot(tokens[slot], weights[n])
                copy = pltpu.make_async_copy(
                    staged.at[slot, n], outs[n].at[rows], out_sems.at[slot, n]
                )
                copy.start()
                leaving[(slot, n)] = copy

        def finish():
            for copy in leaving.values():
                copy.wait()

        plan = [
            (when * self.unit, functools.partial(run, step, place))
            for step, (place, when) in enumerate(self.order)
        ]
        return plan + [(1e9, finish)]


class FfnBackward:
    CHUNK = 256

    def __init__(self, normed, grad_gate, grad_up, hidden, down):
        self.givens = [normed, grad_gate, grad_up, hidden, down]
        self.given_specs = [HBM_SPEC] * 5
        self.out_specs = [HBM_SPEC] * 3
        rows, depth = normed.shape
        units = hidden.shape[1]
        low = normed.dtype
        self.rows, self.depth, self.units = rows, depth, units
        self.outs = [jax.ShapeDtypeStruct((depth, units), low)] * 2 + [
            jax.ShapeDtypeStruct((rows, depth), low)
        ]
        self.scratch = [
            pltpu.VMEM((rows, units), low),
            pltpu.VMEM((rows, units), low),
            pltpu.VMEM((units, depth), low),
            pltpu.SemaphoreType.DMA((3,)),
        ]

    def phases(self, givens, outs, scratch, board, task_givens, task_outs):
        normed, grad_gate, grad_up, hidden, down = givens
        gate_held, up_held, down_held, sems = scratch
        chunk, rows, units, depth = self.CHUNK, self.rows, self.units, self.depth
        loads = [
            pltpu.make_async_copy(source, target, sems.at[n])
            for n, (source, target) in enumerate(
                ((grad_gate, gate_held), (grad_up, up_held), (down, down_held))
            )
        ]
        for load in loads:
            load.start()

        def gradients(first, count):
            if first == 0:
                loads[0].wait()
                loads[1].wait()

            def body(normed_part, gate_part, up_part):
                left = normed_part[...]
                gate_part[...] = left_transposed(left, gate_held[...]).astype(gate_part.dtype)
                up_part[...] = left_transposed(left, up_held[...]).astype(up_part.dtype)

            pltpu.emit_pipeline(
                body,
                grid=(count,),
                in_specs=[pl.BlockSpec((rows, chunk), lambda n: (0, n + first))],
                out_specs=[pl.BlockSpec((chunk, units), lambda n: (n + first, 0))] * 2,
            )(normed, outs[0], outs[1])

        def products(first, count):
            if first == 0:
                loads[2].wait()

            def body(hidden_part, out_part):
                out_part[...] = column_dot(hidden_part[...], down_held[...]).astype(out_part.dtype)

            pltpu.emit_pipeline(
                body,
                grid=(count,),
                in_specs=[pl.BlockSpec((chunk, units), lambda n: (n + first, 0))],
                out_specs=[pl.BlockSpec((chunk, depth), lambda n: (n + first, 0))],
            )(hidden, outs[2])

        plan = []
        when = 8.0
        for first in range(0, depth // chunk, 2):
            plan.append((when, functools.partial(gradients, first, 2)))
            when += 6.0
        for first in range(0, rows // chunk, 2):
            plan.append((when, functools.partial(products, first, 2)))
            when += 4.0
        return plan


class UnitUpdate:
    def __init__(self, parts, weight, first_moment, second_moment, line):
        self.givens = [parts, weight, first_moment, second_moment]
        self.given_specs, self.out_specs = [VMEM_SPEC] * 4, [VMEM_SPEC] * 3
        self.outs = [jax.ShapeDtypeStruct(weight.shape, jnp.float32)] * 3
        self.scratch = []
        self.line = line

    def phases(self, givens, outs, scratch, board, task_givens, task_outs):
        parts, weight, first_moment, second_moment = givens
        rows, columns = weight.shape
        width = columns // (PLANE * self.line)
        step_rows = 16 if rows % 16 == 0 else rows

        def run(half):
            count = rows // step_rows
            split = (0, count // 2, count)

            @pl.loop(split[half], split[half + 1])
            def _(step):
                here = pl.ds(pl.multiple_of(step * step_rows, step_rows), step_rows)
                pieces = [parts[i, here, :].astype(jnp.float32) for i in range(PLANE)]
                gradient = jnp.concatenate(
                    [
                        pieces[i][:, z * width : (z + 1) * width]
                        for z in range(self.line)
                        for i in range(PLANE)
                    ],
                    axis=1,
                )
                results = adamw_update(
                    weight[here, :],
                    first_moment[here, :],
                    second_moment[here, :],
                    gradient,
                    matrix_rate(D),
                )
                for out, result in zip(outs, results):
                    out[here, :] = result

        return [(8.0, functools.partial(run, 0)), (14.0, functools.partial(run, 1))]


def positions(segment_ids):
    token_index = jnp.arange(segment_ids.shape[0], dtype=jnp.int32)
    doc_start = jnp.concatenate(
        [jnp.ones((1,), dtype=jnp.bool_), segment_ids[1:] != segment_ids[:-1]]
    )
    starts = lax.cummax(jnp.where(doc_start, token_index, 0), axis=0)
    return token_index - starts


def rope_tables(position):
    exponent = jnp.arange(DR // 2, dtype=jnp.float32) * (2.0 / DR)
    rope_angle = position[:, None] * (ROPE_BASE ** (-exponent))[None, :]
    return (jnp.cos(rope_angle), jnp.sin(rope_angle))


def local(
    inputs,
    cotangent,
    segment_ids,
    gains,
    gains_first,
    gains_second,
    query_down,
    query_down_first,
    query_down_second,
    latent_down,
    latent_down_first,
    latent_down_second,
    query_up,
    query_up_first,
    query_up_second,
    latent_up,
    latent_up_first,
    latent_up_second,
    output_proj,
    output_proj_first,
    output_proj_second,
    gate_proj,
    gate_proj_first,
    gate_proj_second,
    up_proj,
    up_proj_first,
    up_proj_second,
    down_proj,
    down_proj_first,
    down_proj_second,
):
    size = lax.axis_size("dp")
    tensor = lax.axis_size("tensor")
    line = size // PLANE
    z, i, t = line_index(), plane_index(), lax.axis_index("tensor")
    half_rows = inputs.shape[0]
    pack_rows = segment_ids.shape[0]
    packs = PLANE
    rows_all = packs * pack_rows
    low = jnp.bfloat16
    local_heads = H // (PLANE * tensor)
    units = FF // (PLANE * tensor)
    mixed_width = -(-local_heads // 2) * HEAD

    def column_blocks(weight, columns):
        return weight.astype(low).reshape(-1, PLANE, columns).transpose(1, 0, 2)

    def unit_blocks(weight):
        return (
            weight.astype(low)
            .reshape(weight.shape[0], line, PLANE, units // line)
            .transpose(2, 0, 1, 3)
            .reshape(PLANE, weight.shape[0], units)
        )

    down_rows = query_down.shape[0]
    pack_height = down_rows + 16
    gain_width = gains.shape[0]
    down_pack = jnp.concatenate(
        [
            jnp.concatenate([query_down, latent_down], axis=1).astype(low),
            jnp.pad(gains.astype(low)[None], ((0, 15), (0, QR + KVR + DR - gain_width))),
        ],
        axis=0,
    )
    def head_blocks(weight):
        blocks = weight.astype(low).reshape(-1, PLANE, local_heads, QH)
        blocks = jnp.pad(blocks, ((0, 0), (0, 0), (0, 0), (0, HEAD - QH)))
        return blocks.reshape(-1, PLANE, local_heads * HEAD).transpose(1, 0, 2)

    down_low = down_proj.astype(low)
    pack_all, query_up_all, latent_up_all, gate_plane, down_first = communicate(
        1,
        GatherPack(down_pack),
        GatherColumns(head_blocks(query_up)),
        GatherColumns(column_blocks(latent_up, local_heads * KH)),
        PlaneExchange(unit_blocks(gate_proj)),
        LineGather(down_low[:, : D // 2]),
    )
    query_up_all = query_up_all.reshape(QR, local_heads * HEAD)
    latent_up_all = latent_up_all.reshape(KVR, local_heads * KH)
    down_octet = pack_all.reshape(2, 2, tensor, line, pack_height, QR + KVR + DR)
    down_blocks = jnp.zeros((PLANE, tensor, line, pack_height, QR + KVR + DR), low)
    for k in range(PLANE):
        for y in range(tensor):
            down_blocks = lax.dynamic_update_slice(
                down_blocks,
                down_octet[k % 2, k // 2, y][None, None],
                (i ^ k, (t + y) % tensor, 0, 0, 0),
            )
    down_blocks = down_blocks.transpose(2, 0, 1, 3, 4)
    down_both = down_blocks[..., :down_rows, :].reshape(D, QR + KVR + DR)
    gain_values = down_blocks[..., down_rows, :gain_width].reshape(-1).astype(jnp.float32)
    gain_attention = gain_values[:D]
    gain_query = gain_values[D : D + QR]
    gain_latent = gain_values[D + QR : D + QR + KVR]
    gain_ffn = gain_values[D + QR + KVR :]

    incoming = inputs.astype(jnp.float32)
    attn_unit, inverse_attention = norm_forward(incoming, gain_attention)
    normed_attn = attn_unit.astype(low)
    both_latent = jnp.dot(normed_attn, down_both, preferred_element_type=jnp.float32)
    query_latent = both_latent[:, :QR]
    latent = both_latent[:, QR:]
    query_unit, inverse_query = norm_forward(query_latent, gain_query)
    latent_unit, inverse_latent = norm_forward(latent[:, :KVR], gain_latent)
    own_position = lax.dynamic_slice_in_dim(positions(segment_ids), t * half_rows, half_rows)
    own_segment = lax.dynamic_slice_in_dim(segment_ids, t * half_rows, half_rows)
    own_cosine, own_sine = rope_tables(own_position.astype(jnp.float32))
    own_rope_key = rotate(latent[:, KVR:], own_cosine, own_sine)
    marks = jnp.stack(
        [own_segment // 16, own_segment % 16, own_position // 16, own_position % 16], axis=1
    )
    tokens_own = jnp.concatenate(
        [
            query_unit.astype(low),
            latent_unit.astype(low),
            own_rope_key.astype(low),
            marks.astype(low),
            jnp.zeros((half_rows, 128 - DR - 4), low),
        ],
        axis=1,
    )
    tokens_all, output_all = communicate(
        3, OctetGather(tokens_own), GatherMoved(output_proj.astype(low))
    )
    output_all = jnp.pad(
        output_all.reshape(local_heads * DV, D), ((0, mixed_width - local_heads * DV), (0, 0))
    )
    marks_all = tokens_all[:, QR + KVR + DR : QR + KVR + DR + 4].astype(jnp.float32)
    key_base = (marks_all[:, 0] * 16.0 + marks_all[:, 1]) * pack_rows
    position = marks_all[:, 2] * 16.0 + marks_all[:, 3]
    key = key_base + position
    keys = jnp.broadcast_to(key.reshape(packs, 1, pack_rows), (packs, 8, pack_rows))
    bounds = jnp.pad(jnp.stack([key_base, key], axis=1), ((0, 0), (0, HEAD - 2)))
    rope_cosine, rope_sine = rope_tables(position)
    nothing = jnp.zeros((rows_all, DR), jnp.float32)
    still = jnp.zeros((rows_all, DN), jnp.float32)
    waves = (
        jnp.concatenate([still + 1.0, rope_cosine, rope_cosine, nothing], axis=1),
        jnp.concatenate([still, -rope_sine, nothing, nothing[:, : DR // 2]], axis=1),
        jnp.concatenate([still, nothing[:, : DR // 2], rope_sine, nothing], axis=1),
    )
    grad_ffn, up_plane, gate_all, (queries, latent_heads, mixed_heads, log_totals) = communicate(
        2,
        OctetGather((RESIDUAL * cotangent.astype(jnp.float32)).astype(low)),
        PlaneExchange(unit_blocks(up_proj)),
        LineGather(gate_plane),
        compute=AttentionForward(
            tokens_all, keys, bounds, waves, query_up_all, latent_up_all, packs, local_heads
        ),
    )
    gate_all = gate_all.reshape(D, units)
    attention_terms = jnp.dot(mixed_heads, output_all, preferred_element_type=jnp.float32)
    attention_sum, up_all = communicate(
        4, OctetReduce(attention_terms.astype(low)), LineGather(up_plane)
    )
    up_all = up_all.reshape(D, units)
    residual = incoming + RESIDUAL * attention_sum

    ffn_unit, inverse_ffn = norm_forward(residual, gain_ffn)
    normed_own = ffn_unit.astype(low)
    tasks = (OctetGather(normed_own), LineGather(down_low[:, D // 2 :]))
    if line == LINE:
        normed_ffn, down_second, (gate_value, up_value) = communicate(
            5,
            *tasks,
            compute=FfnForward(gate_all, up_all, half_rows, octet_unit((half_rows, D))),
        )
    else:
        normed_ffn, down_second = communicate(5, *tasks)
        gate_value = jnp.dot(normed_ffn, gate_all, preferred_element_type=jnp.float32)
        up_value = jnp.dot(normed_ffn, up_all, preferred_element_type=jnp.float32)
    down_all = jnp.concatenate([down_first, down_second], axis=2).reshape(units, D)
    gate_sigmoid = lax.logistic(gate_value)
    silu_gate = gate_value * gate_sigmoid
    hidden = (silu_gate * up_value).astype(low)
    grad_hidden = right_transposed(grad_ffn, down_all)
    grad_gate = (
        grad_hidden * up_value * gate_sigmoid * (1.0 + gate_value * (1.0 - gate_sigmoid))
    ).astype(low)
    grad_up = (grad_hidden * silu_gate).astype(low)
    ffn_back_terms = right_transposed(grad_gate, gate_all) + right_transposed(grad_up, up_all)
    down_grad = left_transposed(hidden, grad_ffn).astype(low).reshape(line, -1, D)
    grad_normed_ffn, down_shard, (gate_grad, up_grad, ffn_terms) = communicate(
        6,
        OctetReduce(ffn_back_terms.astype(low)),
        LineReduce(down_grad),
        compute=FfnBackward(normed_ffn, grad_gate, grad_up, hidden, down_all),
    )
    outer_grad = cotangent.astype(jnp.float32)
    grad_incoming_ffn, gain_ffn_grad = norm_backward(
        residual, inverse_ffn, gain_ffn, grad_normed_ffn
    )
    grad_residual = outer_grad + grad_incoming_ffn

    grad_branch, gate_sum = communicate(
        7,
        OctetGather((RESIDUAL * grad_residual).astype(low)),
        LineReduce(gate_grad.reshape(line, PLANE, -1, units)),
    )
    output_grad = (
        left_transposed(mixed_heads, grad_branch)
        .astype(low)[: local_heads * DV]
        .reshape(line, -1, D)
    )
    grad_mixed = right_transposed(grad_branch, output_all).astype(low)
    ffn_sum, up_sum, gate_parts, (grad_query_heads, grad_latent_heads, grad_unit_terms) = communicate(
        8,
        OctetReduce(ffn_terms),
        LineReduce(up_grad.reshape(line, PLANE, -1, units)),
        PlaneExchange(gate_sum.astype(low)),
        compute=AttentionBackward(
            queries,
            latent_heads,
            log_totals,
            grad_mixed,
            tokens_all,
            keys,
            bounds,
            waves,
            query_up_all,
            latent_up_all,
            packs,
            local_heads,
        ),
    )
    block_output = (residual + RESIDUAL * ffn_sum).astype(low)
    query_up_grad = left_transposed(tokens_all[:, :QR], grad_query_heads).astype(low)
    latent_up_grad = left_transposed(tokens_all[:, QR : QR + KVR], grad_latent_heads).astype(low)
    grad_units, output_sum, up_parts, gate_out = communicate(
        9,
        OctetReduce(grad_unit_terms),
        LineReduce(output_grad),
        PlaneExchange(up_sum.astype(low)),
        compute=UnitUpdate(gate_parts, gate_proj, gate_proj_first, gate_proj_second, line),
    )
    grad_query_wide, gain_query_grad = norm_backward(
        query_latent, inverse_query, gain_query, grad_units[:, :QR]
    )
    grad_latent_part, gain_latent_grad = norm_backward(
        latent[:, :KVR], inverse_latent, gain_latent, grad_units[:, QR : QR + KVR]
    )
    grad_rope = unrotate(grad_units[:, QR + KVR : QR + KVR + DR], own_cosine, own_sine)
    grad_both = jnp.concatenate([grad_query_wide, grad_latent_part, grad_rope], axis=1).astype(low)
    down_both_grad = left_transposed(normed_attn, grad_both).astype(low)
    grad_normed_attn = right_transposed(grad_both, down_both)
    grad_incoming_attn, gain_attention_grad = norm_backward(
        incoming, inverse_attention, gain_attention, grad_normed_attn
    )
    input_grad = (grad_residual + grad_incoming_attn).astype(low)
    gains_grad = jnp.concatenate(
        [gain_attention_grad, gain_query_grad, gain_latent_grad, gain_ffn_grad]
    ).astype(low)
    pack_grad = jnp.concatenate(
        [
            down_both_grad.reshape(line, PLANE, tensor, down_rows, QR + KVR + DR),
            jnp.pad(
                gains_grad.reshape(line, PLANE, tensor, 1, gain_width),
                ((0, 0), (0, 0), (0, 0), (0, 15), (0, QR + KVR + DR - gain_width)),
            ),
        ],
        axis=3,
    ).transpose(1, 2, 0, 3, 4)
    pack_terms = jnp.concatenate(
        [
            lax.dynamic_slice(
                pack_grad,
                (i ^ (core + 2 * x), (t + y) % tensor, 0, 0, 0),
                (1, 1) + pack_grad.shape[2:],
            ).reshape(line * pack_height, QR + KVR + DR)
            for core in range(2)
            for x in range(2)
            for y in range(tensor)
        ],
        axis=0,
    )
    pack_octet, query_up_sum, latent_up_sum, output_shard, up_out = communicate(
        10,
        OctetReduce(pack_terms),
        LineReduce(query_up_grad.reshape(line, PLANE, -1, local_heads * HEAD)),
        LineReduce(latent_up_grad.reshape(line, PLANE, -1, local_heads * KH)),
        Transpose(output_sum.astype(low), back=True),
        compute=UnitUpdate(up_parts, up_proj, up_proj_first, up_proj_second, line),
    )
    pack_sum, query_up_parts, latent_up_parts = communicate(
        11,
        LineReduce(pack_octet.astype(low).reshape(line, pack_height, QR + KVR + DR)),
        PlaneExchange(query_up_sum.astype(low)),
        PlaneExchange(latent_up_sum.astype(low)),
    )
    query_down_shard = pack_sum[:down_rows, :QR]
    latent_down_shard = pack_sum[:down_rows, QR:]
    gains_shard = pack_sum[down_rows, :gain_width]

    def head_columns(blocks):
        return blocks.astype(jnp.float32).transpose(1, 0, 2).reshape(blocks.shape[1], -1)

    query_up_parts = query_up_parts.reshape(PLANE, -1, local_heads, HEAD)[..., :QH]
    query_up_shard = head_columns(query_up_parts.reshape(PLANE, -1, local_heads * QH))
    latent_up_shard = head_columns(latent_up_parts)
    output_shard = output_shard.astype(jnp.float32)

    gains_out = adamw_update(gains, gains_first, gains_second, gains_shard, GAIN_RATE)
    query_down_out = adamw_update(
        query_down, query_down_first, query_down_second, query_down_shard, matrix_rate(D)
    )
    latent_down_out = adamw_update(
        latent_down, latent_down_first, latent_down_second, latent_down_shard, matrix_rate(D)
    )
    query_up_out = adamw_update(
        query_up, query_up_first, query_up_second, query_up_shard, matrix_rate(QR)
    )
    latent_up_out = adamw_update(
        latent_up, latent_up_first, latent_up_second, latent_up_shard, matrix_rate(KVR)
    )
    output_out = adamw_update(
        output_proj, output_proj_first, output_proj_second, output_shard, matrix_rate(H * DV // 64)
    )
    down_out = adamw_update(
        down_proj, down_proj_first, down_proj_second, down_shard, matrix_rate(FF // 8)
    )
    return (
        block_output,
        input_grad,
        gains_out[0],
        gains_out[1],
        gains_out[2],
        query_down_out[0],
        query_down_out[1],
        query_down_out[2],
        latent_down_out[0],
        latent_down_out[1],
        latent_down_out[2],
        query_up_out[0],
        query_up_out[1],
        query_up_out[2],
        latent_up_out[0],
        latent_up_out[1],
        latent_up_out[2],
        output_out[0],
        output_out[1],
        output_out[2],
        gate_out[0],
        gate_out[1],
        gate_out[2],
        up_out[0],
        up_out[1],
        up_out[2],
        down_out[0],
        down_out[1],
        down_out[2],
    )


def solution(mesh):
    in_specs = (
        P(("dp", "tensor"), None),
        P(("dp", "tensor"), None),
        P("dp"),
        P(("dp", "tensor")),
        P(("dp", "tensor")),
        P(("dp", "tensor")),
        P(("dp", "tensor"), None),
        P(("dp", "tensor"), None),
        P(("dp", "tensor"), None),
        P(("dp", "tensor"), None),
        P(("dp", "tensor"), None),
        P(("dp", "tensor"), None),
        P("dp", "tensor"),
        P("dp", "tensor"),
        P("dp", "tensor"),
        P("dp", "tensor"),
        P("dp", "tensor"),
        P("dp", "tensor"),
        P(("tensor", "dp"), None),
        P(("tensor", "dp"), None),
        P(("tensor", "dp"), None),
        P("dp", "tensor"),
        P("dp", "tensor"),
        P("dp", "tensor"),
        P("dp", "tensor"),
        P("dp", "tensor"),
        P("dp", "tensor"),
        P(("tensor", "dp"), None),
        P(("tensor", "dp"), None),
        P(("tensor", "dp"), None),
    )
    out_specs = (
        P(("dp", "tensor"), None),
        P(("dp", "tensor"), None),
        P(("dp", "tensor")),
        P(("dp", "tensor")),
        P(("dp", "tensor")),
        P(("dp", "tensor"), None),
        P(("dp", "tensor"), None),
        P(("dp", "tensor"), None),
        P(("dp", "tensor"), None),
        P(("dp", "tensor"), None),
        P(("dp", "tensor"), None),
        P("dp", "tensor"),
        P("dp", "tensor"),
        P("dp", "tensor"),
        P("dp", "tensor"),
        P("dp", "tensor"),
        P("dp", "tensor"),
        P(("tensor", "dp"), None),
        P(("tensor", "dp"), None),
        P(("tensor", "dp"), None),
        P("dp", "tensor"),
        P("dp", "tensor"),
        P("dp", "tensor"),
        P("dp", "tensor"),
        P("dp", "tensor"),
        P("dp", "tensor"),
        P(("tensor", "dp"), None),
        P(("tensor", "dp"), None),
        P(("tensor", "dp"), None),
    )
    return jax.shard_map(local, mesh=mesh, in_specs=in_specs, out_specs=out_specs, check_vma=False)
```

```python
import functools
import math

import jax
import jax.numpy as jnp
from jax import lax
from jax.experimental import pallas as pl
from jax.experimental.pallas import tpu as pltpu
from jax.sharding import PartitionSpec as P

D = 2560
H = 40
DN = 64
DR = 32
DV = 64
QR = 768
KVR = 256
FF = 6400
STEP = 10
QH = 96
KH = 128


RESIDUAL = 1.4 / math.sqrt(62.0)
NORM_EPSILON = 1e-05
MOMENT_DECAY = 0.9
SQUARE_DECAY = 0.95
ADAM_EPSILON = 1e-08
WEIGHT_DECAY = 0.1
GAIN_RATE = 0.3
ROPE_BASE = 10000.0
MASKED = -1e30


def right_transposed(left_side, right_side):
    return lax.dot_general(
        left_side, right_side, (((1,), (1,)), ((), ())), preferred_element_type=jnp.float32
    )


def left_transposed(left_side, right_side):
    return lax.dot_general(
        left_side, right_side, (((0,), (0,)), ((), ())), preferred_element_type=jnp.float32
    )


def norm_forward(values, gain_values):
    inverse = lax.rsqrt(jnp.mean(values * values, axis=-1, keepdims=True) + NORM_EPSILON)
    return (values * inverse * gain_values, inverse)


def norm_backward(values, inverse, gain_values, grad_out):
    unit_values = values * inverse
    weighted = grad_out * gain_values
    grad_values = inverse * (
        weighted - unit_values * jnp.mean(weighted * unit_values, axis=-1, keepdims=True)
    )
    return (grad_values, jnp.sum(grad_out * unit_values, axis=0))


def rotate(values, rope_cosine, rope_sine):
    half_width = values.shape[-1] // 2
    first_half = values[..., :half_width]
    second_half = values[..., half_width:]
    return jnp.concatenate(
        [
            first_half * rope_cosine - second_half * rope_sine,
            second_half * rope_cosine + first_half * rope_sine,
        ],
        axis=-1,
    )


def unrotate(grads_in, rope_cosine, rope_sine):
    half_width = grads_in.shape[-1] // 2
    first_half = grads_in[..., :half_width]
    second_half = grads_in[..., half_width:]
    return jnp.concatenate(
        [
            first_half * rope_cosine + second_half * rope_sine,
            second_half * rope_cosine - first_half * rope_sine,
        ],
        axis=-1,
    )


def adamw_update(weight, first_moment, second_moment, gradient, step_rate):
    new_first = MOMENT_DECAY * first_moment + (1.0 - MOMENT_DECAY) * gradient
    new_second = SQUARE_DECAY * second_moment + (1.0 - SQUARE_DECAY) * gradient * gradient
    first_hat = new_first / (1.0 - MOMENT_DECAY**STEP)
    second_hat = new_second / (1.0 - SQUARE_DECAY**STEP)
    new_weight = weight - step_rate * (
        first_hat / (jnp.sqrt(second_hat) + ADAM_EPSILON) + WEIGHT_DECAY * weight
    )
    return (new_weight, new_first, new_second)


def matrix_rate(fan_in):
    return 2.0 / math.sqrt(fan_in)


PLANE = 4
LINE = 4
LINK = 8.4e4
MESH = pl.DeviceIdType.MESH
VMEM_LIMIT = 56 * 1024 * 1024
HBM_SPEC = pl.BlockSpec(memory_space=pl.ANY)
VMEM_SPEC = pl.BlockSpec(memory_space=pltpu.VMEM)


class Board:
    def __init__(self, send_sems, recv_sems, local_sems):
        self.sems = (send_sems, recv_sems, local_sems)
        self.remotes = 0
        self.locals = 0
        self.closing = []
        self.here = set()
        self.d = lax.axis_index("dp")
        self.t = lax.axis_index("tensor")
        self.z = self.d // PLANE
        self.i = self.d % PLANE
        self.middle = (self.z == 1) | (self.z == 2)
        self.known = {
            name: self.work_out(name) for name in NEAR_OCTET + NEAR_PLANE + NEAR_LINE
        }

    def place_xor(self, k):
        i = self.i
        return (i, i + 1 - 2 * (i % 2), i + 2 - 4 * (i // 2), 3 - i)[k]

    def line_xor(self, k):
        z = self.z
        return (z, z + 1 - 2 * (z % 2), z + 2 - 4 * (z // 2), 3 - z)[k]

    def device(self, name):
        return self.known[name]

    def work_out(self, name):
        if name == "y":
            return (self.d, 1 - self.t)
        kind, k = name
        if kind == "plane":
            return (self.z * PLANE + self.place_xor(k), self.t)
        return (self.line_xor(k) * PLANE + self.i, self.t)

    def greet(self, names):
        barrier = pltpu.get_barrier_semaphore()
        known = [name for name in names if name != "transposed"]
        for name in known:
            pl.semaphore_signal(
                barrier, inc=1, device_id=self.device(name), device_id_type=MESH
            )
        if len(known) == len(names):
            pl.semaphore_wait(barrier, len(known))
            return

        @pl.when(self.i != self.z)
        def _():
            pl.semaphore_signal(
                barrier,
                inc=1,
                device_id=(self.i * PLANE + self.z, self.t),
                device_id_type=MESH,
            )
            pl.semaphore_wait(barrier, len(known) + 1)

        @pl.when(self.i == self.z)
        def _():
            pl.semaphore_wait(barrier, len(known))

    def slot(self):
        self.remotes += 1
        return self.remotes - 1

    def make(self, slot, source, target, name):
        return pltpu.make_async_remote_copy(
            src_ref=source,
            dst_ref=target,
            send_sem=self.sems[0].at[slot],
            recv_sem=self.sems[1].at[slot],
            device_id=self.device(name),
            device_id_type=MESH,
        )

    def send(self, source, target, name):
        copy = self.make(self.slot(), source, target, name)
        copy.start()
        self.closing.append(copy.wait_send)
        return copy

    def move(self, source, target, close=True):
        copy = pltpu.make_async_copy(source, target, self.sems[2].at[self.locals])
        self.locals += 1
        copy.start()
        if close:
            self.closing.append(copy.wait)
        return copy


def octet_place(core, x, y, half):
    return ((core * 2 + x) * 2 + y) * 2 + half


def octet_unit(shape):
    return 2.0 * math.prod(shape) / LINK


def octet_gather_steps(board, own_ref, all_ref, begin=0.0):
    h = own_ref.shape[0] // 2
    unit = octet_unit(own_ref.shape)

    def rows(place, count=1):
        return all_ref.at[pl.ds(place * h, count * h)]

    core, along_x, along_y = ("plane", 1), ("plane", 2), "y"
    first, second = own_ref.at[pl.ds(0, h)], own_ref.at[pl.ds(h, h)]
    first_x = board.send(first, rows(octet_place(0, 1, 0, 0)), along_x)
    second_y = board.send(second, rows(octet_place(0, 0, 1, 1)), along_y)
    first_y = board.send(first, rows(octet_place(0, 0, 1, 0)), along_y)
    second_x = board.send(second, rows(octet_place(0, 1, 0, 1)), along_x)
    whole_core = board.send(own_ref, rows(octet_place(1, 0, 0, 0), 2), core)
    board.move(own_ref, rows(0, 2))

    def onward(start, end, name):
        return board.send(rows(octet_place(*start)), rows(octet_place(*end)), name)

    def to_core(*place):
        return onward((0,) + place, (1,) + place, core)

    yield begin + 0.25 * unit
    whole_core.wait_recv()
    board.here.add((1, 0, 0))
    yield begin + unit
    first_x.wait_recv()
    first_xy = onward((0, 1, 0, 0), (0, 1, 1, 0), along_y)
    core_x = [to_core(1, 0, 0)]
    second_y.wait_recv()
    second_xy = onward((0, 0, 1, 1), (0, 1, 1, 1), along_x)
    core_y = [to_core(0, 1, 1)]
    yield begin + 2.0 * unit
    first_y.wait_recv()
    core_y.append(to_core(0, 1, 0))
    second_x.wait_recv()
    core_x.append(to_core(1, 0, 1))
    board.here.update(((0, 0, 1), (0, 1, 0)))
    yield begin + 2.3 * unit
    for copy in core_x + core_y:
        copy.wait_recv()
    board.here.update(((1, 0, 1), (1, 1, 0)))
    yield begin + 3.0 * unit
    first_xy.wait_recv()
    core_xy = [to_core(1, 1, 0)]
    second_xy.wait_recv()
    core_xy.append(to_core(1, 1, 1))
    board.here.add((0, 1, 1))
    yield begin + 3.3 * unit
    for copy in core_xy:
        copy.wait_recv()
    board.here.add((1, 1, 1))


def add_rows(target, other):
    if target.shape[-2] % 16 == 0:
        count = target.shape[-2] // 16

        def part(step):
            return (pl.ds(pl.multiple_of(step * 16, 16), 16), slice(None))

    else:
        assert target.shape[-1] % 128 == 0
        count = target.shape[-1] // 128

        def part(step):
            return (slice(None), pl.ds(pl.multiple_of(step * 128, 128), 128))

    for lead in range(math.prod(target.shape[:-2])):
        a, b = target, other
        if len(target.shape) > 2:
            a, b = target.at[lead], other.at[lead]

        @pl.loop(0, count)
        def _(step):
            here = part(step)
            a[here] = (a[here].astype(jnp.float32) + b[here].astype(jnp.float32)).astype(a.dtype)


def octet_reduce_steps(board, terms_ref, sum_ref, mine, from_core, from_link, begin=0.0):
    h = sum_ref.shape[0] // 2
    unit = octet_unit(sum_ref.shape)
    core, along_x, along_y = ("plane", 1), ("plane", 2), "y"
    order = (
        (1, 1, 0),
        (1, 1, 1),
        (0, 1, 0),
        (1, 0, 1),
        (1, 0, 0),
        (0, 1, 1),
        (0, 0, 0),
        (0, 0, 1),
    )
    over_core = {}
    loads = {}
    for x, y, half in order:
        place = octet_place(0, x, y, half)
        loads[place] = board.move(
            terms_ref.at[pl.ds(place * h, h)], mine.at[place], close=False
        )
        over_core[place] = board.send(
            terms_ref.at[pl.ds((8 + place) * h, h)], from_core.at[place], core
        )

    def add_core(x, y, half):
        place = octet_place(0, x, y, half)
        loads[place].wait()
        over_core[place].wait_recv()
        add_rows(mine.at[place], from_core.at[place])
        return place

    second = {}
    for n, (x, y, half) in enumerate(order[:4]):
        yield begin + 0.1 * unit * (n + 1)
        place = add_core(x, y, half)
        second[(x, y, half)] = board.send(
            mine.at[place], from_link.at[n], along_y if half == 0 else along_x
        )
    third = {}
    for n, (x, y, half) in enumerate(order[4:6]):
        yield begin + unit * 1.2
        place = add_core(x, y, half)
        second[(1, 1, half)].wait_recv()
        add_rows(mine.at[place], from_link.at[half])
        third[half] = board.send(
            mine.at[place], from_link.at[4 + n], along_x if half == 0 else along_y
        )
    for half, sent in ((0, (0, 1, 0)), (1, (1, 0, 1))):
        yield begin + unit * 3.1
        place = add_core(0, 0, half)
        second[sent].wait_recv()
        third[half].wait_recv()

        @pl.loop(0, h // 16)
        def _(step):
            rows = pl.ds(pl.multiple_of(step * 16, 16), 16)
            out_rows = pl.ds(pl.multiple_of(half * h + step * 16, 16), 16)
            sum_ref[out_rows, :] = (
                mine[place, rows, :].astype(jnp.float32)
                + from_link[2 + half, rows, :].astype(jnp.float32)
                + from_link[4 + half, rows, :].astype(jnp.float32)
            )


OCTET_ORDER = ((1, 1), (0, 1), (1, 0), (0, 0))


def octet_reduce_inside_steps(
    board, sum_ref, outgoing, mine, from_core, from_link, piece_time, begin=0.0
):
    h = sum_ref.shape[0] // 2
    unit = octet_unit(sum_ref.shape)
    core, along_x, along_y = ("plane", 1), ("plane", 2), "y"
    board.terms = (outgoing, mine)
    over_core, second, third = {}, {}, {}

    def add_core(x, y, half):
        place = octet_place(0, x, y, half)
        over_core[place].wait_recv()
        add_rows(mine.at[place], from_core.at[place])
        return place

    def pass_second(x, y, half, n):
        place = add_core(x, y, half)
        second[(x, y, half)] = board.send(
            mine.at[place], from_link.at[n], along_y if half == 0 else along_x
        )

    for n, (x, y) in enumerate(OCTET_ORDER):
        yield begin + piece_time * (2 * n + 0.5)
        for half in range(2):
            place = octet_place(0, x, y, half)
            over_core[place] = board.send(outgoing.at[place], from_core.at[place], core)
        yield begin + piece_time * (2 * n + 1.5)
        if n == 0:
            pass_second(1, 1, 0, 0)
            pass_second(1, 1, 1, 1)
        elif n == 1:
            pass_second(0, 1, 0, 2)
        elif n == 2:
            pass_second(1, 0, 1, 3)
    for n, (x, y, half) in enumerate(((1, 0, 0), (0, 1, 1))):
        yield begin + max(unit * 1.2 + 2.0 * piece_time, 7.6 * piece_time)
        place = add_core(x, y, half)
        second[(1, 1, half)].wait_recv()
        add_rows(mine.at[place], from_link.at[half])
        third[half] = board.send(
            mine.at[place], from_link.at[4 + n], along_x if half == 0 else along_y
        )
    for half, sent in ((0, (0, 1, 0)), (1, (1, 0, 1))):
        yield begin + unit * 3.1 + 2.0 * piece_time
        place = add_core(0, 0, half)
        second[sent].wait_recv()
        third[half].wait_recv()

        @pl.loop(0, h // 16)
        def _(step):
            rows = pl.ds(pl.multiple_of(step * 16, 16), 16)
            out_rows = pl.ds(pl.multiple_of(half * h + step * 16, 16), 16)
            sum_ref[out_rows, :] = (
                mine[place, rows, :].astype(jnp.float32)
                + from_link[2 + half, rows, :].astype(jnp.float32)
                + from_link[4 + half, rows, :].astype(jnp.float32)
            )


def octet_pieces(board, m, piece_time, product):
    def run(core, x, y):
        value = product(((core * 2 + x) * 2 + y) * m)
        target = board.terms[0 if core else 1]
        for half in range(2):
            place = octet_place(0, x, y, half)
            target[place] = value[half * (m // 2) : (half + 1) * (m // 2)].astype(target.dtype)

    plan = []
    for x, y in OCTET_ORDER:
        for core in (1, 0):
            plan.append((piece_time * len(plan), functools.partial(run, core, x, y)))
    return plan


def line_gather_steps(board, shard_ref, whole_ref, begin=0.0):
    unit = 4.0 * math.prod(shard_ref.shape) / LINK
    z = board.z
    far, near = board.line_xor(2), ("line", 1)
    two = board.send(shard_ref, whole_ref.at[z], ("line", 2))
    one = board.send(shard_ref, whole_ref.at[z], near)
    three_slot, on_slot = board.slot(), board.slot()
    three = board.make(three_slot, shard_ref, whole_ref.at[z], ("line", 3))
    onward = pltpu.make_async_remote_copy(
        src_ref=whole_ref.at[far],
        dst_ref=whole_ref.at[far],
        send_sem=board.sems[0].at[on_slot],
        recv_sem=board.sems[1].at[three_slot],
        device_id=board.device(near),
        device_id_type=MESH,
    )

    keep = board.move(shard_ref, whole_ref.at[z], close=False)
    yield begin + 2.0 * unit
    two.wait_recv()

    @pl.when(board.middle)
    def _():
        onward.start()
        three.start()

    yield begin + 3.1 * unit
    keep.wait()
    one.wait_recv()
    three.wait_recv()

    @pl.when(board.middle)
    def _():
        three.wait_send()
        onward.wait_send()


def line_reduce_steps(board, terms_ref, got_ref, held, carried, begin=0.0):
    unit = 4.0 * math.prod(got_ref.shape[1:]) / LINK
    near, two_off, three_off = ("line", 1), ("line", 2), ("line", 3)
    z_near, z_two, z_three = (board.line_xor(k) for k in (1, 2, 3))
    carry = board.make(board.slot(), terms_ref.at[z_three], carried, near)
    direct = board.make(board.slot(), terms_ref.at[z_three], got_ref.at[2], three_off)
    two_slot = board.slot()
    two_end = board.make(two_slot, terms_ref.at[z_two], got_ref.at[1], two_off)
    two_mid = board.make(two_slot, held, got_ref.at[1], two_off)

    one = board.make(board.slot(), terms_ref.at[z_near], got_ref.at[0], near)

    @pl.when(jnp.logical_not(board.middle))
    def _():
        carry.start()

    @pl.when(board.middle)
    def _():
        one.start()
        direct.start()

    load = board.move(terms_ref.at[z_two], held, close=False)
    yield begin + 1.05 * unit
    load.wait()

    @pl.when(jnp.logical_not(board.middle))
    def _():
        carry.wait_send()
        two_end.start()
        one.start()

    @pl.when(board.middle)
    def _():
        carry.wait_recv()
        add_rows(held, carried)
        two_mid.start()

    yield begin + 3.1 * unit
    one.wait_recv()
    one.wait_send()
    two_end.wait_recv()
    two_end.wait_send()

    @pl.when(board.middle)
    def _():
        direct.wait_recv()
        direct.wait_send()


def plane_exchange_steps(board, blocks_ref, given_ref, begin=0.0):
    copies = [
        board.send(
            blocks_ref.at[board.place_xor(k)], given_ref.at[board.i], ("plane", k)
        )
        for k in (3, 2, 1)
    ]
    keep = board.move(blocks_ref.at[board.i], given_ref.at[board.i], close=False)
    yield begin + 9.0 * math.prod(blocks_ref.shape[1:]) / LINK
    for copy in copies:
        copy.wait_recv()
    keep.wait()


def transpose_steps(board, shard_ref, given_ref, begin=0.0):
    slot, spot = board.slot(), board.locals
    board.locals += 1
    other = (board.i * PLANE + board.z, board.t)
    copy = pltpu.make_async_remote_copy(
        src_ref=shard_ref,
        dst_ref=given_ref,
        send_sem=board.sems[0].at[slot],
        recv_sem=board.sems[1].at[slot],
        device_id=other,
        device_id_type=MESH,
    )
    keep = pltpu.make_async_copy(shard_ref, given_ref, board.sems[2].at[spot])

    @pl.when(board.i != board.z)
    def _():
        copy.start()

    @pl.when(board.i == board.z)
    def _():
        keep.start()

    yield begin + 9.0 * math.prod(shard_ref.shape) / LINK

    @pl.when(board.i != board.z)
    def _():
        copy.wait()

    @pl.when(board.i == board.z)
    def _():
        keep.wait()


NEAR_OCTET = (("plane", 1), ("plane", 2), "y")
NEAR_PLANE = (("plane", 1), ("plane", 2), ("plane", 3))
NEAR_LINE = (("line", 1), ("line", 2), ("line", 3))


def hbm(shape):
    return (jax.ShapeDtypeStruct(shape, jnp.bfloat16), HBM_SPEC)


class OctetGather:
    near, remotes, moves = NEAR_OCTET, 13, 1

    def __init__(self, own):
        self.given = own
        self.outs = [hbm((8 * own.shape[0],) + own.shape[1:])]
        self.scratch = []

    def steps(self, board, own, outs, scratch):
        return octet_gather_steps(board, own, outs[0])

    def read(self, outs):
        return outs[0]


class OctetReduce:
    near, remotes, moves = NEAR_OCTET, 14, 8

    def __init__(self, terms):
        self.given = terms
        m, n = terms.shape[0] // 8, terms.shape[1]
        self.outs = [(jax.ShapeDtypeStruct((m, n), jnp.float32), VMEM_SPEC)]
        self.scratch = [pltpu.VMEM((k, m // 2, n), terms.dtype) for k in (8, 8, 6)]

    def steps(self, board, terms, outs, scratch):
        return octet_reduce_steps(board, terms, outs[0], *scratch)

    def read(self, outs):
        return outs[0]


class LineGather:
    near, remotes, moves = NEAR_LINE, 4, 1

    def __init__(self, shard):
        self.given = shard
        self.outs = [hbm((LINE,) + shard.shape)]
        self.scratch = []

    def steps(self, board, shard, outs, scratch):
        return line_gather_steps(board, shard, outs[0])

    def read(self, outs):
        return outs[0]

    def plain(self):
        return lax.all_gather(self.given, "dp", axis_index_groups=line_groups(), axis=0)


class LineReduce:
    near, remotes, moves = NEAR_LINE, 4, 1

    def __init__(self, terms):
        self.given = terms
        shape = terms.shape[1:]
        self.outs = [hbm((3,) + shape)]
        self.scratch = [pltpu.VMEM(shape, terms.dtype)] * 2

    def steps(self, board, terms, outs, scratch):
        return line_reduce_steps(board, terms, outs[0], *scratch)

    def read(self, outs):
        z = line_index()
        got = outs[0].astype(jnp.float32)
        middle = (z == 1) | (z == 2)
        own = take(self.given, z).astype(jnp.float32)
        return own + got[0] + got[1] + jnp.where(middle, got[2], 0.0)

    def plain(self):
        return lax.psum_scatter(
            self.given, "dp", axis_index_groups=line_groups(), scatter_dimension=0
        ).astype(jnp.float32)


class PlaneExchange:
    near, remotes, moves = NEAR_PLANE, 3, 1

    def __init__(self, blocks):
        self.given = blocks
        self.outs = [hbm(blocks.shape)]
        self.scratch = []

    def steps(self, board, blocks, outs, scratch):
        return plane_exchange_steps(board, blocks, outs[0])

    def read(self, outs):
        return outs[0]

    def plain(self):
        i = plane_index()
        whole = jnp.zeros_like(self.given)
        for k in range(PLANE):
            piece = take(self.given, i ^ k)
            if k:
                piece = swap(piece, k)
            whole = lax.dynamic_update_index_in_dim(whole, piece, i ^ k, 0)
        return whole


class GatherColumns:
    near, remotes, moves = NEAR_PLANE + NEAR_LINE, 7, 2

    def __init__(self, blocks, hold=0.0):
        self.given = blocks
        self.outs = [hbm(blocks.shape), hbm((LINE,) + blocks.shape)]
        self.scratch = []
        self.hold = hold

    def steps(self, board, blocks, outs, scratch):
        begin = max(self.hold, 9.0 * math.prod(blocks.shape[1:]) / LINK)
        yield from plane_exchange_steps(board, blocks, outs[0])
        yield begin
        yield from line_gather_steps(board, outs[0], outs[1], begin)

    def read(self, outs):
        return outs[1]

    def plain(self):
        return LineGather(PlaneExchange(self.given).plain()).plain()


class GatherPack:
    near, remotes, moves = NEAR_LINE + NEAR_OCTET, 17, 2

    def __init__(self, shard):
        self.given = shard
        self.outs = [hbm((LINE,) + shard.shape), hbm((8 * LINE,) + shard.shape)]
        self.scratch = []

    def steps(self, board, shard, outs, scratch):
        begin = 13.2 * math.prod(shard.shape) / LINK
        yield from line_gather_steps(board, shard, outs[0])
        yield from octet_gather_steps(board, outs[0], outs[1], begin)

    def read(self, outs):
        return outs[1]


class Transpose:
    near, remotes, moves = ("transposed",), 1, 1

    def __init__(self, shard, back=False):
        self.given = shard
        self.back = back
        self.outs = [hbm(shard.shape)]
        self.scratch = []

    def steps(self, board, shard, outs, scratch):
        return transpose_steps(board, shard, outs[0])

    def read(self, outs):
        return outs[0]

    def plain(self):
        line = lax.axis_size("dp") // PLANE
        pairs = [(i * line + z, z * PLANE + i) for i in range(PLANE) for z in range(line)]
        if self.back:
            pairs = [(b, a) for a, b in pairs]
        return lax.ppermute(self.given, "dp", pairs)


class GatherMoved(Transpose):
    near, remotes, moves = ("transposed",) + NEAR_LINE, 5, 2

    def __init__(self, shard):
        super().__init__(shard)
        self.outs = [hbm(shard.shape), hbm((LINE,) + shard.shape)]

    def steps(self, board, shard, outs, scratch):
        begin = 9.0 * math.prod(shard.shape) / LINK
        yield from transpose_steps(board, shard, outs[0])
        yield from line_gather_steps(board, outs[0], outs[1], begin)

    def read(self, outs):
        return outs[1]

    def plain(self):
        return LineGather(super().plain()).plain()


class OctetReduceInside:
    near, remotes, moves = NEAR_OCTET, 14, 0

    def __init__(self, m, n, piece_time):
        self.given = None
        self.outs = [(jax.ShapeDtypeStruct((m, n), jnp.float32), VMEM_SPEC)]
        self.scratch = [pltpu.VMEM((k, m // 2, n), jnp.bfloat16) for k in (8, 8, 8, 6)]
        self.piece_time = piece_time

    def steps(self, board, given, outs, scratch):
        return octet_reduce_inside_steps(board, outs[0], *scratch, self.piece_time)

    def read(self, outs):
        return outs[0]


class Later:
    def __init__(self, task, when):
        self.task, self.when = task, when
        self.near, self.remotes, self.moves = task.near, task.remotes, task.moves
        self.given, self.outs, self.scratch = task.given, task.outs, task.scratch
        self.read, self.plain = task.read, getattr(task, "plain", None)

    def steps(self, *where):
        yield self.when
        yield from self.task.steps(*where)


class Together:
    def __init__(self, first, second):
        self.parts = (first, second)
        self.givens = first.givens + second.givens
        self.outs = first.outs + second.outs
        self.scratch = first.scratch + second.scratch
        self.given_specs = first.given_specs + second.given_specs
        self.out_specs = first.out_specs + second.out_specs

    def phases(self, givens, outs, scratch, *rest):
        a = self.parts[0]
        cuts = len(a.givens), len(a.outs), len(a.scratch)
        plan = a.phases(givens[: cuts[0]], outs[: cuts[1]], scratch[: cuts[2]], *rest)
        plan = plan + self.parts[1].phases(
            givens[cuts[0] :], outs[cuts[1] :], scratch[cuts[2] :], *rest
        )
        return sorted(plan, key=lambda item: item[0])


class PieceProduct:
    def __init__(self, left, right, m, piece_time, columns=False):
        self.givens, self.outs, self.scratch = [left, right], [], []
        self.given_specs, self.out_specs = [VMEM_SPEC] * 2, []
        self.m, self.piece_time, self.columns = m, piece_time, columns

    def phases(self, givens, outs, scratch, board, task_givens, task_outs):
        left, right = givens

        def product(row):
            if self.columns:
                return left_transposed(left[:, row : row + self.m], right[...])
            return column_dot(left[row : row + self.m, :], right[...])

        return octet_pieces(board, self.m, self.piece_time, product)


class UnitBlocks:
    def __init__(self, gate, up, line):
        self.givens = [gate, up]
        rows, columns = gate.shape
        self.given_specs, self.out_specs = [VMEM_SPEC] * 2, [VMEM_SPEC] * 2
        self.outs = [
            jax.ShapeDtypeStruct((PLANE, rows, columns // PLANE), jnp.bfloat16)
        ] * 2
        self.scratch = []
        self.line = line

    def phases(self, givens, outs, scratch, board, task_givens, task_outs):
        rows, columns = givens[0].shape
        width = columns // (PLANE * self.line)
        step_rows = 16 if rows % 16 == 0 else rows

        def run(source, target):
            @pl.loop(0, rows // step_rows)
            def _(step):
                here = pl.ds(pl.multiple_of(step * step_rows, step_rows), step_rows)
                values = source[here, :]
                for i in range(PLANE):
                    target[i, here, :] = jnp.concatenate(
                        [
                            values[:, (z * PLANE + i) * width : (z * PLANE + i + 1) * width]
                            for z in range(self.line)
                        ],
                        axis=1,
                    ).astype(target.dtype)

        return [
            (1.0 + 6.0 * n, functools.partial(run, givens[n], outs[n])) for n in range(2)
        ]


def communicate(collective_id, *tasks, compute=None):
    if lax.axis_size("dp") != PLANE * LINE:
        results = []
        for n, task in enumerate(tasks):
            alone = 4 * collective_id + n
            if isinstance(task, (OctetGather, OctetReduce)):
                results += run_kernel(alone, [task])
            elif isinstance(task, GatherPack):
                results += run_kernel(alone, [OctetGather(LineGather(task.given).plain())])
            else:
                results.append(task.plain())
        return results + (run_kernel(None, [], compute) if compute else [])
    return run_kernel(collective_id, tasks, compute)


def run_kernel(collective_id, tasks, compute=None):
    near = []
    for task in tasks:
        near += [name for name in task.near if name not in near]
    n_outs = [len(task.outs) for task in tasks]
    n_scratch = [len(task.scratch) for task in tasks]
    inputs = [task.given for task in tasks if task.given is not None]
    more_givens = compute.givens if compute else []
    more_outs = compute.outs if compute else []
    more_scratch = compute.scratch if compute else []
    more_given_specs = compute.given_specs if compute else []
    more_out_specs = compute.out_specs if compute else []

    def kernel(*refs):
        refs = list(refs)

        def first(count):
            part = refs[:count]
            del refs[:count]
            return part

        givens = [None if task.given is None else first(1)[0] for task in tasks]
        compute_givens = first(len(more_givens))
        outs, compute_outs = first(sum(n_outs)), first(len(more_outs))
        scratch, compute_scratch = first(sum(n_scratch)), first(len(more_scratch))
        running, closing = [], []
        if tasks:
            board = Board(*refs)
            closing = board.closing
            board.greet(near)
        for n, task in enumerate(tasks):
            steps = task.steps(
                board,
                givens[n],
                outs[sum(n_outs[:n]) : sum(n_outs[: n + 1])],
                scratch[sum(n_scratch[:n]) : sum(n_scratch[: n + 1])],
            )
            running.append((next(steps), n, steps))
        phases = []
        if compute:
            phases = compute.phases(
                compute_givens,
                compute_outs,
                compute_scratch,
                board if tasks else None,
                givens,
                outs,
            )
        while running or phases:
            running.sort(key=lambda item: item[:2])
            if phases and not (running and running[0][0] <= phases[0][0]):
                phases.pop(0)[1]()
                continue
            when, n, steps = running.pop(0)
            when = next(steps, None)
            if when is not None:
                running.append((when, n, steps))
        for close in closing:
            close()

    sems = []
    if tasks:
        sems = [
            pltpu.SemaphoreType.DMA((sum(task.remotes for task in tasks),)),
            pltpu.SemaphoreType.DMA((sum(task.remotes for task in tasks),)),
            pltpu.SemaphoreType.DMA((sum(task.moves for task in tasks),)),
        ]
    outs = pl.pallas_call(
        kernel,
        out_shape=[shape for task in tasks for shape, _ in task.outs] + more_outs,
        in_specs=[HBM_SPEC] * len(inputs) + more_given_specs,
        out_specs=[spec for task in tasks for _, spec in task.outs]
        + more_out_specs,
        scratch_shapes=[shape for task in tasks for shape in task.scratch]
        + more_scratch
        + sems,
        compiler_params=pltpu.CompilerParams(
            collective_id=collective_id,
            has_side_effects=bool(tasks),
            vmem_limit_bytes=VMEM_LIMIT,
        ),
        cost_estimate=pl.CostEstimate(flops=0, bytes_accessed=2**28, transcendentals=0),
    )(*inputs, *more_givens)
    results = [
        task.read(outs[sum(n_outs[:n]) : sum(n_outs[: n + 1])]) for n, task in enumerate(tasks)
    ]
    return results + ([outs[sum(n_outs) :]] if compute else [])


def take(array, position):
    return lax.dynamic_index_in_dim(array, position, 0, keepdims=False)


def line_index():
    return lax.axis_index("dp") // PLANE


def plane_index():
    return lax.axis_index("dp") % PLANE


def line_groups():
    size = lax.axis_size("dp")
    return [[i + PLANE * z for z in range(size // PLANE)] for i in range(PLANE)]


def swap(array, bits):
    size = lax.axis_size("dp")
    return lax.ppermute(array, "dp", [(d, d ^ bits) for d in range(size)])


HEAD = 128
ROW_BLOCK = 64


def column_dot(left_side, right_side):
    return jnp.dot(left_side, right_side, preferred_element_type=jnp.float32)


def lane_index(shape):
    return lax.broadcasted_iota(jnp.int32, shape, len(shape) - 1)


def turn(values, wave, low_wave, high_wave):
    half = DR // 2
    return (
        values * wave
        + pltpu.roll(values, HEAD - half, 1) * low_wave
        + pltpu.roll(values, half, 1) * high_wave
    )


def score_bias(keys_ref, bounds_ref, bias, pack, pack_rows):
    @pl.loop(0, pack_rows // ROW_BLOCK)
    def _(block):
        rows = pl.ds(pl.multiple_of(block * ROW_BLOCK, ROW_BLOCK), ROW_BLOCK)
        here = bounds_ref[pl.ds(pack * pack_rows + block * ROW_BLOCK, ROW_BLOCK), :]
        key = keys_ref[pack, 0:1, :]
        allowed = (key >= here[:, 0:1]) & (key <= here[:, 1:2])
        bias[rows, :] = jnp.where(allowed, 0.0, MASKED)


class AttentionForward:
    def __init__(self, tokens, keys, bounds, waves, query_up, latent_up, packs, heads):
        rows = tokens.shape[0]
        self.packs, self.heads, self.pack_rows = packs, heads, rows // packs
        self.givens = [tokens, keys, bounds, *waves, query_up, latent_up]
        low = jnp.bfloat16
        self.pairs = -(-heads // 2)
        self.outs = [
            jax.ShapeDtypeStruct((rows, heads * HEAD), low),
            jax.ShapeDtypeStruct((rows, heads * HEAD), low),
            jax.ShapeDtypeStruct((rows, self.pairs * HEAD), low),
            jax.ShapeDtypeStruct((rows, HEAD), jnp.float32),
        ]
        self.scratch = [
            pltpu.VMEM((self.pack_rows, self.pack_rows), jnp.float32),
            pltpu.VMEM((self.pack_rows, heads * HEAD), jnp.float32),
            pltpu.VMEM((self.pack_rows, self.pack_rows), jnp.float32),
            pltpu.VMEM((self.pack_rows, self.pack_rows), low),
        ]
        self.phase_time = 9.5
        self.given_specs = [VMEM_SPEC] * len(self.givens)
        self.out_specs = [VMEM_SPEC] * len(self.outs)

    def phases(self, givens, outs, scratch, board, task_givens, task_outs):
        tokens, keys, bounds, wave, low_wave, high_wave, query_up, latent_up = givens
        queries, heads_out, mixed, totals = outs
        bias, raw, held, prob_low = scratch
        scale = QH ** (-0.5)
        size = self.pack_rows

        def run(pack, part):
            first, last = (0, self.heads // 2 + 1) if part == 0 else (self.heads // 2 + 1, self.heads)
            start = pack * size
            whole = slice(start, start + size)
            rope_key = pltpu.roll(
                tokens[whole, QR + KVR : QR + KVR + HEAD].astype(jnp.float32), DN, 1
            )
            if part == 0:
                score_bias(keys, bounds, bias, pack, size)
                for n in range(self.pairs):
                    mixed[whole, n * HEAD : (n + 1) * HEAD] = jnp.zeros((size, HEAD), mixed.dtype)
                totals[whole, :] = jnp.zeros((size, HEAD), jnp.float32)
                heads_out[whole, :] = column_dot(
                    tokens[whole, QR : QR + KVR], latent_up[...]
                ).astype(jnp.bfloat16)
                raw[...] = column_dot(tokens[whole, 0:QR], query_up[...])

            @pl.loop(first, last)
            def _(head):
                lanes = pl.ds(pl.multiple_of(head * HEAD, HEAD), HEAD)
                pair = pl.ds(pl.multiple_of((head // 2) * HEAD, HEAD), HEAD)
                even = head % 2 == 0
                tile = heads_out[whole, lanes]
                key_all = jnp.where(
                    lane_index((size, HEAD)) < DN, tile.astype(jnp.float32), rope_key
                ).astype(jnp.bfloat16)
                query_all = turn(
                    raw[:, lanes], wave[whole, :], low_wave[whole, :], high_wave[whole, :]
                ).astype(jnp.bfloat16)
                queries[whole, lanes] = query_all
                held[...] = right_transposed(query_all, key_all)
                for block in range(size // ROW_BLOCK):
                    part = slice(block * ROW_BLOCK, (block + 1) * ROW_BLOCK)
                    rows = slice(start + block * ROW_BLOCK, start + (block + 1) * ROW_BLOCK)
                    scores = held[part, :] * scale + bias[part, :]
                    top = jnp.max(scores, axis=1, keepdims=True)
                    exponent = jnp.exp(scores - top)
                    total = jnp.sum(exponent, axis=1, keepdims=True)
                    prob_low[part, :] = (exponent * (1.0 / total)).astype(jnp.bfloat16)
                    totals[rows, :] = jnp.where(
                        lane_index((ROW_BLOCK, HEAD)) == head,
                        top + jnp.log(total),
                        totals[rows, :],
                    )
                out = column_dot(prob_low[...], tile)
                lane = lane_index((size, HEAD))
                placed = jnp.where(even, pltpu.roll(out, DN, 1), out)
                before = mixed[whole, pair].astype(jnp.float32)
                mixed[whole, pair] = jnp.where((lane < DN) == even, placed, before).astype(
                    mixed.dtype
                )

        return [
            (self.phase_time * n, functools.partial(run, n // 2, n % 2))
            for n in range(2 * self.packs)
        ]


class AttentionBackward:
    def __init__(
        self,
        queries,
        latent_heads,
        totals,
        grad_mixed,
        tokens,
        keys,
        bounds,
        waves,
        query_up,
        latent_up,
        packs,
        heads,
    ):
        rows = tokens.shape[0]
        self.packs, self.heads, self.pack_rows = packs, heads, rows // packs
        self.givens = [
            queries,
            latent_heads,
            totals,
            grad_mixed,
            tokens,
            keys,
            bounds,
            *waves,
            query_up,
            latent_up,
        ]
        low = jnp.bfloat16
        self.outs = [
            jax.ShapeDtypeStruct((rows, heads * HEAD), low),
            jax.ShapeDtypeStruct((rows, heads * HEAD), low),
            jax.ShapeDtypeStruct((rows, QR + KVR + HEAD), low),
        ]
        size = self.pack_rows
        self.scratch = [
            pltpu.VMEM((size, size), jnp.float32),
            pltpu.VMEM((size, size), jnp.float32),
            pltpu.VMEM((size, size), jnp.float32),
            pltpu.VMEM((size, size), low),
            pltpu.VMEM((size, size), low),
            pltpu.VMEM((size, HEAD), jnp.float32),
        ]
        self.phase_time = 9.0
        self.given_specs = [VMEM_SPEC] * len(self.givens)
        self.out_specs = [VMEM_SPEC] * len(self.outs)

    def phases(self, givens, outs, scratch, board, task_givens, task_outs):
        (
            queries,
            heads_in,
            totals,
            grad_mixed,
            tokens,
            keys,
            bounds,
            wave,
            low_wave,
            high_wave,
            query_up,
            latent_up,
        ) = givens
        grad_queries, grad_heads, terms = outs
        bias, held, grad_held, prob_low, score_low, grad_rope = scratch
        scale = QH ** (-0.5)
        size = self.pack_rows

        def run(pack, part):
            first, last = (0, self.heads // 2 + 1) if part == 0 else (self.heads // 2 + 1, self.heads)
            start = pack * size
            whole = slice(start, start + size)
            rope_key = pltpu.roll(
                tokens[whole, QR + KVR : QR + KVR + HEAD].astype(jnp.float32), DN, 1
            )
            if part == 0:
                score_bias(keys, bounds, bias, pack, size)
                grad_rope[...] = jnp.zeros_like(grad_rope)

            @pl.loop(first, last)
            def _(head):
                lanes = pl.ds(pl.multiple_of(head * HEAD, HEAD), HEAD)
                pair = pl.ds(pl.multiple_of((head // 2) * HEAD, HEAD), HEAD)
                even = head % 2 == 0
                lane = lane_index((size, HEAD))
                tile = heads_in[whole, lanes]
                query_all = queries[whole, lanes]
                key_all = jnp.where(lane < DN, tile.astype(jnp.float32), rope_key).astype(
                    jnp.bfloat16
                )
                grad_pair = grad_mixed[whole, pair].astype(jnp.float32)
                grad_out = jnp.where(
                    lane < DN, 0.0, jnp.where(even, pltpu.roll(grad_pair, DN, 1), grad_pair)
                ).astype(jnp.bfloat16)
                total_all = jnp.sum(
                    jnp.where(lane == head, totals[whole, :], 0.0), axis=1, keepdims=True
                )
                held[...] = right_transposed(query_all, key_all)
                grad_held[...] = right_transposed(grad_out, tile)
                for block in range(size // ROW_BLOCK):
                    part = slice(block * ROW_BLOCK, (block + 1) * ROW_BLOCK)
                    prob = jnp.exp(held[part, :] * scale + bias[part, :] - total_all[part])
                    grad_prob = grad_held[part, :]
                    inner = jnp.sum(prob * grad_prob, axis=1, keepdims=True)
                    prob_low[part, :] = prob.astype(jnp.bfloat16)
                    score_low[part, :] = (prob * (grad_prob - inner)).astype(jnp.bfloat16)
                grad_query = column_dot(score_low[...], key_all) * scale
                grad_queries[whole, lanes] = turn(
                    grad_query, wave[whole, :], -low_wave[whole, :], -high_wave[whole, :]
                ).astype(grad_queries.dtype)
                grad_value = left_transposed(prob_low[...], grad_out)
                grad_key = left_transposed(score_low[...], query_all) * scale
                grad_rope[...] += grad_key
                grad_heads[whole, lanes] = jnp.where(lane < DN, grad_key, grad_value).astype(
                    grad_heads.dtype
                )

            if part == 0:
                return
            terms[whole, 0:QR] = right_transposed(grad_queries[whole, :], query_up[...]).astype(
                terms.dtype
            )
            terms[whole, QR : QR + KVR] = right_transposed(
                grad_heads[whole, :], latent_up[...]
            ).astype(terms.dtype)
            terms[whole, QR + KVR :] = pltpu.roll(grad_rope[...], HEAD - DN, 1).astype(terms.dtype)

        return [
            (self.phase_time * n, functools.partial(run, n // 2, n % 2))
            for n in range(2 * self.packs)
        ]


class FfnForward:
    order = (
        ((0, 0, 0), 0.0),
        ((1, 0, 0), 0.26),
        ((0, 0, 1), 2.01),
        ((0, 1, 0), 2.02),
        ((1, 0, 1), 2.31),
        ((1, 1, 0), 2.32),
        ((0, 1, 1), 3.01),
        ((1, 1, 1), 3.31),
    )

    def __init__(self, gate, up, rows, unit):
        self.givens = [gate, up]
        self.given_specs = self.out_specs = [HBM_SPEC] * 2
        depth, units = gate.shape
        self.rows, self.unit = rows, unit
        self.outs = [jax.ShapeDtypeStruct((8 * rows, units), jnp.float32)] * 2
        self.scratch = [
            pltpu.VMEM((2, depth, units), gate.dtype),
            pltpu.VMEM((2, rows, depth), gate.dtype),
            pltpu.VMEM((2, 2, rows, units), jnp.float32),
            pltpu.SemaphoreType.DMA((2,)),
            pltpu.SemaphoreType.DMA((2,)),
            pltpu.SemaphoreType.DMA((2, 2)),
        ]

    def phases(self, givens, outs, scratch, board, task_givens, task_outs):
        weights, tokens, staged, weight_sems, token_sems, out_sems = scratch
        own, gathered = task_givens[0], task_outs[0]
        loads = [
            pltpu.make_async_copy(givens[n], weights.at[n], weight_sems.at[n]) for n in range(2)
        ]
        for load in loads:
            load.start()
        leaving = {}

        def run(step, place):
            spot = (place[0] * 2 + place[1]) * 2 + place[2]
            rows = pl.ds(spot * self.rows, self.rows)
            if spot:
                assert place in board.here
            slot = step % 2
            fetch = pltpu.make_async_copy(
                gathered.at[rows] if spot else own, tokens.at[slot], token_sems.at[slot]
            )
            fetch.start()
            fetch.wait()
            for n in range(2):
                if step == 0:
                    loads[n].wait()
                if step >= 2:
                    leaving.pop((slot, n)).wait()
                staged[slot, n] = column_dot(tokens[slot], weights[n])
                copy = pltpu.make_async_copy(
                    staged.at[slot, n], outs[n].at[rows], out_sems.at[slot, n]
                )
                copy.start()
                leaving[(slot, n)] = copy

        def finish():
            for copy in leaving.values():
                copy.wait()

        plan = [
            (when * self.unit, functools.partial(run, step, place))
            for step, (place, when) in enumerate(self.order)
        ]
        return plan + [(1e9, finish)]


class FfnBackward:
    CHUNK = 256

    def __init__(self, normed, grad_gate, grad_up, gate, up, m, piece_time):
        self.givens = [normed, grad_gate, grad_up, gate, up]
        self.given_specs = [HBM_SPEC] * 5
        self.out_specs = [HBM_SPEC] * 2
        rows, depth = normed.shape
        units = gate.shape[1]
        low = normed.dtype
        self.rows, self.depth, self.units = rows, depth, units
        self.m, self.piece_time = m, piece_time
        self.outs = [jax.ShapeDtypeStruct((depth, units), low)] * 2
        self.scratch = [
            pltpu.VMEM((rows, units), low),
            pltpu.VMEM((rows, units), low),
            pltpu.VMEM((depth, units), low),
            pltpu.VMEM((depth, units), low),
            pltpu.SemaphoreType.DMA((4,)),
        ]

    def phases(self, givens, outs, scratch, board, task_givens, task_outs):
        normed = givens[0]
        held, sems = scratch[:4], scratch[4]
        gate_held, up_held, gate_weight, up_weight = held
        chunk, rows, units, depth = self.CHUNK, self.rows, self.units, self.depth
        loads = [
            pltpu.make_async_copy(givens[n + 1], held[n], sems.at[n]) for n in (0, 2, 1, 3)
        ]
        for load in loads:
            load.start()

        def product(row):
            while loads:
                loads.pop(0).wait()
            part = slice(row, row + self.m)
            return right_transposed(gate_held[part, :], gate_weight[...]) + right_transposed(
                up_held[part, :], up_weight[...]
            )

        def gradients(first, count):
            def body(normed_part, gate_part, up_part):
                left = normed_part[...]
                gate_part[...] = left_transposed(left, gate_held[...]).astype(gate_part.dtype)
                up_part[...] = left_transposed(left, up_held[...]).astype(up_part.dtype)

            pltpu.emit_pipeline(
                body,
                grid=(count,),
                in_specs=[pl.BlockSpec((rows, chunk), lambda n: (0, n + first))],
                out_specs=[pl.BlockSpec((chunk, units), lambda n: (n + first, 0))] * 2,
            )(normed, outs[0], outs[1])

        plan = octet_pieces(board, self.m, self.piece_time, product)
        when = plan[-1][0] + self.piece_time
        for first in range(0, depth // chunk, 2):
            plan.append((when, functools.partial(gradients, first, 2)))
            when += 6.0
        return plan


class FfnProducts:
    CHUNK = 256

    def __init__(self, hidden, down):
        self.givens = [hidden, down]
        self.given_specs, self.out_specs = [HBM_SPEC] * 2, [HBM_SPEC]
        self.outs = [jax.ShapeDtypeStruct((hidden.shape[0], down.shape[1]), down.dtype)]
        self.scratch = [pltpu.VMEM(down.shape, down.dtype), pltpu.SemaphoreType.DMA]

    def phases(self, givens, outs, scratch, board, task_givens, task_outs):
        hidden, down = givens
        down_held, sem = scratch
        chunk = self.CHUNK
        load = pltpu.make_async_copy(down, down_held, sem)
        load.start()

        def products(first, count):
            if first == 0:
                load.wait()

            def body(hidden_part, out_part):
                out_part[...] = column_dot(hidden_part[...], down_held[...]).astype(out_part.dtype)

            pltpu.emit_pipeline(
                body,
                grid=(count,),
                in_specs=[pl.BlockSpec((chunk, hidden.shape[1]), lambda n: (n + first, 0))],
                out_specs=[pl.BlockSpec((chunk, down.shape[1]), lambda n: (n + first, 0))],
            )(hidden, outs[0])

        return [
            (2.0 + 2.0 * first, functools.partial(products, first, 2))
            for first in range(0, hidden.shape[0] // chunk, 2)
        ]


class UnitUpdate:
    def __init__(self, parts, weight, first_moment, second_moment, line):
        self.givens = [parts, weight, first_moment, second_moment]
        self.given_specs, self.out_specs = [VMEM_SPEC] * 4, [VMEM_SPEC] * 3
        self.outs = [jax.ShapeDtypeStruct(weight.shape, jnp.float32)] * 3
        self.scratch = []
        self.line = line

    def phases(self, givens, outs, scratch, board, task_givens, task_outs):
        parts, weight, first_moment, second_moment = givens
        rows, columns = weight.shape
        width = columns // (PLANE * self.line)
        step_rows = 16 if rows % 16 == 0 else rows

        def run(half):
            count = rows // step_rows
            split = (0, count // 2, count)

            @pl.loop(split[half], split[half + 1])
            def _(step):
                here = pl.ds(pl.multiple_of(step * step_rows, step_rows), step_rows)
                pieces = [parts[i, here, :].astype(jnp.float32) for i in range(PLANE)]
                gradient = jnp.concatenate(
                    [
                        pieces[i][:, z * width : (z + 1) * width]
                        for z in range(self.line)
                        for i in range(PLANE)
                    ],
                    axis=1,
                )
                results = adamw_update(
                    weight[here, :],
                    first_moment[here, :],
                    second_moment[here, :],
                    gradient,
                    matrix_rate(D),
                )
                for out, result in zip(outs, results):
                    out[here, :] = result

        return [(12.5, functools.partial(run, 0)), (18.5, functools.partial(run, 1))]


def positions(segment_ids):
    token_index = jnp.arange(segment_ids.shape[0], dtype=jnp.int32)
    doc_start = jnp.concatenate(
        [jnp.ones((1,), dtype=jnp.bool_), segment_ids[1:] != segment_ids[:-1]]
    )
    starts = lax.cummax(jnp.where(doc_start, token_index, 0), axis=0)
    return token_index - starts


def rope_tables(position):
    exponent = jnp.arange(DR // 2, dtype=jnp.float32) * (2.0 / DR)
    rope_angle = position[:, None] * (ROPE_BASE ** (-exponent))[None, :]
    return (jnp.cos(rope_angle), jnp.sin(rope_angle))


def local(
    inputs,
    cotangent,
    segment_ids,
    gains,
    gains_first,
    gains_second,
    query_down,
    query_down_first,
    query_down_second,
    latent_down,
    latent_down_first,
    latent_down_second,
    query_up,
    query_up_first,
    query_up_second,
    latent_up,
    latent_up_first,
    latent_up_second,
    output_proj,
    output_proj_first,
    output_proj_second,
    gate_proj,
    gate_proj_first,
    gate_proj_second,
    up_proj,
    up_proj_first,
    up_proj_second,
    down_proj,
    down_proj_first,
    down_proj_second,
):
    size = lax.axis_size("dp")
    tensor = lax.axis_size("tensor")
    line = size // PLANE
    z, i, t = line_index(), plane_index(), lax.axis_index("tensor")
    half_rows = inputs.shape[0]
    pack_rows = segment_ids.shape[0]
    packs = PLANE
    rows_all = packs * pack_rows
    low = jnp.bfloat16
    local_heads = H // (PLANE * tensor)
    units = FF // (PLANE * tensor)
    mixed_width = -(-local_heads // 2) * HEAD

    def column_blocks(weight, columns):
        return weight.astype(low).reshape(-1, PLANE, columns).transpose(1, 0, 2)

    down_rows = query_down.shape[0]
    pack_height = down_rows + 16
    gain_width = gains.shape[0]
    down_pack = jnp.concatenate(
        [
            jnp.concatenate([query_down, latent_down], axis=1).astype(low),
            jnp.pad(gains.astype(low)[None], ((0, 15), (0, QR + KVR + DR - gain_width))),
        ],
        axis=0,
    )
    def head_blocks(weight):
        blocks = weight.astype(low).reshape(-1, PLANE, local_heads, QH)
        blocks = jnp.pad(blocks, ((0, 0), (0, 0), (0, 0), (0, HEAD - QH)))
        return blocks.reshape(-1, PLANE, local_heads * HEAD).transpose(1, 0, 2)

    pack_all, query_up_all, latent_up_all, output_moved, (gate_blocks, up_blocks) = communicate(
        1,
        GatherPack(down_pack),
        GatherColumns(head_blocks(query_up), 16.0),
        GatherColumns(column_blocks(latent_up, local_heads * KH), 16.0),
        Later(Transpose(output_proj.astype(low)), 16.0),
        compute=UnitBlocks(gate_proj, up_proj, line),
    )
    query_up_all = query_up_all.reshape(QR, local_heads * HEAD)
    latent_up_all = latent_up_all.reshape(KVR, local_heads * KH)
    down_octet = pack_all.reshape(2, 2, tensor, line, pack_height, QR + KVR + DR)
    down_blocks = jnp.zeros((PLANE, tensor, line, pack_height, QR + KVR + DR), low)
    for k in range(PLANE):
        for y in range(tensor):
            down_blocks = lax.dynamic_update_slice(
                down_blocks,
                down_octet[k % 2, k // 2, y][None, None],
                (i ^ k, (t + y) % tensor, 0, 0, 0),
            )
    down_blocks = down_blocks.transpose(2, 0, 1, 3, 4)
    down_both = down_blocks[..., :down_rows, :].reshape(D, QR + KVR + DR)
    gain_values = down_blocks[..., down_rows, :gain_width].reshape(-1).astype(jnp.float32)
    gain_attention = gain_values[:D]
    gain_query = gain_values[D : D + QR]
    gain_latent = gain_values[D + QR : D + QR + KVR]
    gain_ffn = gain_values[D + QR + KVR :]

    incoming = inputs.astype(jnp.float32)
    attn_unit, inverse_attention = norm_forward(incoming, gain_attention)
    normed_attn = attn_unit.astype(low)
    both_latent = jnp.dot(normed_attn, down_both, preferred_element_type=jnp.float32)
    query_latent = both_latent[:, :QR]
    latent = both_latent[:, QR:]
    query_unit, inverse_query = norm_forward(query_latent, gain_query)
    latent_unit, inverse_latent = norm_forward(latent[:, :KVR], gain_latent)
    own_position = lax.dynamic_slice_in_dim(positions(segment_ids), t * half_rows, half_rows)
    own_segment = lax.dynamic_slice_in_dim(segment_ids, t * half_rows, half_rows)
    own_cosine, own_sine = rope_tables(own_position.astype(jnp.float32))
    own_rope_key = rotate(latent[:, KVR:], own_cosine, own_sine)
    marks = jnp.stack(
        [own_segment // 16, own_segment % 16, own_position // 16, own_position % 16], axis=1
    )
    tokens_own = jnp.concatenate(
        [
            query_unit.astype(low),
            latent_unit.astype(low),
            own_rope_key.astype(low),
            marks.astype(low),
            jnp.zeros((half_rows, 128 - DR - 4), low),
        ],
        axis=1,
    )
    tokens_all, output_all, gate_plane = communicate(
        3, OctetGather(tokens_own), LineGather(output_moved), PlaneExchange(gate_blocks)
    )
    output_all = jnp.pad(
        output_all.reshape(local_heads * DV, D), ((0, mixed_width - local_heads * DV), (0, 0))
    )
    marks_all = tokens_all[:, QR + KVR + DR : QR + KVR + DR + 4].astype(jnp.float32)
    key_base = (marks_all[:, 0] * 16.0 + marks_all[:, 1]) * pack_rows
    position = marks_all[:, 2] * 16.0 + marks_all[:, 3]
    key = key_base + position
    keys = jnp.broadcast_to(key.reshape(packs, 1, pack_rows), (packs, 8, pack_rows))
    bounds = jnp.pad(jnp.stack([key_base, key], axis=1), ((0, 0), (0, HEAD - 2)))
    rope_cosine, rope_sine = rope_tables(position)
    nothing = jnp.zeros((rows_all, DR), jnp.float32)
    still = jnp.zeros((rows_all, DN), jnp.float32)
    waves = (
        jnp.concatenate([still + 1.0, rope_cosine, rope_cosine, nothing], axis=1),
        jnp.concatenate([still, -rope_sine, nothing, nothing[:, : DR // 2]], axis=1),
        jnp.concatenate([still, nothing[:, : DR // 2], rope_sine, nothing], axis=1),
    )
    grad_ffn, up_plane, gate_all, (queries, latent_heads, mixed_heads, log_totals) = communicate(
        2,
        OctetGather((RESIDUAL * cotangent.astype(jnp.float32)).astype(low)),
        PlaneExchange(up_blocks),
        LineGather(gate_plane),
        compute=AttentionForward(
            tokens_all, keys, bounds, waves, query_up_all, latent_up_all, packs, local_heads
        ),
    )
    gate_all = gate_all.reshape(D, units)
    if line == LINE:
        attention_sum, up_all, _ = communicate(
            4,
            OctetReduceInside(half_rows, D, 2.0),
            LineGather(up_plane),
            compute=PieceProduct(mixed_heads, output_all, half_rows, 2.0),
        )
    else:
        attention_terms = jnp.dot(mixed_heads, output_all, preferred_element_type=jnp.float32)
        attention_sum, up_all = communicate(
            4, OctetReduce(attention_terms.astype(low)), LineGather(up_plane)
        )
    up_all = up_all.reshape(D, units)
    residual = incoming + RESIDUAL * attention_sum

    ffn_unit, inverse_ffn = norm_forward(residual, gain_ffn)
    normed_own = ffn_unit.astype(low)
    tasks = (OctetGather(normed_own), LineGather(down_proj.astype(low)))
    if line == LINE:
        normed_ffn, down_all, (gate_value, up_value) = communicate(
            5,
            *tasks,
            compute=FfnForward(gate_all, up_all, half_rows, octet_unit((half_rows, D))),
        )
    else:
        normed_ffn, down_all = communicate(5, *tasks)
        gate_value = jnp.dot(normed_ffn, gate_all, preferred_element_type=jnp.float32)
        up_value = jnp.dot(normed_ffn, up_all, preferred_element_type=jnp.float32)
    down_all = down_all.reshape(units, D)
    gate_sigmoid = lax.logistic(gate_value)
    silu_gate = gate_value * gate_sigmoid
    hidden = (silu_gate * up_value).astype(low)
    grad_hidden = right_transposed(grad_ffn, down_all)
    grad_gate = (
        grad_hidden * up_value * gate_sigmoid * (1.0 + gate_value * (1.0 - gate_sigmoid))
    ).astype(low)
    grad_up = (grad_hidden * silu_gate).astype(low)
    down_grad = left_transposed(hidden, grad_ffn).astype(low).reshape(line, -1, D)
    if line == LINE:
        grad_normed_ffn, down_shard, (gate_grad, up_grad) = communicate(
            6,
            OctetReduceInside(half_rows, D, 5.0),
            LineReduce(down_grad),
            compute=FfnBackward(normed_ffn, grad_gate, grad_up, gate_all, up_all, half_rows, 5.0),
        )
    else:
        back_terms = right_transposed(grad_gate, gate_all) + right_transposed(grad_up, up_all)
        gate_grad = left_transposed(normed_ffn, grad_gate).astype(low)
        up_grad = left_transposed(normed_ffn, grad_up).astype(low)
        grad_normed_ffn, down_shard = communicate(
            6, OctetReduce(back_terms.astype(low)), LineReduce(down_grad)
        )
    outer_grad = cotangent.astype(jnp.float32)
    grad_incoming_ffn, gain_ffn_grad = norm_backward(
        residual, inverse_ffn, gain_ffn, grad_normed_ffn
    )
    grad_residual = outer_grad + grad_incoming_ffn

    grad_branch, gate_sum, (ffn_terms,) = communicate(
        7,
        OctetGather((RESIDUAL * grad_residual).astype(low)),
        LineReduce(gate_grad.reshape(line, PLANE, -1, units)),
        compute=FfnProducts(hidden, down_all),
    )
    output_grad = (
        left_transposed(mixed_heads, grad_branch)
        .astype(low)[: local_heads * DV]
        .reshape(line, -1, D)
    )
    grad_mixed = right_transposed(grad_branch, output_all).astype(low)
    ffn_sum, up_sum, gate_parts, (grad_query_heads, grad_latent_heads, grad_unit_terms) = communicate(
        8,
        OctetReduce(ffn_terms),
        LineReduce(up_grad.reshape(line, PLANE, -1, units)),
        PlaneExchange(gate_sum.astype(low)),
        compute=AttentionBackward(
            queries,
            latent_heads,
            log_totals,
            grad_mixed,
            tokens_all,
            keys,
            bounds,
            waves,
            query_up_all,
            latent_up_all,
            packs,
            local_heads,
        ),
    )
    block_output = (residual + RESIDUAL * ffn_sum).astype(low)
    query_up_grad = left_transposed(tokens_all[:, :QR], grad_query_heads).astype(low)
    latent_up_grad = left_transposed(tokens_all[:, QR : QR + KVR], grad_latent_heads).astype(low)
    grad_units, output_sum, up_parts, gate_out = communicate(
        9,
        OctetReduce(grad_unit_terms),
        LineReduce(output_grad),
        PlaneExchange(up_sum.astype(low)),
        compute=UnitUpdate(gate_parts, gate_proj, gate_proj_first, gate_proj_second, line),
    )
    grad_query_wide, gain_query_grad = norm_backward(
        query_latent, inverse_query, gain_query, grad_units[:, :QR]
    )
    grad_latent_part, gain_latent_grad = norm_backward(
        latent[:, :KVR], inverse_latent, gain_latent, grad_units[:, QR : QR + KVR]
    )
    grad_rope = unrotate(grad_units[:, QR + KVR : QR + KVR + DR], own_cosine, own_sine)
    grad_both = jnp.concatenate([grad_query_wide, grad_latent_part, grad_rope], axis=1).astype(low)
    grad_normed_attn = right_transposed(grad_both, down_both)
    grad_incoming_attn, gain_attention_grad = norm_backward(
        incoming, inverse_attention, gain_attention, grad_normed_attn
    )
    input_grad = (grad_residual + grad_incoming_attn).astype(low)
    gains_grad = jnp.concatenate(
        [gain_attention_grad, gain_query_grad, gain_latent_grad, gain_ffn_grad]
    ).astype(low)
    shards = size * tensor
    left_blocks = normed_attn.reshape(half_rows, line, PLANE, tensor, down_rows)
    left_blocks = jnp.pad(left_blocks, ((0, 0), (0, 0), (0, 0), (0, 0), (0, 16)))
    spots = jnp.arange(pack_height)[None, None, :] == down_rows
    shard_index = jnp.arange(shards)
    left_marks = (
        (shard_index[:, None, None] == shard_index[None, :, None]) & spots
    ).astype(low)
    left_blocks = jnp.concatenate(
        [left_blocks, left_marks.reshape(shards, line, PLANE, tensor, pack_height)], axis=0
    ).transpose(2, 3, 0, 1, 4)
    pack_left = jnp.concatenate(
        [
            lax.dynamic_slice(
                left_blocks,
                (i ^ (core + 2 * x), (t + y) % tensor, 0, 0, 0),
                (1, 1) + left_blocks.shape[2:],
            ).reshape(half_rows + shards, line * pack_height)
            for core in range(2)
            for x in range(2)
            for y in range(tensor)
        ],
        axis=1,
    )
    pack_right = jnp.concatenate(
        [
            grad_both,
            jnp.pad(
                gains_grad.reshape(shards, gain_width),
                ((0, 0), (0, QR + KVR + DR - gain_width)),
            ),
        ],
        axis=0,
    )
    pack_rows_all = line * pack_height
    up_update = UnitUpdate(up_parts, up_proj, up_proj_first, up_proj_second, line)
    if line == LINE:
        pack_task = OctetReduceInside(pack_rows_all, QR + KVR + DR, 1.5)
        tail_compute = Together(
            PieceProduct(pack_left, pack_right, pack_rows_all, 1.5, columns=True), up_update
        )
    else:
        pack_task = OctetReduce(left_transposed(pack_left, pack_right).astype(low))
        tail_compute = up_update
    pack_octet, query_up_sum, latent_up_sum, output_shard, up_out = communicate(
        10,
        pack_task,
        LineReduce(query_up_grad.reshape(line, PLANE, -1, local_heads * HEAD)),
        LineReduce(latent_up_grad.reshape(line, PLANE, -1, local_heads * KH)),
        Transpose(output_sum.astype(low), back=True),
        compute=tail_compute,
    )
    pack_sum, query_up_parts, latent_up_parts = communicate(
        11,
        LineReduce(pack_octet.astype(low).reshape(line, pack_height, QR + KVR + DR)),
        PlaneExchange(query_up_sum.astype(low)),
        PlaneExchange(latent_up_sum.astype(low)),
    )
    query_down_shard = pack_sum[:down_rows, :QR]
    latent_down_shard = pack_sum[:down_rows, QR:]
    gains_shard = pack_sum[down_rows, :gain_width]

    def head_columns(blocks):
        return blocks.astype(jnp.float32).transpose(1, 0, 2).reshape(blocks.shape[1], -1)

    query_up_parts = query_up_parts.reshape(PLANE, -1, local_heads, HEAD)[..., :QH]
    query_up_shard = head_columns(query_up_parts.reshape(PLANE, -1, local_heads * QH))
    latent_up_shard = head_columns(latent_up_parts)
    output_shard = output_shard.astype(jnp.float32)

    gains_out = adamw_update(gains, gains_first, gains_second, gains_shard, GAIN_RATE)
    query_down_out = adamw_update(
        query_down, query_down_first, query_down_second, query_down_shard, matrix_rate(D)
    )
    latent_down_out = adamw_update(
        latent_down, latent_down_first, latent_down_second, latent_down_shard, matrix_rate(D)
    )
    query_up_out = adamw_update(
        query_up, query_up_first, query_up_second, query_up_shard, matrix_rate(QR)
    )
    latent_up_out = adamw_update(
        latent_up, latent_up_first, latent_up_second, latent_up_shard, matrix_rate(KVR)
    )
    output_out = adamw_update(
        output_proj, output_proj_first, output_proj_second, output_shard, matrix_rate(H * DV // 64)
    )
    down_out = adamw_update(
        down_proj, down_proj_first, down_proj_second, down_shard, matrix_rate(FF // 8)
    )
    return (
        block_output,
        input_grad,
        gains_out[0],
        gains_out[1],
        gains_out[2],
        query_down_out[0],
        query_down_out[1],
        query_down_out[2],
        latent_down_out[0],
        latent_down_out[1],
        latent_down_out[2],
        query_up_out[0],
        query_up_out[1],
        query_up_out[2],
        latent_up_out[0],
        latent_up_out[1],
        latent_up_out[2],
        output_out[0],
        output_out[1],
        output_out[2],
        gate_out[0],
        gate_out[1],
        gate_out[2],
        up_out[0],
        up_out[1],
        up_out[2],
        down_out[0],
        down_out[1],
        down_out[2],
    )


def solution(mesh):
    in_specs = (
        P(("dp", "tensor"), None),
        P(("dp", "tensor"), None),
        P("dp"),
        P(("dp", "tensor")),
        P(("dp", "tensor")),
        P(("dp", "tensor")),
        P(("dp", "tensor"), None),
        P(("dp", "tensor"), None),
        P(("dp", "tensor"), None),
        P(("dp", "tensor"), None),
        P(("dp", "tensor"), None),
        P(("dp", "tensor"), None),
        P("dp", "tensor"),
        P("dp", "tensor"),
        P("dp", "tensor"),
        P("dp", "tensor"),
        P("dp", "tensor"),
        P("dp", "tensor"),
        P(("tensor", "dp"), None),
        P(("tensor", "dp"), None),
        P(("tensor", "dp"), None),
        P("dp", "tensor"),
        P("dp", "tensor"),
        P("dp", "tensor"),
        P("dp", "tensor"),
        P("dp", "tensor"),
        P("dp", "tensor"),
        P(("tensor", "dp"), None),
        P(("tensor", "dp"), None),
        P(("tensor", "dp"), None),
    )
    out_specs = (
        P(("dp", "tensor"), None),
        P(("dp", "tensor"), None),
        P(("dp", "tensor")),
        P(("dp", "tensor")),
        P(("dp", "tensor")),
        P(("dp", "tensor"), None),
        P(("dp", "tensor"), None),
        P(("dp", "tensor"), None),
        P(("dp", "tensor"), None),
        P(("dp", "tensor"), None),
        P(("dp", "tensor"), None),
        P("dp", "tensor"),
        P("dp", "tensor"),
        P("dp", "tensor"),
        P("dp", "tensor"),
        P("dp", "tensor"),
        P("dp", "tensor"),
        P(("tensor", "dp"), None),
        P(("tensor", "dp"), None),
        P(("tensor", "dp"), None),
        P("dp", "tensor"),
        P("dp", "tensor"),
        P("dp", "tensor"),
        P("dp", "tensor"),
        P("dp", "tensor"),
        P("dp", "tensor"),
        P(("tensor", "dp"), None),
        P(("tensor", "dp"), None),
        P(("tensor", "dp"), None),
    )
    return jax.shard_map(local, mesh=mesh, in_specs=in_specs, out_specs=out_specs, check_vma=False)
```

```python
import functools
import math

import jax
import jax.numpy as jnp
from jax import lax
from jax.experimental import pallas as pl
from jax.experimental.pallas import tpu as pltpu
from jax.sharding import PartitionSpec as P

D = 2560
H = 40
DN = 64
DR = 32
DV = 64
QR = 768
KVR = 256
FF = 6400
STEP = 10
QH = 96
KH = 128


RESIDUAL = 1.4 / math.sqrt(62.0)
NORM_EPSILON = 1e-05
MOMENT_DECAY = 0.9
SQUARE_DECAY = 0.95
ADAM_EPSILON = 1e-08
WEIGHT_DECAY = 0.1
GAIN_RATE = 0.3
ROPE_BASE = 10000.0
MASKED = -1e30


def right_transposed(left_side, right_side):
    return lax.dot_general(
        left_side, right_side, (((1,), (1,)), ((), ())), preferred_element_type=jnp.float32
    )


def left_transposed(left_side, right_side):
    return lax.dot_general(
        left_side, right_side, (((0,), (0,)), ((), ())), preferred_element_type=jnp.float32
    )


def norm_forward(values, gain_values):
    inverse = lax.rsqrt(jnp.mean(values * values, axis=-1, keepdims=True) + NORM_EPSILON)
    return (values * inverse * gain_values, inverse)


def norm_backward(values, inverse, gain_values, grad_out):
    unit_values = values * inverse
    weighted = grad_out * gain_values
    grad_values = inverse * (
        weighted - unit_values * jnp.mean(weighted * unit_values, axis=-1, keepdims=True)
    )
    return (grad_values, jnp.sum(grad_out * unit_values, axis=0))


def rotate(values, rope_cosine, rope_sine):
    half_width = values.shape[-1] // 2
    first_half = values[..., :half_width]
    second_half = values[..., half_width:]
    return jnp.concatenate(
        [
            first_half * rope_cosine - second_half * rope_sine,
            second_half * rope_cosine + first_half * rope_sine,
        ],
        axis=-1,
    )


def unrotate(grads_in, rope_cosine, rope_sine):
    half_width = grads_in.shape[-1] // 2
    first_half = grads_in[..., :half_width]
    second_half = grads_in[..., half_width:]
    return jnp.concatenate(
        [
            first_half * rope_cosine + second_half * rope_sine,
            second_half * rope_cosine - first_half * rope_sine,
        ],
        axis=-1,
    )


def adamw_update(weight, first_moment, second_moment, gradient, step_rate):
    new_first = MOMENT_DECAY * first_moment + (1.0 - MOMENT_DECAY) * gradient
    new_second = SQUARE_DECAY * second_moment + (1.0 - SQUARE_DECAY) * gradient * gradient
    first_hat = new_first / (1.0 - MOMENT_DECAY**STEP)
    second_hat = new_second / (1.0 - SQUARE_DECAY**STEP)
    new_weight = weight - step_rate * (
        first_hat / (jnp.sqrt(second_hat) + ADAM_EPSILON) + WEIGHT_DECAY * weight
    )
    return (new_weight, new_first, new_second)


def matrix_rate(fan_in):
    return 2.0 / math.sqrt(fan_in)


PLANE = 4
LINE = 4
LINK = 8.4e4
MESH = pl.DeviceIdType.MESH
VMEM_LIMIT = 56 * 1024 * 1024
HBM_SPEC = pl.BlockSpec(memory_space=pl.ANY)
VMEM_SPEC = pl.BlockSpec(memory_space=pltpu.VMEM)


class Board:
    def __init__(self, send_sems, recv_sems, local_sems):
        self.sems = (send_sems, recv_sems, local_sems)
        self.remotes = 0
        self.locals = 0
        self.closing = []
        self.here = set()
        self.d = lax.axis_index("dp")
        self.t = lax.axis_index("tensor")
        self.z = self.d // PLANE
        self.i = self.d % PLANE
        self.middle = (self.z == 1) | (self.z == 2)
        self.known = {
            name: self.work_out(name) for name in NEAR_OCTET + NEAR_PLANE + NEAR_LINE
        }

    def place_xor(self, k):
        i = self.i
        return (i, i + 1 - 2 * (i % 2), i + 2 - 4 * (i // 2), 3 - i)[k]

    def line_xor(self, k):
        z = self.z
        return (z, z + 1 - 2 * (z % 2), z + 2 - 4 * (z // 2), 3 - z)[k]

    def device(self, name):
        return self.known[name]

    def work_out(self, name):
        if name == "y":
            return (self.d, 1 - self.t)
        kind, k = name
        if kind == "plane":
            return (self.z * PLANE + self.place_xor(k), self.t)
        return (self.line_xor(k) * PLANE + self.i, self.t)

    def greet(self, names):
        barrier = pltpu.get_barrier_semaphore()
        known = [name for name in names if name != "transposed"]
        for name in known:
            pl.semaphore_signal(
                barrier, inc=1, device_id=self.device(name), device_id_type=MESH
            )
        if len(known) == len(names):
            pl.semaphore_wait(barrier, len(known))
            return

        @pl.when(self.i != self.z)
        def _():
            pl.semaphore_signal(
                barrier,
                inc=1,
                device_id=(self.i * PLANE + self.z, self.t),
                device_id_type=MESH,
            )
            pl.semaphore_wait(barrier, len(known) + 1)

        @pl.when(self.i == self.z)
        def _():
            pl.semaphore_wait(barrier, len(known))

    def slot(self):
        self.remotes += 1
        return self.remotes - 1

    def make(self, slot, source, target, name):
        return pltpu.make_async_remote_copy(
            src_ref=source,
            dst_ref=target,
            send_sem=self.sems[0].at[slot],
            recv_sem=self.sems[1].at[slot],
            device_id=self.device(name),
            device_id_type=MESH,
        )

    def send(self, source, target, name):
        copy = self.make(self.slot(), source, target, name)
        copy.start()
        self.closing.append(copy.wait_send)
        return copy

    def move(self, source, target, close=True):
        copy = pltpu.make_async_copy(source, target, self.sems[2].at[self.locals])
        self.locals += 1
        copy.start()
        if close:
            self.closing.append(copy.wait)
        return copy


def octet_place(core, x, y, half):
    return ((core * 2 + x) * 2 + y) * 2 + half


def octet_unit(shape):
    return 2.0 * math.prod(shape) / LINK


def octet_gather_steps(board, own_ref, all_ref, begin=0.0):
    h = own_ref.shape[0] // 2
    unit = octet_unit(own_ref.shape)

    def rows(place, count=1):
        return all_ref.at[pl.ds(place * h, count * h)]

    core, along_x, along_y = ("plane", 1), ("plane", 2), "y"
    first, second = own_ref.at[pl.ds(0, h)], own_ref.at[pl.ds(h, h)]
    first_x = board.send(first, rows(octet_place(0, 1, 0, 0)), along_x)
    second_y = board.send(second, rows(octet_place(0, 0, 1, 1)), along_y)
    first_y = board.send(first, rows(octet_place(0, 0, 1, 0)), along_y)
    second_x = board.send(second, rows(octet_place(0, 1, 0, 1)), along_x)
    whole_core = board.send(own_ref, rows(octet_place(1, 0, 0, 0), 2), core)
    board.move(own_ref, rows(0, 2))

    def onward(start, end, name):
        return board.send(rows(octet_place(*start)), rows(octet_place(*end)), name)

    def to_core(*place):
        return onward((0,) + place, (1,) + place, core)

    yield begin + 0.25 * unit
    whole_core.wait_recv()
    board.here.add((1, 0, 0))
    yield begin + unit
    first_x.wait_recv()
    first_xy = onward((0, 1, 0, 0), (0, 1, 1, 0), along_y)
    core_x = [to_core(1, 0, 0)]
    second_y.wait_recv()
    second_xy = onward((0, 0, 1, 1), (0, 1, 1, 1), along_x)
    core_y = [to_core(0, 1, 1)]
    yield begin + 2.0 * unit
    first_y.wait_recv()
    core_y.append(to_core(0, 1, 0))
    second_x.wait_recv()
    core_x.append(to_core(1, 0, 1))
    board.here.update(((0, 0, 1), (0, 1, 0)))
    yield begin + 2.3 * unit
    for copy in core_x + core_y:
        copy.wait_recv()
    board.here.update(((1, 0, 1), (1, 1, 0)))
    yield begin + 3.0 * unit
    first_xy.wait_recv()
    core_xy = [to_core(1, 1, 0)]
    second_xy.wait_recv()
    core_xy.append(to_core(1, 1, 1))
    board.here.add((0, 1, 1))
    yield begin + 3.3 * unit
    for copy in core_xy:
        copy.wait_recv()
    board.here.add((1, 1, 1))


def add_rows(target, other):
    if target.shape[-2] % 16 == 0:
        count = target.shape[-2] // 16

        def part(step):
            return (pl.ds(pl.multiple_of(step * 16, 16), 16), slice(None))

    else:
        assert target.shape[-1] % 128 == 0
        count = target.shape[-1] // 128

        def part(step):
            return (slice(None), pl.ds(pl.multiple_of(step * 128, 128), 128))

    for lead in range(math.prod(target.shape[:-2])):
        a, b = target, other
        if len(target.shape) > 2:
            a, b = target.at[lead], other.at[lead]

        @pl.loop(0, count)
        def _(step):
            here = part(step)
            a[here] = (a[here].astype(jnp.float32) + b[here].astype(jnp.float32)).astype(a.dtype)


def octet_reduce_steps(board, terms_ref, sum_ref, mine, from_core, from_link, begin=0.0):
    h = sum_ref.shape[0] // 2
    unit = octet_unit(sum_ref.shape)
    core, along_x, along_y = ("plane", 1), ("plane", 2), "y"
    order = (
        (1, 1, 0),
        (1, 1, 1),
        (0, 1, 0),
        (1, 0, 1),
        (1, 0, 0),
        (0, 1, 1),
        (0, 0, 0),
        (0, 0, 1),
    )
    over_core = {}
    loads = {}
    for x, y, half in order:
        place = octet_place(0, x, y, half)
        loads[place] = board.move(
            terms_ref.at[pl.ds(place * h, h)], mine.at[place], close=False
        )
        over_core[place] = board.send(
            terms_ref.at[pl.ds((8 + place) * h, h)], from_core.at[place], core
        )

    def add_core(x, y, half):
        place = octet_place(0, x, y, half)
        loads[place].wait()
        over_core[place].wait_recv()
        add_rows(mine.at[place], from_core.at[place])
        return place

    second = {}
    for n, (x, y, half) in enumerate(order[:4]):
        yield begin + 0.1 * unit * (n + 1)
        place = add_core(x, y, half)
        second[(x, y, half)] = board.send(
            mine.at[place], from_link.at[n], along_y if half == 0 else along_x
        )
    third = {}
    for n, (x, y, half) in enumerate(order[4:6]):
        yield begin + unit * 1.2
        place = add_core(x, y, half)
        second[(1, 1, half)].wait_recv()
        add_rows(mine.at[place], from_link.at[half])
        third[half] = board.send(
            mine.at[place], from_link.at[4 + n], along_x if half == 0 else along_y
        )
    for half, sent in ((0, (0, 1, 0)), (1, (1, 0, 1))):
        yield begin + unit * 3.1
        place = add_core(0, 0, half)
        second[sent].wait_recv()
        third[half].wait_recv()

        @pl.loop(0, h // 16)
        def _(step):
            rows = pl.ds(pl.multiple_of(step * 16, 16), 16)
            out_rows = pl.ds(pl.multiple_of(half * h + step * 16, 16), 16)
            sum_ref[out_rows, :] = (
                mine[place, rows, :].astype(jnp.float32)
                + from_link[2 + half, rows, :].astype(jnp.float32)
                + from_link[4 + half, rows, :].astype(jnp.float32)
            )


OCTET_ORDER = ((1, 1), (0, 1), (1, 0), (0, 0))


def octet_reduce_inside_steps(
    board, sum_ref, outgoing, mine, from_core, from_link, piece_time, begin=0.0
):
    h = sum_ref.shape[0] // 2
    unit = octet_unit(sum_ref.shape)
    core, along_x, along_y = ("plane", 1), ("plane", 2), "y"
    board.terms = (outgoing, mine)
    over_core, second, third = {}, {}, {}

    def add_core(x, y, half):
        place = octet_place(0, x, y, half)
        over_core[place].wait_recv()
        add_rows(mine.at[place], from_core.at[place])
        return place

    def pass_second(x, y, half, n):
        place = add_core(x, y, half)
        second[(x, y, half)] = board.send(
            mine.at[place], from_link.at[n], along_y if half == 0 else along_x
        )

    for n, (x, y) in enumerate(OCTET_ORDER):
        yield begin + piece_time * (2 * n + 0.5)
        for half in range(2):
            place = octet_place(0, x, y, half)
            over_core[place] = board.send(outgoing.at[place], from_core.at[place], core)
        yield begin + piece_time * (2 * n + 1.5)
        if n == 0:
            pass_second(1, 1, 0, 0)
            pass_second(1, 1, 1, 1)
        elif n == 1:
            pass_second(0, 1, 0, 2)
        elif n == 2:
            pass_second(1, 0, 1, 3)
    for n, (x, y, half) in enumerate(((1, 0, 0), (0, 1, 1))):
        yield begin + max(unit * 1.2 + 2.0 * piece_time, 7.6 * piece_time)
        place = add_core(x, y, half)
        second[(1, 1, half)].wait_recv()
        add_rows(mine.at[place], from_link.at[half])
        third[half] = board.send(
            mine.at[place], from_link.at[4 + n], along_x if half == 0 else along_y
        )
    for half, sent in ((0, (0, 1, 0)), (1, (1, 0, 1))):
        yield begin + unit * 3.1 + 2.0 * piece_time
        place = add_core(0, 0, half)
        second[sent].wait_recv()
        third[half].wait_recv()

        @pl.loop(0, h // 16)
        def _(step):
            rows = pl.ds(pl.multiple_of(step * 16, 16), 16)
            out_rows = pl.ds(pl.multiple_of(half * h + step * 16, 16), 16)
            sum_ref[out_rows, :] = (
                mine[place, rows, :].astype(jnp.float32)
                + from_link[2 + half, rows, :].astype(jnp.float32)
                + from_link[4 + half, rows, :].astype(jnp.float32)
            )


def octet_pieces(board, m, piece_time, product):
    def run(core, x, y):
        value = product(((core * 2 + x) * 2 + y) * m)
        target = board.terms[0 if core else 1]
        for half in range(2):
            place = octet_place(0, x, y, half)
            target[place] = value[half * (m // 2) : (half + 1) * (m // 2)].astype(target.dtype)

    plan = []
    for x, y in OCTET_ORDER:
        for core in (1, 0):
            plan.append((piece_time * len(plan), functools.partial(run, core, x, y)))
    return plan


def line_gather_steps(board, shard_ref, whole_ref, begin=0.0):
    unit = 4.0 * math.prod(shard_ref.shape) / LINK
    z = board.z
    far, near = board.line_xor(2), ("line", 1)
    two = board.send(shard_ref, whole_ref.at[z], ("line", 2))
    one = board.send(shard_ref, whole_ref.at[z], near)
    three_slot, on_slot = board.slot(), board.slot()
    three = board.make(three_slot, shard_ref, whole_ref.at[z], ("line", 3))
    onward = pltpu.make_async_remote_copy(
        src_ref=whole_ref.at[far],
        dst_ref=whole_ref.at[far],
        send_sem=board.sems[0].at[on_slot],
        recv_sem=board.sems[1].at[three_slot],
        device_id=board.device(near),
        device_id_type=MESH,
    )

    keep = board.move(shard_ref, whole_ref.at[z], close=False)
    yield begin + 2.0 * unit
    two.wait_recv()

    @pl.when(board.middle)
    def _():
        onward.start()
        three.start()

    yield begin + 3.1 * unit
    keep.wait()
    one.wait_recv()
    three.wait_recv()

    @pl.when(board.middle)
    def _():
        three.wait_send()
        onward.wait_send()


def line_reduce_steps(board, terms_ref, got_ref, held, carried, begin=0.0):
    unit = 4.0 * math.prod(got_ref.shape[1:]) / LINK
    near, two_off, three_off = ("line", 1), ("line", 2), ("line", 3)
    z_near, z_two, z_three = (board.line_xor(k) for k in (1, 2, 3))
    carry = board.make(board.slot(), terms_ref.at[z_three], carried, near)
    direct = board.make(board.slot(), terms_ref.at[z_three], got_ref.at[2], three_off)
    two_slot = board.slot()
    two_end = board.make(two_slot, terms_ref.at[z_two], got_ref.at[1], two_off)
    two_mid = board.make(two_slot, held, got_ref.at[1], two_off)

    one = board.make(board.slot(), terms_ref.at[z_near], got_ref.at[0], near)

    @pl.when(jnp.logical_not(board.middle))
    def _():
        carry.start()

    @pl.when(board.middle)
    def _():
        one.start()
        direct.start()

    load = board.move(terms_ref.at[z_two], held, close=False)
    yield begin + 1.05 * unit
    load.wait()

    @pl.when(jnp.logical_not(board.middle))
    def _():
        carry.wait_send()
        two_end.start()
        one.start()

    @pl.when(board.middle)
    def _():
        carry.wait_recv()
        add_rows(held, carried)
        two_mid.start()

    yield begin + 3.1 * unit
    one.wait_recv()
    one.wait_send()
    two_end.wait_recv()
    two_end.wait_send()

    @pl.when(board.middle)
    def _():
        direct.wait_recv()
        direct.wait_send()


def plane_exchange_steps(board, blocks_ref, given_ref, begin=0.0):
    copies = [
        board.send(
            blocks_ref.at[board.place_xor(k)], given_ref.at[board.i], ("plane", k)
        )
        for k in (3, 2, 1)
    ]
    keep = board.move(blocks_ref.at[board.i], given_ref.at[board.i], close=False)
    yield begin + 9.0 * math.prod(blocks_ref.shape[1:]) / LINK
    for copy in copies:
        copy.wait_recv()
    keep.wait()


def transpose_steps(board, shard_ref, given_ref, begin=0.0):
    slot, spot = board.slot(), board.locals
    board.locals += 1
    other = (board.i * PLANE + board.z, board.t)
    copy = pltpu.make_async_remote_copy(
        src_ref=shard_ref,
        dst_ref=given_ref,
        send_sem=board.sems[0].at[slot],
        recv_sem=board.sems[1].at[slot],
        device_id=other,
        device_id_type=MESH,
    )
    keep = pltpu.make_async_copy(shard_ref, given_ref, board.sems[2].at[spot])

    @pl.when(board.i != board.z)
    def _():
        copy.start()

    @pl.when(board.i == board.z)
    def _():
        keep.start()

    yield begin + 16.0 * math.prod(shard_ref.shape) / LINK

    @pl.when(board.i != board.z)
    def _():
        copy.wait()

    @pl.when(board.i == board.z)
    def _():
        keep.wait()


NEAR_OCTET = (("plane", 1), ("plane", 2), "y")
NEAR_PLANE = (("plane", 1), ("plane", 2), ("plane", 3))
NEAR_LINE = (("line", 1), ("line", 2), ("line", 3))


def hbm(shape):
    return (jax.ShapeDtypeStruct(shape, jnp.bfloat16), HBM_SPEC)


class OctetGather:
    near, remotes, moves = NEAR_OCTET, 13, 1

    def __init__(self, own):
        self.given = own
        self.outs = [hbm((8 * own.shape[0],) + own.shape[1:])]
        self.scratch = []

    def steps(self, board, own, outs, scratch):
        return octet_gather_steps(board, own, outs[0])

    def read(self, outs):
        return outs[0]


class OctetReduce:
    near, remotes, moves = NEAR_OCTET, 14, 8

    def __init__(self, terms):
        self.given = terms
        m, n = terms.shape[0] // 8, terms.shape[1]
        self.outs = [(jax.ShapeDtypeStruct((m, n), jnp.float32), VMEM_SPEC)]
        self.scratch = [pltpu.VMEM((k, m // 2, n), terms.dtype) for k in (8, 8, 6)]

    def steps(self, board, terms, outs, scratch):
        return octet_reduce_steps(board, terms, outs[0], *scratch)

    def read(self, outs):
        return outs[0]


class LineGather:
    near, remotes, moves = NEAR_LINE, 4, 1

    def __init__(self, shard):
        self.given = shard
        self.outs = [hbm((LINE,) + shard.shape)]
        self.scratch = []

    def steps(self, board, shard, outs, scratch):
        return line_gather_steps(board, shard, outs[0])

    def read(self, outs):
        return outs[0]

    def plain(self):
        return lax.all_gather(self.given, "dp", axis_index_groups=line_groups(), axis=0)


class LineReduce:
    near, remotes, moves = NEAR_LINE, 4, 1

    def __init__(self, terms):
        self.given = terms
        shape = terms.shape[1:]
        self.outs = [hbm((3,) + shape)]
        self.scratch = [pltpu.VMEM(shape, terms.dtype)] * 2

    def steps(self, board, terms, outs, scratch):
        return line_reduce_steps(board, terms, outs[0], *scratch)

    def read(self, outs):
        z = line_index()
        got = [outs[0][k].astype(jnp.float32) for k in range(3)]
        middle = (z == 1) | (z == 2)
        own = take(self.given, z).astype(jnp.float32)
        return own + got[0] + got[1] + jnp.where(middle, got[2], 0.0)

    def plain(self):
        return lax.psum_scatter(
            self.given, "dp", axis_index_groups=line_groups(), scatter_dimension=0
        ).astype(jnp.float32)


class PlaneExchange:
    near, remotes, moves = NEAR_PLANE, 3, 1

    def __init__(self, blocks):
        self.given = blocks
        self.outs = [hbm(blocks.shape)]
        self.scratch = []

    def steps(self, board, blocks, outs, scratch):
        return plane_exchange_steps(board, blocks, outs[0])

    def read(self, outs):
        return outs[0]

    def plain(self):
        i = plane_index()
        whole = jnp.zeros_like(self.given)
        for k in range(PLANE):
            piece = take(self.given, i ^ k)
            if k:
                piece = swap(piece, k)
            whole = lax.dynamic_update_index_in_dim(whole, piece, i ^ k, 0)
        return whole


class GatherColumns:
    near, remotes, moves = NEAR_PLANE + NEAR_LINE, 7, 2

    def __init__(self, blocks, hold=0.0):
        self.given = blocks
        self.outs = [hbm(blocks.shape), hbm((LINE,) + blocks.shape)]
        self.scratch = []
        self.hold = hold

    def steps(self, board, blocks, outs, scratch):
        begin = max(self.hold, 9.0 * math.prod(blocks.shape[1:]) / LINK)
        yield from plane_exchange_steps(board, blocks, outs[0])
        yield begin
        yield from line_gather_steps(board, outs[0], outs[1], begin)

    def read(self, outs):
        return outs[1]

    def plain(self):
        return LineGather(PlaneExchange(self.given).plain()).plain()


class GatherPack:
    near, remotes, moves = NEAR_LINE + NEAR_OCTET, 17, 2

    def __init__(self, shard):
        self.given = shard
        self.outs = [hbm((LINE,) + shard.shape), hbm((8 * LINE,) + shard.shape)]
        self.scratch = []

    def steps(self, board, shard, outs, scratch):
        begin = 13.2 * math.prod(shard.shape) / LINK
        yield from line_gather_steps(board, shard, outs[0])
        yield from octet_gather_steps(board, outs[0], outs[1], begin)

    def read(self, outs):
        return outs[1]


class Transpose:
    near, remotes, moves = ("transposed",), 1, 1

    def __init__(self, shard, back=False):
        self.given = shard
        self.back = back
        self.outs = [hbm(shard.shape)]
        self.scratch = []

    def steps(self, board, shard, outs, scratch):
        return transpose_steps(board, shard, outs[0])

    def read(self, outs):
        return outs[0]

    def plain(self):
        line = lax.axis_size("dp") // PLANE
        pairs = [(i * line + z, z * PLANE + i) for i in range(PLANE) for z in range(line)]
        if self.back:
            pairs = [(b, a) for a, b in pairs]
        return lax.ppermute(self.given, "dp", pairs)


class GatherMoved(Transpose):
    near, remotes, moves = ("transposed",) + NEAR_LINE, 5, 2

    def __init__(self, shard):
        super().__init__(shard)
        self.outs = [hbm(shard.shape), hbm((LINE,) + shard.shape)]

    def steps(self, board, shard, outs, scratch):
        begin = 9.0 * math.prod(shard.shape) / LINK
        yield from transpose_steps(board, shard, outs[0])
        yield from line_gather_steps(board, outs[0], outs[1], begin)

    def read(self, outs):
        return outs[1]

    def plain(self):
        return LineGather(super().plain()).plain()


class OctetReduceInside:
    near, remotes, moves = NEAR_OCTET, 14, 0

    def __init__(self, m, n, piece_time):
        self.given = None
        self.outs = [(jax.ShapeDtypeStruct((m, n), jnp.float32), VMEM_SPEC)]
        self.scratch = [pltpu.VMEM((k, m // 2, n), jnp.bfloat16) for k in (8, 8, 8, 6)]
        self.piece_time = piece_time

    def steps(self, board, given, outs, scratch):
        return octet_reduce_inside_steps(board, outs[0], *scratch, self.piece_time)

    def read(self, outs):
        return outs[0]


class Later:
    def __init__(self, task, when):
        self.task, self.when = task, when
        self.near, self.remotes, self.moves = task.near, task.remotes, task.moves
        self.given, self.outs, self.scratch = task.given, task.outs, task.scratch
        self.read, self.plain = task.read, getattr(task, "plain", None)

    def steps(self, *where):
        yield self.when
        for when in self.task.steps(*where):
            yield self.when + when


class Together:
    def __init__(self, first, second):
        self.parts = (first, second)
        self.givens = first.givens + second.givens
        self.outs = first.outs + second.outs
        self.scratch = first.scratch + second.scratch
        self.given_specs = first.given_specs + second.given_specs
        self.out_specs = first.out_specs + second.out_specs

    def phases(self, givens, outs, scratch, *rest):
        a = self.parts[0]
        cuts = len(a.givens), len(a.outs), len(a.scratch)
        plan = a.phases(givens[: cuts[0]], outs[: cuts[1]], scratch[: cuts[2]], *rest)
        plan = plan + self.parts[1].phases(
            givens[cuts[0] :], outs[cuts[1] :], scratch[cuts[2] :], *rest
        )
        return sorted(plan, key=lambda item: item[0])


class PieceProduct:
    def __init__(self, left, right, m, piece_time, columns=False):
        self.givens, self.outs, self.scratch = [left, right], [], []
        self.given_specs, self.out_specs = [VMEM_SPEC] * 2, []
        self.m, self.piece_time, self.columns = m, piece_time, columns

    def phases(self, givens, outs, scratch, board, task_givens, task_outs):
        left, right = givens

        def product(row):
            if self.columns:
                spot = row // self.m
                tensor = board.t if spot % 2 == 0 else 1 - board.t
                place = board.place_xor(spot // 4 + spot // 2 % 2 * 2) * 2 + tensor
                return left_transposed(left[place], right[...])
            return column_dot(left[row : row + self.m, :], right[...])

        return octet_pieces(board, self.m, self.piece_time, product)


class UnitBlocks:
    def __init__(self, gate, up, line):
        self.givens = [gate, up]
        rows, columns = gate.shape
        self.given_specs, self.out_specs = [VMEM_SPEC] * 2, [VMEM_SPEC] * 2
        self.outs = [
            jax.ShapeDtypeStruct((PLANE, rows, columns // PLANE), jnp.bfloat16)
        ] * 2
        self.scratch = []
        self.line = line

    def phases(self, givens, outs, scratch, board, task_givens, task_outs):
        rows, columns = givens[0].shape
        width = columns // (PLANE * self.line)
        step_rows = 16 if rows % 16 == 0 else rows

        count = rows // step_rows

        def run(source, target, first, last):
            @pl.loop(first, last)
            def _(step):
                here = pl.ds(pl.multiple_of(step * step_rows, step_rows), step_rows)
                values = source[here, :]
                for i in range(PLANE):
                    target[i, here, :] = jnp.concatenate(
                        [
                            values[:, (z * PLANE + i) * width : (z * PLANE + i + 1) * width]
                            for z in range(self.line)
                        ],
                        axis=1,
                    ).astype(target.dtype)

        return [
            (16.5, functools.partial(run, givens[0], outs[0], 0, count // 2)),
            (20.0, functools.partial(run, givens[0], outs[0], count // 2, count)),
            (26.0, functools.partial(run, givens[1], outs[1], 0, count // 2)),
            (36.0, functools.partial(run, givens[1], outs[1], count // 2, count)),
        ]


def communicate(collective_id, *tasks, compute=None):
    if lax.axis_size("dp") != PLANE * LINE:
        results = []
        for n, task in enumerate(tasks):
            alone = 4 * collective_id + n
            if isinstance(task, (OctetGather, OctetReduce)):
                results += run_kernel(alone, [task])
            elif isinstance(task, GatherPack):
                results += run_kernel(alone, [OctetGather(LineGather(task.given).plain())])
            else:
                results.append(task.plain())
        return results + (run_kernel(None, [], compute) if compute else [])
    return run_kernel(collective_id, tasks, compute)


def run_kernel(collective_id, tasks, compute=None):
    near = []
    for task in tasks:
        near += [name for name in task.near if name not in near]
    n_outs = [len(task.outs) for task in tasks]
    n_scratch = [len(task.scratch) for task in tasks]
    inputs = [task.given for task in tasks if task.given is not None]
    more_givens = compute.givens if compute else []
    more_outs = compute.outs if compute else []
    more_scratch = compute.scratch if compute else []
    given_staged = [spec is VMEM_SPEC for spec in compute.given_specs] if compute else []
    out_staged = [spec is VMEM_SPEC for spec in compute.out_specs] if compute else []
    staging = [
        pltpu.VMEM(array.shape, array.dtype)
        for arrays, staged in ((more_givens, given_staged), (more_outs, out_staged))
        for array, flag in zip(arrays, staged)
        if flag
    ]

    def kernel(*refs):
        refs = list(refs)

        def first(count):
            part = refs[:count]
            del refs[:count]
            return part

        givens = [None if task.given is None else first(1)[0] for task in tasks]
        compute_givens = first(len(more_givens))
        outs, compute_outs = first(sum(n_outs)), first(len(more_outs))
        scratch, compute_scratch = first(sum(n_scratch)), first(len(more_scratch))
        staged, loads, stores = first(len(staging)), [], []
        if staging:
            stage_sems = first(1)[0]
        copies = 0
        for n, flag in enumerate(given_staged):
            if flag:
                held = staged[copies]
                loads.append(
                    pltpu.make_async_copy(compute_givens[n], held, stage_sems.at[copies])
                )
                compute_givens[n] = held
                copies += 1
        for n, flag in enumerate(out_staged):
            if flag:
                held = staged[copies]
                stores.append(
                    pltpu.make_async_copy(held, compute_outs[n], stage_sems.at[copies])
                )
                compute_outs[n] = held
                copies += 1
        running, closing = [], []
        if tasks:
            board = Board(*refs)
            closing = board.closing
            board.greet(near)
        for n, task in enumerate(tasks):
            steps = task.steps(
                board,
                givens[n],
                outs[sum(n_outs[:n]) : sum(n_outs[: n + 1])],
                scratch[sum(n_scratch[:n]) : sum(n_scratch[: n + 1])],
            )
            running.append((next(steps), n, steps))
        phases = []
        for load in loads:
            load.start()
        if compute:
            phases = compute.phases(
                compute_givens,
                compute_outs,
                compute_scratch,
                board if tasks else None,
                givens,
                outs,
            )
        while running or phases:
            running.sort(key=lambda item: item[:2])
            if phases and not (running and running[0][0] <= phases[0][0]):
                while loads:
                    loads.pop(0).wait()
                phases.pop(0)[1]()
                if not phases:
                    for store in stores:
                        store.start()
                continue
            when, n, steps = running.pop(0)
            when = next(steps, None)
            if when is not None:
                running.append((when, n, steps))
        for close in closing:
            close()
        for store in stores:
            store.wait()

    sems = []
    if tasks:
        sems = [
            pltpu.SemaphoreType.DMA((sum(task.remotes for task in tasks),)),
            pltpu.SemaphoreType.DMA((sum(task.remotes for task in tasks),)),
            pltpu.SemaphoreType.DMA((sum(task.moves for task in tasks),)),
        ]
    outs = pl.pallas_call(
        kernel,
        out_shape=[shape for task in tasks for shape, _ in task.outs] + more_outs,
        in_specs=[HBM_SPEC] * (len(inputs) + len(more_givens)),
        out_specs=[spec for task in tasks for _, spec in task.outs]
        + [HBM_SPEC] * len(more_outs),
        scratch_shapes=[shape for task in tasks for shape in task.scratch]
        + more_scratch
        + staging
        + ([pltpu.SemaphoreType.DMA((len(staging),))] if staging else [])
        + sems,
        compiler_params=pltpu.CompilerParams(
            collective_id=collective_id,
            has_side_effects=bool(tasks),
            vmem_limit_bytes=VMEM_LIMIT,
        ),
        cost_estimate=pl.CostEstimate(flops=0, bytes_accessed=2**28, transcendentals=0),
    )(*inputs, *more_givens)
    results = [
        task.read(outs[sum(n_outs[:n]) : sum(n_outs[: n + 1])]) for n, task in enumerate(tasks)
    ]
    return results + ([outs[sum(n_outs) :]] if compute else [])


def take(array, position):
    return lax.dynamic_index_in_dim(array, position, 0, keepdims=False)


def line_index():
    return lax.axis_index("dp") // PLANE


def plane_index():
    return lax.axis_index("dp") % PLANE


def line_groups():
    size = lax.axis_size("dp")
    return [[i + PLANE * z for z in range(size // PLANE)] for i in range(PLANE)]


def swap(array, bits):
    size = lax.axis_size("dp")
    return lax.ppermute(array, "dp", [(d, d ^ bits) for d in range(size)])


HEAD = 128
ROW_BLOCK = 64


def column_dot(left_side, right_side):
    return jnp.dot(left_side, right_side, preferred_element_type=jnp.float32)


def lane_index(shape):
    return lax.broadcasted_iota(jnp.int32, shape, len(shape) - 1)


def turn(values, wave, low_wave, high_wave):
    half = DR // 2
    return (
        values * wave
        + pltpu.roll(values, HEAD - half, 1) * low_wave
        + pltpu.roll(values, half, 1) * high_wave
    )


def score_bias(keys_ref, bounds_ref, bias, pack, pack_rows):
    @pl.loop(0, pack_rows // ROW_BLOCK)
    def _(block):
        rows = pl.ds(pl.multiple_of(block * ROW_BLOCK, ROW_BLOCK), ROW_BLOCK)
        here = bounds_ref[pl.ds(pack * pack_rows + block * ROW_BLOCK, ROW_BLOCK), :]
        key = keys_ref[pack, 0:1, :]
        allowed = (key >= here[:, 0:1]) & (key <= here[:, 1:2])
        bias[rows, :] = jnp.where(allowed, 0.0, MASKED)


class AttentionForward:
    def __init__(self, tokens, keys, bounds, waves, query_up, latent_up, packs, heads):
        rows = tokens.shape[0]
        self.packs, self.heads, self.pack_rows = packs, heads, rows // packs
        self.givens = [tokens, keys, bounds, *waves, query_up, latent_up]
        low = jnp.bfloat16
        self.pairs = -(-heads // 2)
        self.outs = [
            jax.ShapeDtypeStruct((rows, heads * HEAD), low),
            jax.ShapeDtypeStruct((rows, heads * HEAD), low),
            jax.ShapeDtypeStruct((rows, self.pairs * HEAD), low),
            jax.ShapeDtypeStruct((rows, HEAD), jnp.float32),
        ]
        self.scratch = [
            pltpu.VMEM((self.pack_rows, self.pack_rows), jnp.float32),
            pltpu.VMEM((self.pack_rows, heads * HEAD), jnp.float32),
            pltpu.VMEM((self.pack_rows, self.pack_rows), jnp.float32),
            pltpu.VMEM((self.pack_rows, self.pack_rows), low),
        ]
        self.phase_time = 9.5
        self.given_specs = [VMEM_SPEC] * len(self.givens)
        self.out_specs = [VMEM_SPEC] * len(self.outs)

    def phases(self, givens, outs, scratch, board, task_givens, task_outs):
        tokens, keys, bounds, wave, low_wave, high_wave, query_up, latent_up = givens
        queries, heads_out, mixed, totals = outs
        bias, raw, held, prob_low = scratch
        scale = QH ** (-0.5)
        size = self.pack_rows

        def run(pack, part):
            first, last = (0, self.heads // 2 + 1) if part == 0 else (self.heads // 2 + 1, self.heads)
            start = pack * size
            whole = slice(start, start + size)
            rope_key = pltpu.roll(
                tokens[whole, QR + KVR : QR + KVR + HEAD].astype(jnp.float32), DN, 1
            )
            if part == 0:
                score_bias(keys, bounds, bias, pack, size)
                for n in range(self.pairs):
                    mixed[whole, n * HEAD : (n + 1) * HEAD] = jnp.zeros((size, HEAD), mixed.dtype)
                totals[whole, :] = jnp.zeros((size, HEAD), jnp.float32)
                heads_out[whole, :] = column_dot(
                    tokens[whole, QR : QR + KVR], latent_up[...]
                ).astype(jnp.bfloat16)
                raw[...] = column_dot(tokens[whole, 0:QR], query_up[...])

            @pl.loop(first, last)
            def _(head):
                lanes = pl.ds(pl.multiple_of(head * HEAD, HEAD), HEAD)
                pair = pl.ds(pl.multiple_of((head // 2) * HEAD, HEAD), HEAD)
                even = head % 2 == 0
                tile = heads_out[whole, lanes]
                key_all = jnp.where(
                    lane_index((size, HEAD)) < DN, tile.astype(jnp.float32), rope_key
                ).astype(jnp.bfloat16)
                query_all = turn(
                    raw[:, lanes], wave[whole, :], low_wave[whole, :], high_wave[whole, :]
                ).astype(jnp.bfloat16)
                queries[whole, lanes] = query_all
                held[...] = right_transposed(query_all, key_all)
                for block in range(size // ROW_BLOCK):
                    part = slice(block * ROW_BLOCK, (block + 1) * ROW_BLOCK)
                    rows = slice(start + block * ROW_BLOCK, start + (block + 1) * ROW_BLOCK)
                    scores = held[part, :] * scale + bias[part, :]
                    top = jnp.max(scores, axis=1, keepdims=True)
                    exponent = jnp.exp(scores - top)
                    total = jnp.sum(exponent, axis=1, keepdims=True)
                    prob_low[part, :] = (exponent * (1.0 / total)).astype(jnp.bfloat16)
                    totals[rows, :] = jnp.where(
                        lane_index((ROW_BLOCK, HEAD)) == head,
                        top + jnp.log(total),
                        totals[rows, :],
                    )
                out = column_dot(prob_low[...], tile)
                lane = lane_index((size, HEAD))
                placed = jnp.where(even, pltpu.roll(out, DN, 1), out)
                before = mixed[whole, pair].astype(jnp.float32)
                mixed[whole, pair] = jnp.where((lane < DN) == even, placed, before).astype(
                    mixed.dtype
                )

        return [
            (self.phase_time * n, functools.partial(run, n // 2, n % 2))
            for n in range(2 * self.packs)
        ]


class AttentionBackward:
    def __init__(
        self,
        queries,
        latent_heads,
        totals,
        grad_mixed,
        tokens,
        keys,
        bounds,
        waves,
        query_up,
        latent_up,
        packs,
        heads,
    ):
        rows = tokens.shape[0]
        self.packs, self.heads, self.pack_rows = packs, heads, rows // packs
        self.givens = [
            queries,
            latent_heads,
            totals,
            grad_mixed,
            tokens,
            keys,
            bounds,
            *waves,
            query_up,
            latent_up,
        ]
        low = jnp.bfloat16
        self.outs = [
            jax.ShapeDtypeStruct((rows, heads * HEAD), low),
            jax.ShapeDtypeStruct((rows, heads * HEAD), low),
            jax.ShapeDtypeStruct((rows, QR + KVR + HEAD), low),
        ]
        size = self.pack_rows
        self.scratch = [
            pltpu.VMEM((size, size), jnp.float32),
            pltpu.VMEM((size, size), jnp.float32),
            pltpu.VMEM((size, size), jnp.float32),
            pltpu.VMEM((size, size), low),
            pltpu.VMEM((size, size), low),
            pltpu.VMEM((size, HEAD), jnp.float32),
        ]
        self.phase_time = 9.0
        self.given_specs = [VMEM_SPEC] * len(self.givens)
        self.out_specs = [VMEM_SPEC] * len(self.outs)

    def phases(self, givens, outs, scratch, board, task_givens, task_outs):
        (
            queries,
            heads_in,
            totals,
            grad_mixed,
            tokens,
            keys,
            bounds,
            wave,
            low_wave,
            high_wave,
            query_up,
            latent_up,
        ) = givens
        grad_queries, grad_heads, terms = outs
        bias, held, grad_held, prob_low, score_low, grad_rope = scratch
        scale = QH ** (-0.5)
        size = self.pack_rows

        def run(pack, part):
            first, last = (0, self.heads // 2 + 1) if part == 0 else (self.heads // 2 + 1, self.heads)
            start = pack * size
            whole = slice(start, start + size)
            rope_key = pltpu.roll(
                tokens[whole, QR + KVR : QR + KVR + HEAD].astype(jnp.float32), DN, 1
            )
            if part == 0:
                score_bias(keys, bounds, bias, pack, size)
                grad_rope[...] = jnp.zeros_like(grad_rope)

            @pl.loop(first, last)
            def _(head):
                lanes = pl.ds(pl.multiple_of(head * HEAD, HEAD), HEAD)
                pair = pl.ds(pl.multiple_of((head // 2) * HEAD, HEAD), HEAD)
                even = head % 2 == 0
                lane = lane_index((size, HEAD))
                tile = heads_in[whole, lanes]
                query_all = queries[whole, lanes]
                key_all = jnp.where(lane < DN, tile.astype(jnp.float32), rope_key).astype(
                    jnp.bfloat16
                )
                grad_pair = grad_mixed[whole, pair].astype(jnp.float32)
                grad_out = jnp.where(
                    lane < DN, 0.0, jnp.where(even, pltpu.roll(grad_pair, DN, 1), grad_pair)
                ).astype(jnp.bfloat16)
                total_all = jnp.sum(
                    jnp.where(lane == head, totals[whole, :], 0.0), axis=1, keepdims=True
                )
                held[...] = right_transposed(query_all, key_all)
                grad_held[...] = right_transposed(grad_out, tile)
                for block in range(size // ROW_BLOCK):
                    part = slice(block * ROW_BLOCK, (block + 1) * ROW_BLOCK)
                    prob = jnp.exp(held[part, :] * scale + bias[part, :] - total_all[part])
                    grad_prob = grad_held[part, :]
                    inner = jnp.sum(prob * grad_prob, axis=1, keepdims=True)
                    prob_low[part, :] = prob.astype(jnp.bfloat16)
                    score_low[part, :] = (prob * (grad_prob - inner)).astype(jnp.bfloat16)
                grad_query = column_dot(score_low[...], key_all) * scale
                grad_queries[whole, lanes] = turn(
                    grad_query, wave[whole, :], -low_wave[whole, :], -high_wave[whole, :]
                ).astype(grad_queries.dtype)
                grad_value = left_transposed(prob_low[...], grad_out)
                grad_key = left_transposed(score_low[...], query_all) * scale
                grad_rope[...] += grad_key
                grad_heads[whole, lanes] = jnp.where(lane < DN, grad_key, grad_value).astype(
                    grad_heads.dtype
                )

            if part == 0:
                return
            terms[whole, 0:QR] = right_transposed(grad_queries[whole, :], query_up[...]).astype(
                terms.dtype
            )
            terms[whole, QR : QR + KVR] = right_transposed(
                grad_heads[whole, :], latent_up[...]
            ).astype(terms.dtype)
            terms[whole, QR + KVR :] = pltpu.roll(grad_rope[...], HEAD - DN, 1).astype(terms.dtype)

        return [
            (self.phase_time * n, functools.partial(run, n // 2, n % 2))
            for n in range(2 * self.packs)
        ]


class FfnForward:
    order = (
        ((0, 0, 0), 0.0),
        ((1, 0, 0), 0.26),
        ((0, 0, 1), 2.01),
        ((0, 1, 0), 2.02),
        ((1, 0, 1), 2.31),
        ((1, 1, 0), 2.32),
        ((0, 1, 1), 3.01),
        ((1, 1, 1), 3.31),
    )

    def __init__(self, gate, up, rows, unit):
        self.givens = [gate, up]
        self.given_specs = self.out_specs = [HBM_SPEC] * 2
        depth, units = gate.shape
        self.rows, self.unit = rows, unit
        self.outs = [jax.ShapeDtypeStruct((8 * rows, units), jnp.float32)] * 2
        self.scratch = [
            pltpu.VMEM((2, depth, units), gate.dtype),
            pltpu.VMEM((2, rows, depth), gate.dtype),
            pltpu.VMEM((2, 2, rows, units), jnp.float32),
            pltpu.SemaphoreType.DMA((2,)),
            pltpu.SemaphoreType.DMA((2,)),
            pltpu.SemaphoreType.DMA((2, 2)),
        ]

    def phases(self, givens, outs, scratch, board, task_givens, task_outs):
        weights, tokens, staged, weight_sems, token_sems, out_sems = scratch
        own, gathered = task_givens[0], task_outs[0]
        loads = [
            pltpu.make_async_copy(givens[n], weights.at[n], weight_sems.at[n]) for n in range(2)
        ]
        for load in loads:
            load.start()
        leaving = {}

        def run(step, place):
            spot = (place[0] * 2 + place[1]) * 2 + place[2]
            rows = pl.ds(spot * self.rows, self.rows)
            if spot:
                assert place in board.here
            slot = step % 2
            fetch = pltpu.make_async_copy(
                gathered.at[rows] if spot else own, tokens.at[slot], token_sems.at[slot]
            )
            fetch.start()
            fetch.wait()
            for n in range(2):
                if step == 0:
                    loads[n].wait()
                if step >= 2:
                    leaving.pop((slot, n)).wait()
                staged[slot, n] = column_dot(tokens[slot], weights[n])
                copy = pltpu.make_async_copy(
                    staged.at[slot, n], outs[n].at[rows], out_sems.at[slot, n]
                )
                copy.start()
                leaving[(slot, n)] = copy

        def finish():
            for copy in leaving.values():
                copy.wait()

        plan = [
            (when * self.unit, functools.partial(run, step, place))
            for step, (place, when) in enumerate(self.order)
        ]
        return plan + [(1e9, finish)]


class FfnBackward:
    CHUNK = 256

    def __init__(self, normed, grad_gate, grad_up, gate, up, m, piece_time):
        self.givens = [normed, grad_gate, grad_up, gate, up]
        self.given_specs = [HBM_SPEC] * 5
        self.out_specs = [HBM_SPEC] * 2
        rows, depth = normed.shape
        units = gate.shape[1]
        low = normed.dtype
        self.rows, self.depth, self.units = rows, depth, units
        self.m, self.piece_time = m, piece_time
        self.outs = [jax.ShapeDtypeStruct((depth, units), low)] * 2
        self.scratch = [
            pltpu.VMEM((rows, units), low),
            pltpu.VMEM((rows, units), low),
            pltpu.VMEM((depth, units), low),
            pltpu.VMEM((depth, units), low),
            pltpu.SemaphoreType.DMA((4,)),
        ]

    def phases(self, givens, outs, scratch, board, task_givens, task_outs):
        normed = givens[0]
        held, sems = scratch[:4], scratch[4]
        gate_held, up_held, gate_weight, up_weight = held
        chunk, rows, units, depth = self.CHUNK, self.rows, self.units, self.depth
        loads = [
            pltpu.make_async_copy(givens[n + 1], held[n], sems.at[n]) for n in (0, 2, 1, 3)
        ]
        for load in loads:
            load.start()

        def product(row):
            while loads:
                loads.pop(0).wait()
            part = slice(row, row + self.m)
            return right_transposed(gate_held[part, :], gate_weight[...]) + right_transposed(
                up_held[part, :], up_weight[...]
            )

        def gradients(first, count):
            def body(normed_part, gate_part, up_part):
                left = normed_part[...]
                gate_part[...] = left_transposed(left, gate_held[...]).astype(gate_part.dtype)
                up_part[...] = left_transposed(left, up_held[...]).astype(up_part.dtype)

            pltpu.emit_pipeline(
                body,
                grid=(count,),
                in_specs=[pl.BlockSpec((rows, chunk), lambda n: (0, n + first))],
                out_specs=[pl.BlockSpec((chunk, units), lambda n: (n + first, 0))] * 2,
            )(normed, outs[0], outs[1])

        plan = octet_pieces(board, self.m, self.piece_time, product)
        when = plan[-1][0] + self.piece_time
        for first in range(0, depth // chunk, 2):
            plan.append((when, functools.partial(gradients, first, 2)))
            when += 6.0
        return plan


class FfnProducts:
    CHUNK = 256

    def __init__(self, hidden, down):
        self.givens = [hidden, down]
        self.given_specs, self.out_specs = [HBM_SPEC] * 2, [HBM_SPEC]
        self.outs = [jax.ShapeDtypeStruct((hidden.shape[0], down.shape[1]), down.dtype)]
        self.scratch = [pltpu.VMEM(down.shape, down.dtype), pltpu.SemaphoreType.DMA]

    def phases(self, givens, outs, scratch, board, task_givens, task_outs):
        hidden, down = givens
        down_held, sem = scratch
        chunk = self.CHUNK
        load = pltpu.make_async_copy(down, down_held, sem)
        load.start()

        def products(first, count):
            if first == 0:
                load.wait()

            def body(hidden_part, out_part):
                out_part[...] = column_dot(hidden_part[...], down_held[...]).astype(out_part.dtype)

            pltpu.emit_pipeline(
                body,
                grid=(count,),
                in_specs=[pl.BlockSpec((chunk, hidden.shape[1]), lambda n: (n + first, 0))],
                out_specs=[pl.BlockSpec((chunk, down.shape[1]), lambda n: (n + first, 0))],
            )(hidden, outs[0])

        return [
            (2.0 + 2.0 * first, functools.partial(products, first, 2))
            for first in range(0, hidden.shape[0] // chunk, 2)
        ]


class UnitGradient:
    def __init__(self, parts, line, when):
        self.givens = [parts]
        self.given_specs, self.out_specs = [VMEM_SPEC], [VMEM_SPEC]
        self.outs = [
            jax.ShapeDtypeStruct((parts.shape[1], PLANE * parts.shape[2]), jnp.bfloat16)
        ]
        self.scratch = []
        self.line, self.when = line, when

    def phases(self, givens, outs, scratch, board, task_givens, task_outs):
        parts, target = givens[0], outs[0]
        rows, columns = target.shape
        width = columns // (PLANE * self.line)
        step_rows = 16 if rows % 16 == 0 else rows
        count = rows // step_rows

        def run(first, last):
            @pl.loop(first, last)
            def _(step):
                here = pl.ds(pl.multiple_of(step * step_rows, step_rows), step_rows)
                pieces = [parts[i, here, :].astype(jnp.float32) for i in range(PLANE)]
                target[here, :] = jnp.concatenate(
                    [
                        pieces[i][:, z * width : (z + 1) * width]
                        for z in range(self.line)
                        for i in range(PLANE)
                    ],
                    axis=1,
                ).astype(target.dtype)

        return [
            (self.when, functools.partial(run, 0, count // 2)),
            (self.when + 6.0, functools.partial(run, count // 2, count)),
        ]


def positions(segment_ids):
    token_index = jnp.arange(segment_ids.shape[0], dtype=jnp.int32)
    doc_start = jnp.concatenate(
        [jnp.ones((1,), dtype=jnp.bool_), segment_ids[1:] != segment_ids[:-1]]
    )
    starts = lax.cummax(jnp.where(doc_start, token_index, 0), axis=0)
    return token_index - starts


def rope_tables(position):
    exponent = jnp.arange(DR // 2, dtype=jnp.float32) * (2.0 / DR)
    rope_angle = position[:, None] * (ROPE_BASE ** (-exponent))[None, :]
    return (jnp.cos(rope_angle), jnp.sin(rope_angle))


def local(
    inputs,
    cotangent,
    segment_ids,
    gains,
    gains_first,
    gains_second,
    query_down,
    query_down_first,
    query_down_second,
    latent_down,
    latent_down_first,
    latent_down_second,
    query_up,
    query_up_first,
    query_up_second,
    latent_up,
    latent_up_first,
    latent_up_second,
    output_proj,
    output_proj_first,
    output_proj_second,
    gate_proj,
    gate_proj_first,
    gate_proj_second,
    up_proj,
    up_proj_first,
    up_proj_second,
    down_proj,
    down_proj_first,
    down_proj_second,
):
    size = lax.axis_size("dp")
    tensor = lax.axis_size("tensor")
    line = size // PLANE
    z, i, t = line_index(), plane_index(), lax.axis_index("tensor")
    half_rows = inputs.shape[0]
    pack_rows = segment_ids.shape[0]
    packs = PLANE
    rows_all = packs * pack_rows
    low = jnp.bfloat16
    local_heads = H // (PLANE * tensor)
    units = FF // (PLANE * tensor)
    mixed_width = -(-local_heads // 2) * HEAD

    def column_blocks(weight, columns):
        return weight.astype(low).reshape(-1, PLANE, columns).transpose(1, 0, 2)

    down_rows = query_down.shape[0]
    pack_height = down_rows + 16
    gain_width = gains.shape[0]
    down_pack = jnp.concatenate(
        [
            jnp.concatenate([query_down, latent_down], axis=1).astype(low),
            jnp.pad(gains.astype(low)[None], ((0, 15), (0, QR + KVR + DR - gain_width))),
        ],
        axis=0,
    )
    def head_blocks(weight):
        blocks = weight.astype(low).reshape(-1, PLANE, local_heads, QH)
        blocks = jnp.pad(blocks, ((0, 0), (0, 0), (0, 0), (0, HEAD - QH)))
        return blocks.reshape(-1, PLANE, local_heads * HEAD).transpose(1, 0, 2)

    pack_all, query_up_all, latent_up_all, output_moved, (gate_blocks, up_blocks) = communicate(
        1,
        GatherPack(down_pack),
        GatherColumns(head_blocks(query_up), 16.0),
        GatherColumns(column_blocks(latent_up, local_heads * KH), 16.0),
        Later(Transpose(output_proj.astype(low)), 16.0),
        compute=UnitBlocks(gate_proj, up_proj, line),
    )
    query_up_all = query_up_all.reshape(QR, local_heads * HEAD)
    latent_up_all = latent_up_all.reshape(KVR, local_heads * KH)
    pack_lines = pack_all.reshape(2 * 2 * tensor * line, pack_height, QR + KVR + DR)
    found = [
        take(
            pack_lines,
            ((((i ^ place) % 2) * 2 + (i ^ place) // 2) * tensor + (t + side) % tensor) * line + zz,
        )
        for zz in range(line)
        for place in range(PLANE)
        for side in range(tensor)
    ]
    down_both = jnp.concatenate([block[:down_rows] for block in found], axis=0)
    gain_values = jnp.concatenate([block[down_rows, :gain_width] for block in found], axis=0)
    gain_values = gain_values.astype(jnp.float32)
    gain_attention = gain_values[:D]
    gain_query = gain_values[D : D + QR]
    gain_latent = gain_values[D + QR : D + QR + KVR]
    gain_ffn = gain_values[D + QR + KVR :]

    incoming = inputs.astype(jnp.float32)
    attn_unit, inverse_attention = norm_forward(incoming, gain_attention)
    normed_attn = attn_unit.astype(low)
    both_latent = jnp.dot(normed_attn, down_both, preferred_element_type=jnp.float32)
    query_latent = both_latent[:, :QR]
    latent = both_latent[:, QR:]
    query_unit, inverse_query = norm_forward(query_latent, gain_query)
    latent_unit, inverse_latent = norm_forward(latent[:, :KVR], gain_latent)
    own_position = lax.dynamic_slice_in_dim(positions(segment_ids), t * half_rows, half_rows)
    own_segment = lax.dynamic_slice_in_dim(segment_ids, t * half_rows, half_rows)
    own_cosine, own_sine = rope_tables(own_position.astype(jnp.float32))
    own_rope_key = rotate(latent[:, KVR:], own_cosine, own_sine)
    marks = jnp.stack(
        [own_segment // 16, own_segment % 16, own_position // 16, own_position % 16], axis=1
    )
    tokens_own = jnp.concatenate(
        [
            query_unit.astype(low),
            latent_unit.astype(low),
            own_rope_key.astype(low),
            marks.astype(low),
            jnp.zeros((half_rows, 128 - DR - 4), low),
        ],
        axis=1,
    )
    tokens_all, output_all, gate_plane = communicate(
        3, OctetGather(tokens_own), LineGather(output_moved), Later(PlaneExchange(gate_blocks), 14.0)
    )
    output_all = jnp.pad(
        output_all.reshape(local_heads * DV, D), ((0, mixed_width - local_heads * DV), (0, 0))
    )
    marks_all = tokens_all[:, QR + KVR + DR : QR + KVR + DR + 4].astype(jnp.float32)
    key_base = (marks_all[:, 0] * 16.0 + marks_all[:, 1]) * pack_rows
    position = marks_all[:, 2] * 16.0 + marks_all[:, 3]
    key = key_base + position
    keys = jnp.broadcast_to(key.reshape(packs, 1, pack_rows), (packs, 8, pack_rows))
    bounds = jnp.pad(jnp.stack([key_base, key], axis=1), ((0, 0), (0, HEAD - 2)))
    rope_cosine, rope_sine = rope_tables(position)
    nothing = jnp.zeros((rows_all, DR), jnp.float32)
    still = jnp.zeros((rows_all, DN), jnp.float32)
    waves = (
        jnp.concatenate([still + 1.0, rope_cosine, rope_cosine, nothing], axis=1),
        jnp.concatenate([still, -rope_sine, nothing, nothing[:, : DR // 2]], axis=1),
        jnp.concatenate([still, nothing[:, : DR // 2], rope_sine, nothing], axis=1),
    )
    grad_ffn, up_plane, gate_all, (queries, latent_heads, mixed_heads, log_totals) = communicate(
        2,
        OctetGather((RESIDUAL * cotangent.astype(jnp.float32)).astype(low)),
        Later(PlaneExchange(up_blocks), 30.0),
        LineGather(gate_plane),
        compute=AttentionForward(
            tokens_all, keys, bounds, waves, query_up_all, latent_up_all, packs, local_heads
        ),
    )
    gate_all = gate_all.reshape(D, units)
    if line == LINE:
        attention_sum, up_all, _ = communicate(
            4,
            OctetReduceInside(half_rows, D, 2.0),
            LineGather(up_plane),
            compute=PieceProduct(mixed_heads, output_all, half_rows, 2.0),
        )
    else:
        attention_terms = jnp.dot(mixed_heads, output_all, preferred_element_type=jnp.float32)
        attention_sum, up_all = communicate(
            4, OctetReduce(attention_terms.astype(low)), LineGather(up_plane)
        )
    up_all = up_all.reshape(D, units)
    residual = incoming + RESIDUAL * attention_sum

    ffn_unit, inverse_ffn = norm_forward(residual, gain_ffn)
    normed_own = ffn_unit.astype(low)
    tasks = (OctetGather(normed_own), LineGather(down_proj.astype(low)))
    if line == LINE:
        normed_ffn, down_all, (gate_value, up_value) = communicate(
            5,
            *tasks,
            compute=FfnForward(gate_all, up_all, half_rows, octet_unit((half_rows, D))),
        )
    else:
        normed_ffn, down_all = communicate(5, *tasks)
        gate_value = jnp.dot(normed_ffn, gate_all, preferred_element_type=jnp.float32)
        up_value = jnp.dot(normed_ffn, up_all, preferred_element_type=jnp.float32)
    down_all = down_all.reshape(units, D)
    gate_sigmoid = lax.logistic(gate_value)
    silu_gate = gate_value * gate_sigmoid
    hidden = (silu_gate * up_value).astype(low)
    grad_hidden = right_transposed(grad_ffn, down_all)
    grad_gate = (
        grad_hidden * up_value * gate_sigmoid * (1.0 + gate_value * (1.0 - gate_sigmoid))
    ).astype(low)
    grad_up = (grad_hidden * silu_gate).astype(low)
    down_grad = left_transposed(hidden, grad_ffn).astype(low).reshape(line, -1, D)
    if line == LINE:
        grad_normed_ffn, down_shard, (gate_grad, up_grad) = communicate(
            6,
            OctetReduceInside(half_rows, D, 5.0),
            LineReduce(down_grad),
            compute=FfnBackward(normed_ffn, grad_gate, grad_up, gate_all, up_all, half_rows, 5.0),
        )
    else:
        back_terms = right_transposed(grad_gate, gate_all) + right_transposed(grad_up, up_all)
        gate_grad = left_transposed(normed_ffn, grad_gate).astype(low)
        up_grad = left_transposed(normed_ffn, grad_up).astype(low)
        grad_normed_ffn, down_shard = communicate(
            6, OctetReduce(back_terms.astype(low)), LineReduce(down_grad)
        )
    outer_grad = cotangent.astype(jnp.float32)
    grad_incoming_ffn, gain_ffn_grad = norm_backward(
        residual, inverse_ffn, gain_ffn, grad_normed_ffn
    )
    grad_residual = outer_grad + grad_incoming_ffn

    grad_branch, gate_sum, (ffn_terms,) = communicate(
        7,
        OctetGather((RESIDUAL * grad_residual).astype(low)),
        LineReduce(gate_grad.reshape(line, PLANE, -1, units)),
        compute=FfnProducts(hidden, down_all),
    )
    output_grad = (
        left_transposed(mixed_heads, grad_branch)
        .astype(low)[: local_heads * DV]
        .reshape(line, -1, D)
    )
    grad_mixed = right_transposed(grad_branch, output_all).astype(low)
    ffn_sum, up_sum, gate_parts, (grad_query_heads, grad_latent_heads, grad_unit_terms) = communicate(
        8,
        OctetReduce(ffn_terms),
        LineReduce(up_grad.reshape(line, PLANE, -1, units)),
        Later(PlaneExchange(gate_sum.astype(low)), 30.0),
        compute=AttentionBackward(
            queries,
            latent_heads,
            log_totals,
            grad_mixed,
            tokens_all,
            keys,
            bounds,
            waves,
            query_up_all,
            latent_up_all,
            packs,
            local_heads,
        ),
    )
    block_output = (residual + RESIDUAL * ffn_sum).astype(low)
    query_up_grad = left_transposed(tokens_all[:, :QR], grad_query_heads).astype(low)
    latent_up_grad = left_transposed(tokens_all[:, QR : QR + KVR], grad_latent_heads).astype(low)
    grad_units, output_sum, up_parts, (gate_shard,) = communicate(
        9,
        OctetReduce(grad_unit_terms),
        LineReduce(output_grad),
        Later(PlaneExchange(up_sum.astype(low)), 14.0),
        compute=UnitGradient(gate_parts, line, 10.5),
    )
    grad_query_wide, gain_query_grad = norm_backward(
        query_latent, inverse_query, gain_query, grad_units[:, :QR]
    )
    grad_latent_part, gain_latent_grad = norm_backward(
        latent[:, :KVR], inverse_latent, gain_latent, grad_units[:, QR : QR + KVR]
    )
    grad_rope = unrotate(grad_units[:, QR + KVR : QR + KVR + DR], own_cosine, own_sine)
    grad_both = jnp.concatenate([grad_query_wide, grad_latent_part, grad_rope], axis=1).astype(low)
    grad_normed_attn = right_transposed(grad_both, down_both)
    grad_incoming_attn, gain_attention_grad = norm_backward(
        incoming, inverse_attention, gain_attention, grad_normed_attn
    )
    input_grad = (grad_residual + grad_incoming_attn).astype(low)
    gains_grad = jnp.concatenate(
        [gain_attention_grad, gain_query_grad, gain_latent_grad, gain_ffn_grad]
    ).astype(low)
    shards = size * tensor
    left_blocks = normed_attn.reshape(half_rows, line, PLANE, tensor, down_rows)
    left_blocks = jnp.pad(left_blocks, ((0, 0), (0, 0), (0, 0), (0, 0), (0, 16)))
    spots = jnp.arange(pack_height)[None, None, :] == down_rows
    shard_index = jnp.arange(shards)
    left_marks = (
        (shard_index[:, None, None] == shard_index[None, :, None]) & spots
    ).astype(low)
    left_blocks = jnp.concatenate(
        [left_blocks, left_marks.reshape(shards, line, PLANE, tensor, pack_height)], axis=0
    ).transpose(2, 3, 0, 1, 4)
    left_blocks = left_blocks.reshape(PLANE * tensor, half_rows + shards, line * pack_height)
    pack_right = jnp.concatenate(
        [
            grad_both,
            jnp.pad(
                gains_grad.reshape(shards, gain_width),
                ((0, 0), (0, QR + KVR + DR - gain_width)),
            ),
        ],
        axis=0,
    )
    pack_rows_all = line * pack_height
    up_order = UnitGradient(up_parts, line, 15.0)
    if line == LINE:
        pack_task = OctetReduceInside(pack_rows_all, QR + KVR + DR, 1.5)
        tail_compute = Together(
            PieceProduct(left_blocks, pack_right, pack_rows_all, 1.5, columns=True), up_order
        )
    else:
        pack_left = jnp.concatenate(
            [
                take(left_blocks, (i ^ (core + 2 * x)) * tensor + (t + y) % tensor)
                for core in range(2)
                for x in range(2)
                for y in range(tensor)
            ],
            axis=1,
        )
        pack_task = OctetReduce(left_transposed(pack_left, pack_right).astype(low))
        tail_compute = up_order
    pack_octet, query_up_sum, latent_up_sum, output_shard, up_found = communicate(
        10,
        pack_task,
        LineReduce(query_up_grad.reshape(line, PLANE, -1, local_heads * HEAD)),
        LineReduce(latent_up_grad.reshape(line, PLANE, -1, local_heads * KH)),
        Transpose(output_sum.astype(low), back=True),
        compute=tail_compute,
    )
    pack_sum, query_up_parts, latent_up_parts = communicate(
        11,
        LineReduce(pack_octet.astype(low).reshape(line, pack_height, QR + KVR + DR)),
        PlaneExchange(query_up_sum.astype(low)),
        PlaneExchange(latent_up_sum.astype(low)),
    )
    query_down_shard = pack_sum[:down_rows, :QR]
    latent_down_shard = pack_sum[:down_rows, QR:]
    gains_shard = pack_sum[down_rows, :gain_width]

    def head_columns(blocks):
        return blocks.astype(jnp.float32).transpose(1, 0, 2).reshape(blocks.shape[1], -1)

    query_up_parts = query_up_parts.reshape(PLANE, -1, local_heads, HEAD)[..., :QH]
    query_up_shard = head_columns(query_up_parts.reshape(PLANE, -1, local_heads * QH))
    latent_up_shard = head_columns(latent_up_parts)
    output_shard = output_shard.astype(jnp.float32)

    gains_out = adamw_update(gains, gains_first, gains_second, gains_shard, GAIN_RATE)
    query_down_out = adamw_update(
        query_down, query_down_first, query_down_second, query_down_shard, matrix_rate(D)
    )
    latent_down_out = adamw_update(
        latent_down, latent_down_first, latent_down_second, latent_down_shard, matrix_rate(D)
    )
    query_up_out = adamw_update(
        query_up, query_up_first, query_up_second, query_up_shard, matrix_rate(QR)
    )
    latent_up_out = adamw_update(
        latent_up, latent_up_first, latent_up_second, latent_up_shard, matrix_rate(KVR)
    )
    output_out = adamw_update(
        output_proj, output_proj_first, output_proj_second, output_shard, matrix_rate(H * DV // 64)
    )
    gate_out = adamw_update(
        gate_proj,
        gate_proj_first,
        gate_proj_second,
        gate_shard.astype(jnp.float32),
        matrix_rate(D),
    )
    up_out = adamw_update(
        up_proj,
        up_proj_first,
        up_proj_second,
        up_found[0].astype(jnp.float32),
        matrix_rate(D),
    )
    down_out = adamw_update(
        down_proj, down_proj_first, down_proj_second, down_shard, matrix_rate(FF // 8)
    )
    return (
        block_output,
        input_grad,
        gains_out[0],
        gains_out[1],
        gains_out[2],
        query_down_out[0],
        query_down_out[1],
        query_down_out[2],
        latent_down_out[0],
        latent_down_out[1],
        latent_down_out[2],
        query_up_out[0],
        query_up_out[1],
        query_up_out[2],
        latent_up_out[0],
        latent_up_out[1],
        latent_up_out[2],
        output_out[0],
        output_out[1],
        output_out[2],
        gate_out[0],
        gate_out[1],
        gate_out[2],
        up_out[0],
        up_out[1],
        up_out[2],
        down_out[0],
        down_out[1],
        down_out[2],
    )


def solution(mesh):
    in_specs = (
        P(("dp", "tensor"), None),
        P(("dp", "tensor"), None),
        P("dp"),
        P(("dp", "tensor")),
        P(("dp", "tensor")),
        P(("dp", "tensor")),
        P(("dp", "tensor"), None),
        P(("dp", "tensor"), None),
        P(("dp", "tensor"), None),
        P(("dp", "tensor"), None),
        P(("dp", "tensor"), None),
        P(("dp", "tensor"), None),
        P("dp", "tensor"),
        P("dp", "tensor"),
        P("dp", "tensor"),
        P("dp", "tensor"),
        P("dp", "tensor"),
        P("dp", "tensor"),
        P(("tensor", "dp"), None),
        P(("tensor", "dp"), None),
        P(("tensor", "dp"), None),
        P("dp", "tensor"),
        P("dp", "tensor"),
        P("dp", "tensor"),
        P("dp", "tensor"),
        P("dp", "tensor"),
        P("dp", "tensor"),
        P(("tensor", "dp"), None),
        P(("tensor", "dp"), None),
        P(("tensor", "dp"), None),
    )
    out_specs = (
        P(("dp", "tensor"), None),
        P(("dp", "tensor"), None),
        P(("dp", "tensor")),
        P(("dp", "tensor")),
        P(("dp", "tensor")),
        P(("dp", "tensor"), None),
        P(("dp", "tensor"), None),
        P(("dp", "tensor"), None),
        P(("dp", "tensor"), None),
        P(("dp", "tensor"), None),
        P(("dp", "tensor"), None),
        P("dp", "tensor"),
        P("dp", "tensor"),
        P("dp", "tensor"),
        P("dp", "tensor"),
        P("dp", "tensor"),
        P("dp", "tensor"),
        P(("tensor", "dp"), None),
        P(("tensor", "dp"), None),
        P(("tensor", "dp"), None),
        P("dp", "tensor"),
        P("dp", "tensor"),
        P("dp", "tensor"),
        P("dp", "tensor"),
        P("dp", "tensor"),
        P("dp", "tensor"),
        P(("tensor", "dp"), None),
        P(("tensor", "dp"), None),
        P(("tensor", "dp"), None),
    )
    return jax.shard_map(local, mesh=mesh, in_specs=in_specs, out_specs=out_specs, check_vma=False)
```
